128 devices in a mesh: seq: 32 (over z, y, core), exp: 4 (over x).
Axes of the slice: x: 4, y: 4, z: 4, core: 2. Of those that a mesh axis runs over, the one named last changes fastest.
Arguments:
- queries: bfloat16 [2, 8192, 4096], P(None, 'seq', 'exp'), may hold values from -6 to 6
- keys: bfloat16 [2, 8192, 4096], P(None, 'seq', 'exp'), may hold values from -6 to 6
- payload_vectors: bfloat16 [2, 8192, 4096], P(None, 'seq', 'exp'), may hold values from -6 to 6
- log_decay: float32 [2, 8192, 32], P(None, 'seq', 'exp'), may hold values from -1 to 0
- attn_gain: float32 [4096], P('exp'), may hold values from 0.5 to 1.5
- out_weight: bfloat16 [4096, 6144], P('exp', 'seq'), may hold values from -0.09375 to 0.09375
- residual: bfloat16 [2, 8192, 6144], P(None, ('seq', 'exp')), may hold values from -12 to 12
- norm_gain: float32 [6144], replicated, may hold values from 0.5 to 1.5
- router_weight: bfloat16 [6144, 32], replicated, may hold values from -0.078125 to 0.078125
- picks: int32 [2, 8192, 2], P(None, ('seq', 'exp')), may hold values from 0 to 31, as said below
- gate_weight: bfloat16 [4, 9216, 6144], P('exp', 'seq'), may hold values from -0.078125 to 0.078125
- up_weight: bfloat16 [4, 9216, 6144], P('exp', 'seq'), may hold values from -0.078125 to 0.078125
- down_weight: bfloat16 [4, 9216, 6144], P('exp', 'seq'), may hold values from -0.0625 to 0.0625
Outputs:
- layer_out: bfloat16 [2, 8192, 6144], P(None, ('seq', 'exp'))
The draws below stay inside these ranges and needn't reach their ends.
Inputs may be any that keep to these rules, and one draw needn't show every extreme that they name: `picks`: each row names two different experts; among the 128 rows of one device (its positions of every sequence) each expert below 4 is named at most 12 times, and one of them exactly 12 times.
All inputs are finite; a program needn't handle non-finite values.
Results may differ from the reference program's by a relative error of at most 0.015.
Values may be sent and summed in bfloat16 or wider, within the bound.
No kernel may reach another device: no remote copies, remote signals or barrier semaphores. Data moves between devices by JAX's collectives and lax.ppermute only.
A program may use at most 192 MiB of HBM per device.

```python
import jax
import jax.numpy as jnp
from jax import lax

D = 6144
HEAD = 128
HEADS_DEV = 8
FF = 9216
EXPERTS = 32
SAMPLE_TOTAL = 2
BLOCK = 256
ATTENTION_PLANES = 32
TOKEN_SPAN = 8192
SLICE = 64
ROWS = 128
CAP = 12
FLIGHT = 4
N_SEQ = 32
N_EXP = 4


def draw_picks(key, part):
    key = jax.random.fold_in(key, 11)
    nblocks = TOKEN_SPAN // SLICE
    key_hot, key_first, key_second, key_shift, key_turn = jax.random.split(key, 5)
    hots = jax.random.randint(key_hot, (), 0, FLIGHT)
    hot_col = jnp.full((nblocks, 1), hots, jnp.int32)
    first = jax.vmap(lambda k: jax.random.permutation(k, ROWS))(jax.random.split(key_first, nblocks))
    second = jax.vmap(lambda k: jax.random.permutation(k, ROWS))(jax.random.split(key_second, nblocks))
    shift_a = jax.random.randint(key_shift, (nblocks, 1), 0, EXPERTS - FLIGHT)
    shift_b = jax.random.randint(key_turn, (nblocks, 1), 0, EXPERTS - 1)
    pick_a = jnp.where(first < CAP, hot_col, FLIGHT + (first - CAP + shift_a) % (EXPERTS - FLIGHT))
    index_one = (second + shift_b) % (EXPERTS - 1)
    cand_one = index_one + (index_one >= hot_col).astype(jnp.int32)
    index_two = (index_one + 1) % (EXPERTS - 1)
    cand_two = index_two + (index_two >= hot_col).astype(jnp.int32)
    pick_b = jnp.where(cand_one == pick_a, cand_two, cand_one)
    both = jnp.stack([pick_a, pick_b], -1)
    both = both.reshape(nblocks, SAMPLE_TOTAL, SLICE, 2).transpose(1, 0, 2, 3).reshape(SAMPLE_TOTAL, TOKEN_SPAN, 2)
    return both.astype(jnp.int32)


def draw_log_decay(key, part):
    key = jax.random.fold_in(key, 23)
    rapid_seed, rough_seed, tile_seed, spike_seed, stacking_seed = jax.random.split(key, 5)
    share = 0.5
    fast = jax.random.uniform(rapid_seed, (SAMPLE_TOTAL, 1, ATTENTION_PLANES)) < share
    forgetting_factor = jnp.where(fast, 1.0 / 40.0, 0.8 / TOKEN_SPAN)
    rough_approximation = jax.random.uniform(rough_seed, (SAMPLE_TOTAL, TOKEN_SPAN, ATTENTION_PLANES), minval=0.4, maxval=1.6)
    tile_after_tile = jnp.exp(jax.random.uniform(tile_seed, (SAMPLE_TOTAL, TOKEN_SPAN // BLOCK, 1, ATTENTION_PLANES), minval=-0.5, maxval=0.5))
    tile_after_tile = jnp.broadcast_to(tile_after_tile, (SAMPLE_TOTAL, TOKEN_SPAN // BLOCK, BLOCK, ATTENTION_PLANES)).reshape(SAMPLE_TOTAL, TOKEN_SPAN, ATTENTION_PLANES)
    spike_clusters = jax.random.randint(spike_seed, (SAMPLE_TOTAL, TOKEN_SPAN, ATTENTION_PLANES), 0, max(TOKEN_SPAN // 2, 1)) == 0
    stacking_level = jax.random.uniform(stacking_seed, (SAMPLE_TOTAL, TOKEN_SPAN, ATTENTION_PLANES), minval=0.22, maxval=0.69)
    decay_logs = -(forgetting_factor * rough_approximation * tile_after_tile) - jnp.where(spike_clusters, stacking_level, 0.0)
    return decay_logs.astype(jnp.float32)


def draw_residual(key, part):
    key = jax.random.fold_in(key, 37)
    key_rows, key_cols, key_base = jax.random.split(key, 3)
    rows_scale = jnp.exp(jax.random.uniform(key_rows, (SAMPLE_TOTAL, TOKEN_SPAN, 1), minval=jnp.log(0.08), maxval=jnp.log(0.8)))
    cols_scale = jnp.exp(jax.random.uniform(key_cols, (1, 1, D), minval=jnp.log(0.3), maxval=jnp.log(3.0)))
    base = jnp.clip(jax.random.normal(key_base, (SAMPLE_TOTAL, TOKEN_SPAN, D)), -4.0, 4.0)
    return (base * rows_scale * cols_scale).astype(jnp.bfloat16)


def levels(own_key, shape, cuts, low, top_value):
    def one(axis_at, blocks):
        heights = jax.random.uniform(jax.random.fold_in(jax.random.fold_in(own_key, 6), axis_at), (blocks,), jnp.float32, low / len(cuts), top_value / len(cuts))
        return jnp.repeat(jnp.exp(heights), shape[axis_at] // blocks).reshape((-1,) + (1,) * (len(shape) - axis_at - 1))

    factor_of = one(*cuts[0])
    for cut in cuts[1:]:
        factor_of = factor_of * one(*cut)
    return factor_of


def normal_values(stream_key, shape, width, most, cuts=(), held_as=jnp.bfloat16):
    entries = width * jax.random.normal(stream_key, shape, jnp.float32)
    if cuts:
        entries = entries * levels(stream_key, shape, cuts, -0.22, 0.18)
    return jnp.clip(entries, -most, most).astype(held_as)


def setup_inputs(seed: int = 0) -> dict:
    key_of = jax.random.split(jax.random.key(seed), 14)
    return {
        "queries": normal_values(key_of[0], (SAMPLE_TOTAL, TOKEN_SPAN, ATTENTION_PLANES * HEAD), 1.0, 6.0, ((1, 32), (2, 4))),
        "keys": normal_values(key_of[1], (SAMPLE_TOTAL, TOKEN_SPAN, ATTENTION_PLANES * HEAD), 1.0, 6.0, ((1, 32), (2, 4))),
        "payload_vectors": normal_values(key_of[2], (SAMPLE_TOTAL, TOKEN_SPAN, ATTENTION_PLANES * HEAD), 1.0, 6.0, ((1, 32), (2, 4))),
        "log_decay": draw_log_decay(jax.random.fold_in(key_of[13], 71), 0),
        "attn_gain": jnp.clip(0.5 + 1.0 * jax.random.uniform(key_of[4], (ATTENTION_PLANES * HEAD,), jnp.float32) ** levels(key_of[4], (ATTENTION_PLANES * HEAD,), ((0, 4),), -0.2, 0.2), 0.5, 1.5),
        "out_weight": normal_values(key_of[5], (ATTENTION_PLANES * HEAD, D), (ATTENTION_PLANES * HEAD) ** -0.5, 0.09375, ((0, 4), (1, 32))),
        "residual": draw_residual(jax.random.fold_in(key_of[13], 71), 0),
        "norm_gain": jnp.clip(jax.random.uniform(key_of[7], (D,), jnp.float32, 0.5, 1.5), 0.5, 1.5),
        "router_weight": normal_values(key_of[8], (D, EXPERTS), D ** -0.5, 0.078125),
        "picks": draw_picks(jax.random.fold_in(key_of[13], 71), 0),
        "gate_weight": normal_values(key_of[10], (FLIGHT, FF, D), D ** -0.5, 0.078125, ((0, 4), (1, 32))),
        "up_weight": normal_values(key_of[11], (FLIGHT, FF, D), D ** -0.5, 0.078125, ((0, 4), (1, 32))),
        "down_weight": normal_values(key_of[12], (FLIGHT, FF, D), FF ** -0.5, 0.0625, ((0, 4), (1, 32))),
    }


highest = lax.Precision.HIGHEST

def block_parts(q_blk, k_blk, v_blk, d_blk):
    qf = q_blk.astype(jnp.float32)
    kf = k_blk.astype(jnp.float32)
    vf = v_blk.astype(jnp.float32)
    cum = jnp.cumsum(d_blk, axis=1)
    scores = jnp.einsum('sthd,sjhd->shtj', qf, kf, precision=highest)
    turned = jnp.transpose(cum, (0, 2, 1))
    spread = turned[:, :, :, None] - turned[:, :, None, :]
    steps = cum.shape[1]
    later = lax.broadcasted_iota(jnp.int32, (steps, steps), 0) >= lax.broadcasted_iota(jnp.int32, (steps, steps), 1)
    weights = jnp.where(later, jnp.exp(jnp.minimum(spread, 0.0)), 0.0) * scores
    inner = jnp.einsum('shtj,sjhd->sthd', weights, vf, precision=highest)
    final = cum[:, -1, :]
    qscaled = qf * jnp.exp(cum)[..., None]
    kscaled = kf * jnp.exp(final[:, None, :] - cum)[..., None]
    update = jnp.einsum('sjhd,sjhe->shde', kscaled, vf, precision=highest)
    return (inner, qscaled, jnp.exp(final), update)

def gate_pair(inputs, routes, router_weight):
    logits = jnp.dot(inputs, router_weight, preferred_element_type=jnp.float32)
    labels = lax.broadcasted_iota(jnp.int32, (1, logits.shape[1]), 1)
    first = lax.optimization_barrier(jnp.sum(jnp.where(routes[:, 0:1] == labels, logits, 0.0), -1))
    second = lax.optimization_barrier(jnp.sum(jnp.where(routes[:, 1:2] == labels, logits, 0.0), -1))
    return (jax.nn.sigmoid(first - second), jax.nn.sigmoid(second - first))

def reference(queries, keys, payload_vectors, log_decay, attn_gain, out_weight, residual, norm_gain, router_weight, picks, gate_weight, up_weight, down_weight):
    nblocks = TOKEN_SPAN // BLOCK

    def split_blocks(array):
        return array.reshape(SAMPLE_TOTAL, nblocks, BLOCK, ATTENTION_PLANES, HEAD).transpose(1, 0, 2, 3, 4)
    q_blocks = split_blocks(queries)
    k_blocks = split_blocks(keys)
    v_blocks = split_blocks(payload_vectors)
    d_blocks = log_decay.reshape(SAMPLE_TOTAL, nblocks, BLOCK, ATTENTION_PLANES).transpose(1, 0, 2, 3)

    def advance(state, blocks):
        inner, qscaled, decay, update = block_parts(blocks[0], blocks[1], blocks[2], blocks[3])
        output = inner + jnp.einsum('sthd,shde->sthe', qscaled, state, precision=highest)
        state = decay[:, :, None, None] * state + update
        return (state, output)
    initial = jnp.zeros((SAMPLE_TOTAL, ATTENTION_PLANES, HEAD, HEAD), jnp.float32)
    _, outputs = lax.scan(advance, initial, (q_blocks, k_blocks, v_blocks, d_blocks))
    head_out = outputs.transpose(1, 0, 2, 3, 4).reshape(SAMPLE_TOTAL, TOKEN_SPAN, ATTENTION_PLANES, HEAD)
    normed = (head_out * lax.rsqrt(lax.optimization_barrier(jnp.mean(head_out * head_out, -1, keepdims=True)) + 1e-06) * attn_gain.reshape(ATTENTION_PLANES, HEAD)).astype(jnp.bfloat16)
    flat = normed.reshape(SAMPLE_TOTAL * TOKEN_SPAN, ATTENTION_PLANES * HEAD)
    group = HEADS_DEV * HEAD
    mixed = jnp.zeros((SAMPLE_TOTAL * TOKEN_SPAN, D), jnp.float32)
    for index in range(N_EXP):
        product = jnp.dot(flat[:, index * group:(index + 1) * group], out_weight[index * group:(index + 1) * group], preferred_element_type=jnp.float32)
        mixed = mixed + lax.optimization_barrier(product.astype(jnp.bfloat16)).astype(jnp.float32)
    hidden_state = residual.reshape(SAMPLE_TOTAL * TOKEN_SPAN, D).astype(jnp.float32) + mixed
    moe_in = (hidden_state * lax.rsqrt(lax.optimization_barrier(jnp.mean(hidden_state * hidden_state, -1, keepdims=True)) + 1e-06) * norm_gain).astype(jnp.bfloat16)
    routes = picks.reshape(SAMPLE_TOTAL * TOKEN_SPAN, 2)
    first_gate, second_gate = gate_pair(moe_in, routes, router_weight)
    token_count = SAMPLE_TOTAL * TOKEN_SPAN
    padded = jnp.concatenate([moe_in, jnp.zeros((1, D), jnp.bfloat16)], 0)
    moe = jnp.zeros((token_count + 1, D), jnp.float32)
    limit = N_SEQ * N_EXP * CAP
    units = FF // N_SEQ
    for expert in range(FLIGHT):
        hit_first = routes[:, 0] == expert
        hit_second = routes[:, 1] == expert
        weight = jnp.where(hit_first, first_gate, 0.0) + jnp.where(hit_second, second_gate, 0.0)
        weight = jnp.concatenate([weight, jnp.zeros((1,), jnp.float32)])
        chosen = jnp.nonzero(hit_first | hit_second, size=limit, fill_value=token_count)[0].astype(jnp.int32)
        rows_in = padded[chosen]
        gate = lax.dot_general(rows_in, gate_weight[expert], (((1,), (1,)), ((), ())), preferred_element_type=jnp.float32)
        upper = lax.dot_general(rows_in, up_weight[expert], (((1,), (1,)), ((), ())), preferred_element_type=jnp.float32)
        hidden = (jax.nn.silu(gate) * upper).astype(jnp.bfloat16)
        grouped = hidden.reshape(limit, N_SEQ, units).transpose(1, 0, 2)
        downs = down_weight[expert].reshape(N_SEQ, units, D)

        def accumulate(running, pair):
            part_sum = jnp.dot(pair[0], pair[1], preferred_element_type=jnp.float32)
            return (running + lax.optimization_barrier(part_sum.astype(jnp.bfloat16)).astype(jnp.float32), None)
        summed, _ = lax.scan(accumulate, jnp.zeros((limit, D), jnp.float32), (grouped, downs))
        expert_out = lax.optimization_barrier(summed.astype(jnp.bfloat16)).astype(jnp.float32)
        moe = moe.at[chosen].add(weight[chosen][:, None] * expert_out)
    layer_out = (hidden_state + moe[:token_count]).astype(jnp.bfloat16)
    return layer_out.reshape(SAMPLE_TOTAL, TOKEN_SPAN, D)
```

```python
import functools

import jax
import jax.numpy as jnp
from jax import lax
from jax.experimental import pallas as pl
from jax.experimental.pallas import tpu as pltpu
from jax.sharding import Mesh, PartitionSpec as P

HEAD = 128
BF = jnp.bfloat16
F32 = jnp.float32
HI = lax.Precision.HIGHEST
SEQ = ("z", "y", "core")
DEC = 16
OFFS = (1, 3, 2, 0)
JREL = {0: 0, 3: 1, 1: 2, 2: 3}


def ring(n, k):
    return [(i, (i + k) % n) for i in range(n)]


def mm(a, b):
    return jnp.dot(a, b, preferred_element_type=F32)


def mm0(a, b):
    return lax.dot_general(a, b, (((0,), (0,)), ((), ())), preferred_element_type=F32)


def split(a):
    hi = a.astype(BF)
    return hi, (a - hi.astype(F32)).astype(BF)


def local_kernel(q_ref, k_ref, v_ref, d_ref, inner_ref, state_ref, cum_ref):
    steps, heads = d_ref.shape[1], d_ref.shape[2]
    row = lax.broadcasted_iota(jnp.int32, (steps, steps), 0)
    col = lax.broadcasted_iota(jnp.int32, (steps, steps), 1)
    later = row >= col
    decay = d_ref[0]
    cum = jnp.dot(later.astype(F32), decay, precision=HI, preferred_element_type=F32)
    cum_ref[0] = cum
    turned = cum.T
    final = cum[steps - 1 : steps, :]
    tail = jnp.exp(final - cum)
    ends = jnp.exp(final)
    piece = lax.broadcasted_iota(jnp.int32, (DEC, HEAD), 0)
    half = HEAD // 2
    for h in range(heads):
        sl = slice(h * HEAD, (h + 1) * HEAD)
        q, k, v = q_ref[0, :, sl], k_ref[0, :, sl], v_ref[0, :, sl]
        scores = lax.dot_general(q, k, (((1,), (1,)), ((), ())), preferred_element_type=F32)
        spread = cum[:, h : h + 1] - turned[h : h + 1, :]
        weights = jnp.where(later, jnp.exp(jnp.minimum(spread, 0.0)), 0.0) * scores
        whi, wlo = split(weights)
        inner_ref[0, :, sl] = mm(whi, v) + mm(wlo, v)
        khi, klo = split(k.astype(F32) * tail[:, h : h + 1])
        update = (mm0(khi, v) + mm0(klo, v)).astype(BF)
        end = jnp.broadcast_to(ends[:, h : h + 1], (DEC, HEAD))
        e1 = end.astype(BF).astype(F32)
        e2 = (end - e1).astype(BF).astype(F32)
        e3 = end - e1 - e2
        rows = jnp.where(piece == 0, e1, jnp.where(piece == 1, e2, jnp.where(piece == 2, e3, 0.0)))
        for r in range(2):
            state_ref[2 * h + r, :half, :] = update[r * half : (r + 1) * half]
            state_ref[2 * h + r, half:, :] = rows.astype(BF)


def local_part(q, k, v, d):
    seqs, steps, width = q.shape
    heads = width // HEAD
    half = HEAD // 2
    block = pl.BlockSpec((1, steps, width), lambda s: (s, 0, 0))
    thin = pl.BlockSpec((1, steps, heads), lambda s: (s, 0, 0))
    return pl.pallas_call(
        local_kernel,
        grid=(seqs,),
        in_specs=[block, block, block, thin],
        out_specs=[block, pl.BlockSpec((2 * heads, half + DEC, HEAD), lambda s: (s, 0, 0)), thin],
        out_shape=[
            jax.ShapeDtypeStruct((seqs, steps, width), F32),
            jax.ShapeDtypeStruct((seqs * heads * 2, half + DEC, HEAD), BF),
            jax.ShapeDtypeStruct((seqs, steps, heads), F32),
        ],
        compiler_params=pltpu.CompilerParams(vmem_limit_bytes=48 * 2**20),
        name="local_attention",
    )(q, k, v, d)


def scan_kernel(in_ref, out_ref):
    blocks = in_ref.shape[0]
    half = out_ref.shape[1]
    carry = jnp.zeros(out_ref.shape[1:], F32)
    for n in range(blocks):
        out_ref[n] = carry.astype(BF)
        dec = in_ref[n, half:, :].astype(F32)
        carry = carry * (dec[0:1] + dec[1:2] + dec[2:3]) + in_ref[n, :half, :].astype(F32)


def scan_states(arrived):
    blocks, rows, width = arrived.shape
    return pl.pallas_call(
        scan_kernel,
        out_shape=jax.ShapeDtypeStruct((blocks, rows - DEC, width), BF),
        compiler_params=pltpu.CompilerParams(vmem_limit_bytes=48 * 2**20),
        name="state_prefix",
    )(arrived)


def carry_kernel(me_ref, q_ref, inner_ref, cum_ref, state_ref, gain_ref, out_ref):
    shares, slice_len = out_ref.shape[0], out_ref.shape[2]
    heads = cum_ref.shape[2]
    grow = jnp.exp(cum_ref[0])
    me = me_ref[0]
    for h in range(heads):
        sl = slice(h * HEAD, (h + 1) * HEAD)
        head = inner_ref[0, :, sl] + mm(q_ref[0, :, sl], state_ref[h]) * grow[:, h : h + 1]
        scale = lax.rsqrt(jnp.mean(head * head, -1, keepdims=True) + 1e-06)
        normed = (head * scale * gain_ref[:, sl]).astype(BF)
        for a in range(shares):
            out_ref[lax.rem(a - me + shares, shares), 0, :, sl] = normed[
                a * slice_len : (a + 1) * slice_len
            ]


def carried(me, q, inner, cum, state, gain, shares):
    seqs, steps, width = q.shape
    heads = width // HEAD
    block = pl.BlockSpec((1, steps, width), lambda s: (s, 0, 0))
    return pl.pallas_call(
        carry_kernel,
        grid=(seqs,),
        in_specs=[
            pl.BlockSpec(memory_space=pltpu.SMEM),
            block,
            block,
            pl.BlockSpec((1, steps, heads), lambda s: (s, 0, 0)),
            pl.BlockSpec((heads, HEAD, HEAD), lambda s: (s, 0, 0)),
            pl.BlockSpec((1, width), lambda s: (0, 0)),
        ],
        out_specs=pl.BlockSpec((shares, 1, steps // shares, width), lambda s: (0, s, 0, 0)),
        out_shape=jax.ShapeDtypeStruct((shares, seqs, steps // shares, width), BF),
        compiler_params=pltpu.CompilerParams(vmem_limit_bytes=48 * 2**20),
        name="carried_norm",
    )(me, q, inner, cum, state, gain)


def route_kernel(cap, me_ref, routes_ref, place_ref):
    flight, rows = routes_ref.shape[1] // 128, 128
    total = routes_ref.shape[1]
    me = me_ref[0]
    a = lax.broadcasted_iota(jnp.int32, (total, total), 0)
    b = lax.broadcasted_iota(jnp.int32, (total, total), 1)
    before = ((a < b) & (a // rows == b // rows)).astype(BF)
    first, second = routes_ref[0:1, :], routes_ref[1:2, :]
    home = lax.broadcasted_iota(jnp.int32, (1, total), 1) // rows
    slots = lax.broadcasted_iota(jnp.int32, (flight * cap, total), 0)
    for r, off in enumerate(OFFS):
        expert = lax.rem(me + off, flight)
        chosen = ((first == expert) | (second == expert)).astype(F32)
        rank = mm(jnp.broadcast_to(chosen, (8, total)).astype(BF), before)[0:1].astype(jnp.int32)
        start = jnp.zeros((1, total), jnp.int32)
        for delta in range(flight):
            start = jnp.where(home == delta, cap * JREL[(delta - off) % 4], start)
        target = jnp.where(chosen > 0.0, start + rank, -1)
        hits = (slots == target).astype(F32).astype(BF)
        place_ref[r * flight * cap : (r + 1) * flight * cap, :] = hits


def call(kernel, name, outs, *args, **kw):
    limit = kw.pop("vmem", 40)
    return pl.pallas_call(
        kernel,
        out_shape=[jax.ShapeDtypeStruct(s, d) for s, d in outs],
        compiler_params=pltpu.CompilerParams(vmem_limit_bytes=limit * 2**20),
        name=name,
        **kw,
    )(*args)


VM = pl.BlockSpec(memory_space=pltpu.VMEM)
SM = pl.BlockSpec(memory_space=pltpu.SMEM)
ANY = pl.BlockSpec(memory_space=pl.ANY)


def route(me, routes, cap):
    total = routes.shape[1]
    flight = total // 128
    return call(
        functools.partial(route_kernel, cap),
        "route",
        [((flight * flight * cap, total), BF)],
        me,
        routes,
        in_specs=[SM, VM],
        out_specs=[VM],
    )[0]


def nt(a, b):
    return lax.dot_general(a, b, (((1,), (1,)), ((), ())), preferred_element_type=F32)


def selected_kernel(place_ref, normed_ref, weight_ref, res_ref, o0, o1, o2, o3, picked):
    rows = res_ref.shape[0]

    @pl.when(pl.program_id(0) == 0)
    def _():
        picked[...] = mm(place_ref[...], normed_ref[...]).astype(BF)

    full = nt(picked[...], weight_ref[...]) + mm(place_ref[:, :rows], res_ref[...])
    full = full.astype(BF)
    size = o0.shape[0]
    for i, o in enumerate((o0, o1, o2, o3)):
        o[...] = full[i * size : (i + 1) * size]


def selected(place, normed, weight, res, tile=1024):
    picks, (model, width) = place.shape[0], weight.shape
    rows = res.shape[0]
    size = picks // 4
    whole = lambda a: pl.BlockSpec(a.shape, lambda n: (0, 0))
    return call(
        selected_kernel,
        "selected_projection",
        [((size, model), BF)] * 4,
        place,
        normed,
        weight,
        res,
        grid=(model // tile,),
        in_specs=[
            whole(place),
            whole(normed),
            pl.BlockSpec((tile, width), lambda n: (n, 0)),
            pl.BlockSpec((rows, tile), lambda n: (0, n)),
        ],
        out_specs=[pl.BlockSpec((size, tile), lambda n: (0, n))] * 4,
        scratch_shapes=[pltpu.VMEM((picks, width), BF)],
    )


def whole_kernel(normed_ref, weight_ref, o0, o1, o2, o3):
    full = nt(normed_ref[...], weight_ref[...]).astype(BF)
    size = o0.shape[0]
    for i, o in enumerate((o0, o1, o2, o3)):
        o[...] = full[i * size : (i + 1) * size]


def whole_projection(normed, weight, tile=1024):
    total, (model, width) = normed.shape[0], weight.shape
    size = total // 4
    return call(
        whole_kernel,
        "whole_projection",
        [((size, model), BF)] * 4,
        normed,
        weight,
        grid=(model // tile,),
        in_specs=[
            pl.BlockSpec(normed.shape, lambda n: (0, 0)),
            pl.BlockSpec((tile, width), lambda n: (n, 0)),
        ],
        out_specs=[pl.BlockSpec((size, tile), lambda n: (0, n))] * 4,
        cost_estimate=pl.CostEstimate(
            flops=2 * total * model * width, bytes_accessed=4 * model * width, transcendentals=0
        ),
    )


def norm_kernel(a, b, c, d, gain, o0, o1):
    x = a[...].astype(F32) + b[...].astype(F32) + c[...].astype(F32) + d[...].astype(F32)
    x = x * lax.rsqrt(jnp.mean(x * x, -1, keepdims=True) + 1e-06) * gain[...]
    half = o0.shape[1]
    o0[...] = x[:, :half].astype(BF)
    o1[...] = x[:, half:].astype(BF)


def stack_kernel(a0, a1, a2, a3, b0, b1, b2, b3, p0, p1, p2, o0, o1, q0, q1, q2):
    for i, (a, b) in enumerate(((a0, b0), (a1, b1), (a2, b2), (a3, b3))):
        o0[i] = a[...]
        o1[i] = b[...]


def expert_kernel(half_steps, *refs):
    xa, xb = refs[0:5], refs[5:10]
    gate0, gate1, up0, up1, down0, down1 = refs[10:16]
    oa, ob = refs[16:21], refs[21:26]
    x, gates, uppers, hidden = refs[26:]
    step = pl.program_id(0)
    rows, units = xa[0].shape[1], gate0.shape[0]
    steps = 2 * half_steps

    def piece(refs, u, v):
        if u < 3:
            return refs[u].at[v]
        return refs[3].at[v] if v < 2 else refs[4].at[v - 2]

    def span(z, y):
        return pl.ds((z * 4 + y) * rows, rows)

    @pl.when(step < half_steps)
    def _():
        for z in range(4):
            for y in range(4):
                x[span(z, y), :] = piece(xa, z, y)[...]

    @pl.when((step >= half_steps) & (step < steps))
    def _():
        for z in range(4):
            for y in range(4):
                x[span(z, y), :] = piece(xb, y, z)[...]

    @pl.when(step < steps)
    def _():
        for i, (g, u) in enumerate(((gate0, up0), (gate1, up1))):
            sl = slice(i * units, (i + 1) * units)
            new_g, new_u = nt(g[...], x[...]), nt(u[...], x[...])

            @pl.when(step == 0)
            def _():
                gates[sl, :] = new_g
                uppers[sl, :] = new_u

            @pl.when(step > 0)
            def _():
                gates[sl, :] += new_g
                uppers[sl, :] += new_u

    @pl.when(step == steps - 1)
    def _():
        g = gates[...]
        hidden[...] = (g / (1.0 + jnp.exp(-g)) * uppers[...]).T.astype(BF)

    def out(write):
        full = mm(hidden[:, :units], down0[...]) + mm(hidden[:, units:], down1[...])
        for z in range(4):
            for y in range(4):
                at = (z * 4 + y) * rows
                write(z, y, full[at : at + rows].astype(BF))

    @pl.when((step >= steps) & (step < steps + half_steps))
    def _():
        def write(z, y, v):
            piece(oa, z, y)[...] = v

        out(write)

    @pl.when(step >= steps + half_steps)
    def _():
        def write(z, y, v):
            piece(ob, y, z)[...] = v

        out(write)


def expert(xa, xb, gates, ups, downs, tile=1024):
    rows, half = xa[0].shape[1], xa[0].shape[2]
    units = gates[0].shape[0]
    n = half // tile

    def clip(low):
        return lambda s: jnp.clip(s - low, 0, n - 1)

    def cols(low):
        at = clip(low)
        return [pl.BlockSpec((k, rows, tile), lambda s: (0, 0, at(s))) for k in (4, 4, 4, 2, 2)]

    first = pl.BlockSpec((units, tile), lambda s: (0, jnp.clip(s, 0, 2 * n - 1)))
    last = pl.BlockSpec((units, tile), lambda s: (0, jnp.clip(s - 2 * n, 0, 2 * n - 1)))
    total = 16 * rows
    outs = call(
        functools.partial(expert_kernel, n),
        "expert",
        [((k, rows, half), BF) for k in (4, 4, 4, 2, 2)] * 2,
        *xa,
        *xb,
        *gates,
        *ups,
        *downs,
        grid=(4 * n,),
        in_specs=cols(0) + cols(n) + [first] * 4 + [last] * 2,
        out_specs=cols(2 * n) + cols(3 * n),
        scratch_shapes=[
            pltpu.VMEM((total, tile), BF),
            pltpu.VMEM((2 * units, total), F32),
            pltpu.VMEM((2 * units, total), F32),
            pltpu.VMEM((total, 2 * units), BF),
        ],
        vmem=56,
    )
    return outs[:5], outs[5:]


def fold_kernel(bl0, ab0, up0, dn0, bl1, ab1, up1, dn1, ob0, oa0, ob1, oa1):
    for below, above, up, down, o_below, o_above in (
        (bl0, ab0, up0, dn0, ob0, oa0),
        (bl1, ab1, up1, dn1, ob1, oa1),
    ):
        o_above[0:2] = (above[0:2].astype(F32) + up[...].astype(F32)).astype(BF)
        o_above[2:4] = above[2:4]
        o_below[0:2] = below[0:2]
        o_below[2:4] = (below[2:4].astype(F32) + down[...].astype(F32)).astype(BF)


def phase_kernel(m0, u0, d0, m1, u1, d1, *outs):
    for k, (m, u, d) in enumerate(((m0, u0, d0), (m1, u1, d1))):
        total = m[...].astype(F32) + u[...].astype(F32) + d[...].astype(F32)
        for i in range(4):
            outs[4 * k + i][...] = total[i].astype(BF)


def served_kernel(cap, a0, a1, a2, a3, b0, b1, b2, b3, o0, o1, o2, o3):
    half = a0.shape[1]
    rows = a0.shape[0]
    padded = o0.shape[0]
    r = lax.broadcasted_iota(jnp.int32, (padded, rows), 0)
    c = lax.broadcasted_iota(jnp.int32, (padded, rows), 1)
    for k, parts in enumerate(((a0, a1, a2, a3), (b0, b1, b2, b3))):
        total = sum(p[...].astype(F32) for p in parts).astype(BF)
        for i, o in enumerate((o0, o1, o2, o3)):
            pick = ((c == r + i * cap) & (r < cap)).astype(F32).astype(BF)
            o[:, k * half : (k + 1) * half] = mm(pick, total).astype(BF)


def home_kernel(me_ref, routes_ref, res, own, r1, r2, r3, gain, router, late, hidden_ref, hi_ref, lo_ref):
    x = res[...].astype(F32)
    for p in (own, r1, r2, r3):
        x = x + p[...].astype(F32)
    hidden_ref[...] = x
    normed = (x * lax.rsqrt(jnp.mean(x * x, -1, keepdims=True) + 1e-06) * gain[...]).astype(BF)
    logits = mm(normed, router[...])
    rows, experts = logits.shape
    labels = lax.broadcasted_iota(jnp.int32, (rows, experts), 1)
    one, two = routes_ref[:, 0:1], routes_ref[:, 1:2]
    first = jnp.sum(jnp.where(one == labels, logits, 0.0), -1, keepdims=True)
    second = jnp.sum(jnp.where(two == labels, logits, 0.0), -1, keepdims=True)
    gate0 = 1.0 / (1.0 + jnp.exp(second - first))
    gate1 = 1.0 / (1.0 + jnp.exp(first - second))
    cols = hi_ref.shape[1]
    place = lax.broadcasted_iota(jnp.int32, (rows, cols), 1)
    a = lax.broadcasted_iota(jnp.int32, (rows, rows), 0)
    b = lax.broadcasted_iota(jnp.int32, (rows, rows), 1)
    before = (b < a).astype(F32).astype(BF)
    total = jnp.zeros((rows, cols), F32)
    for j, off in enumerate((0, 1, 3, 2)):
        expert_id = lax.rem(me_ref[0] + off, 4)
        hit0, hit1 = (one == expert_id).astype(F32), (two == expert_id).astype(F32)
        chosen = hit0 + hit1
        rank = mm(before, jnp.broadcast_to(chosen, (rows, 128)).astype(BF))[:, 0:1].astype(jnp.int32)
        total = total + jnp.where(place == rank + 16 * j, hit0 * gate0 + hit1 * gate1, 0.0)
    hi, lo = split(total)
    hi_ref[...] = hi
    lo_ref[...] = lo


def final_kernel(hidden, hi, lo, b0, b1, b2, b3, out, back):
    for i, b in enumerate((b0, b1, b2, b3)):
        back[16 * i : 16 * i + 16, :] = b[...]
    moe = mm(hi[...], back[...]) + mm(lo[...], back[...])
    out[...] = (hidden[...] + moe).astype(BF)


def up_one(x, axis):
    return lax.ppermute(x, axis, ring(4, 1))


def down_one(x, axis):
    return lax.ppermute(x, axis, ring(4, -1))


def across(x, axis):
    return lax.ppermute(x, axis, ring(4, 2))


def far_sides(below, above, axis):
    return up_one(below[:2], axis), down_one(above[2:], axis)


def shards(
    queries,
    keys,
    payload_vectors,
    log_decay,
    attn_gain,
    out_weight,
    residual,
    norm_gain,
    router_weight,
    picks,
    gate_weight,
    up_weight,
    down_weight,
):
    seqs, positions, width = queries.shape
    slice_len, model = residual.shape[1], residual.shape[2]
    shares = positions // slice_len
    rows = seqs * slice_len
    cap = 3 * rows // 32
    half = model // 2
    me = lax.axis_index("x").astype(jnp.int32).reshape(1)

    weight_out = lax.all_gather(out_weight.T, SEQ, axis=0, tiled=True)
    swap = ring(2, 1)
    gates, ups, downs = [
        (w[0], lax.ppermute(w[0], "core", swap)) for w in (gate_weight, up_weight, down_weight)
    ]
    routes = picks.reshape(rows, 2)
    turned = routes.T
    all_routes = jnp.concatenate(
        [turned] + [lax.ppermute(turned, "x", ring(4, -delta)) for delta in (1, 2, 3)], axis=1
    )

    inner, states, cum = local_part(queries, keys, payload_vectors, log_decay)
    arrived = lax.all_to_all(states, SEQ, 0, 0, tiled=True)
    prefix = lax.all_to_all(scan_states(arrived), SEQ, 0, 0, tiled=True)
    prefix = prefix.reshape(seqs * width // HEAD, HEAD, HEAD)
    normed = carried(
        me, queries, inner, cum, prefix, attn_gain.reshape(1, width), shares
    ).reshape(shares * rows, width)

    place = route(me, all_routes, cap)
    flat = residual.reshape(rows, model)
    gain = norm_gain.reshape(1, model)
    to_up, to_down, to_far, here = selected(place, normed, weight_out, flat)
    own, d1, d2, d3 = whole_projection(normed, weight_out)

    size = here.shape[0]
    a0, b0 = call(
        norm_kernel,
        "selected_norm",
        [((size, half), BF)] * 2,
        here,
        up_one(to_up, "x"),
        down_one(to_down, "x"),
        across(to_far, "x"),
        gain,
        in_specs=[VM] * 5,
        out_specs=[VM] * 2,
    )

    a4, b4, d1, d2, d3 = call(
        stack_kernel,
        "stack",
        [((4, size, half), BF)] * 2 + [((rows, model), BF)] * 3,
        a0,
        up_one(a0, "y"),
        down_one(a0, "y"),
        across(a0, "y"),
        b0,
        up_one(b0, "z"),
        down_one(b0, "z"),
        across(b0, "z"),
        d1,
        d2,
        d3,
        in_specs=[VM] * 8 + [ANY] * 3,
        out_specs=[VM] * 2 + [ANY] * 3,
        input_output_aliases={8: 2, 9: 3, 10: 4},
    )
    a_below, a_above = up_one(a4, "z"), down_one(a4, "z")
    b_below, b_above = up_one(b4, "y"), down_one(b4, "y")
    a_far, b_far = far_sides(a_below, a_above, "z"), far_sides(b_below, b_above, "y")

    oa, ob = expert(
        (a4, a_below, a_above, *a_far), (b4, b_below, b_above, *b_far), gates, ups, downs
    )
    a_below, a_above, b_below, b_above = call(
        fold_kernel,
        "fold",
        [((4, size, half), BF)] * 4,
        oa[1],
        oa[2],
        up_one(oa[3], "z"),
        down_one(oa[4], "z"),
        ob[1],
        ob[2],
        up_one(ob[3], "y"),
        down_one(ob[4], "y"),
        in_specs=[VM] * 8,
        out_specs=[VM] * 4,
    )
    parts = call(
        phase_kernel,
        "phase",
        [((size, half), BF)] * 8,
        oa[0],
        up_one(a_above, "z"),
        down_one(a_below, "z"),
        ob[0],
        up_one(b_above, "y"),
        down_one(b_below, "y"),
        in_specs=[VM] * 6,
        out_specs=[VM] * 8,
    )
    s0, s1, s2, s3 = call(
        functools.partial(served_kernel, cap),
        "served",
        [((16, model), BF)] * 4,
        parts[0],
        up_one(parts[2], "y"),
        down_one(parts[1], "y"),
        across(parts[3], "y"),
        parts[4],
        up_one(parts[6], "z"),
        down_one(parts[5], "z"),
        across(parts[7], "z"),
        in_specs=[VM] * 8,
        out_specs=[VM] * 4,
    )

    hidden, hi, lo = call(
        home_kernel,
        "home",
        [((rows, model), F32), ((rows, 64), BF), ((rows, 64), BF)],
        me,
        routes,
        flat,
        own,
        up_one(d1, "x"),
        across(d2, "x"),
        down_one(d3, "x"),
        gain,
        router_weight,
        parts[0],
        in_specs=[SM] + [VM] * 8 + [ANY],
        out_specs=[VM] * 3,
        vmem=56,
    )
    out = call(
        final_kernel,
        "combine",
        [((rows, model), BF)],
        hidden,
        hi,
        lo,
        s0,
        down_one(s1, "x"),
        up_one(s2, "x"),
        across(s3, "x"),
        in_specs=[VM] * 7,
        out_specs=[VM],
        scratch_shapes=[pltpu.VMEM((64, model), BF)],
    )[0]
    return out.reshape(seqs, slice_len, model)


def solution(mesh):
    shape = dict(mesh.shape)
    grid = Mesh(mesh.devices.reshape(4, shape["seq"] // 8, 2, shape["exp"]), SEQ + ("x",))
    everyone = SEQ + ("x",)
    placed = (
        P(None, SEQ, "x"),
        P(None, SEQ, "x"),
        P(None, SEQ, "x"),
        P(None, SEQ, "x"),
        P("x"),
        P("x", SEQ),
        P(None, everyone, None),
        P(),
        P(),
        P(None, everyone, None),
        P("x", SEQ, None),
        P("x", SEQ, None),
        P("x", SEQ, None),
    )
    return jax.shard_map(
        shards, mesh=grid, in_specs=placed, out_specs=P(None, everyone, None), check_vma=False
    )
```

```python
import functools

import jax
import jax.numpy as jnp
from jax import lax
from jax.experimental import pallas as pl
from jax.experimental.pallas import tpu as pltpu
from jax.sharding import Mesh, PartitionSpec as P

HEAD = 128
BF = jnp.bfloat16
F32 = jnp.float32
HI = lax.Precision.HIGHEST
SEQ = ("z", "y", "core")
DEC = 16
OFFS = (1, 3, 2, 0)
JREL = {0: 0, 3: 1, 1: 2, 2: 3}


def ring(n, k):
    return [(i, (i + k) % n) for i in range(n)]


def mm(a, b):
    return jnp.dot(a, b, preferred_element_type=F32)


def mm0(a, b):
    return lax.dot_general(a, b, (((0,), (0,)), ((), ())), preferred_element_type=F32)


def split(a):
    hi = a.astype(BF)
    return hi, (a - hi.astype(F32)).astype(BF)


def local_kernel(q_ref, k_ref, v_ref, d_ref, inner_ref, state_ref, cum_ref):
    steps, heads = d_ref.shape[1], d_ref.shape[2]
    row = lax.broadcasted_iota(jnp.int32, (steps, steps), 0)
    col = lax.broadcasted_iota(jnp.int32, (steps, steps), 1)
    later = row >= col
    decay = d_ref[0]
    cum = jnp.dot(later.astype(F32), decay, precision=HI, preferred_element_type=F32)
    cum_ref[0] = cum
    turned = cum.T
    final = cum[steps - 1 : steps, :]
    tail = jnp.exp(final - cum)
    ends = jnp.exp(final)
    piece = lax.broadcasted_iota(jnp.int32, (DEC, HEAD), 0)
    half = HEAD // 2
    for h in range(heads):
        sl = slice(h * HEAD, (h + 1) * HEAD)
        q, k, v = q_ref[0, :, sl], k_ref[0, :, sl], v_ref[0, :, sl]
        scores = lax.dot_general(q, k, (((1,), (1,)), ((), ())), preferred_element_type=F32)
        spread = cum[:, h : h + 1] - turned[h : h + 1, :]
        weights = jnp.where(later, jnp.exp(jnp.minimum(spread, 0.0)), 0.0) * scores
        whi, wlo = split(weights)
        inner_ref[0, :, sl] = mm(whi, v) + mm(wlo, v)
        khi, klo = split(k.astype(F32) * tail[:, h : h + 1])
        update = (mm0(khi, v) + mm0(klo, v)).astype(BF)
        end = jnp.broadcast_to(ends[:, h : h + 1], (DEC, HEAD))
        e1 = end.astype(BF).astype(F32)
        e2 = (end - e1).astype(BF).astype(F32)
        e3 = end - e1 - e2
        rows = jnp.where(piece == 0, e1, jnp.where(piece == 1, e2, jnp.where(piece == 2, e3, 0.0)))
        for r in range(2):
            state_ref[2 * h + r, :half, :] = update[r * half : (r + 1) * half]
            state_ref[2 * h + r, half:, :] = rows.astype(BF)


def local_part(q, k, v, d):
    seqs, steps, width = q.shape
    heads = width // HEAD
    half = HEAD // 2
    block = pl.BlockSpec((1, steps, width), lambda s: (s, 0, 0))
    thin = pl.BlockSpec((1, steps, heads), lambda s: (s, 0, 0))
    return pl.pallas_call(
        local_kernel,
        grid=(seqs,),
        in_specs=[block, block, block, thin],
        out_specs=[block, pl.BlockSpec((2 * heads, half + DEC, HEAD), lambda s: (s, 0, 0)), thin],
        out_shape=[
            jax.ShapeDtypeStruct((seqs, steps, width), F32),
            jax.ShapeDtypeStruct((seqs * heads * 2, half + DEC, HEAD), BF),
            jax.ShapeDtypeStruct((seqs, steps, heads), F32),
        ],
        compiler_params=pltpu.CompilerParams(vmem_limit_bytes=48 * 2**20),
        name="local_attention",
    )(q, k, v, d)


def scan_kernel(in_ref, out_ref):
    blocks = in_ref.shape[0]
    half = out_ref.shape[1]
    carry = jnp.zeros(out_ref.shape[1:], F32)
    for n in range(blocks):
        out_ref[n] = carry.astype(BF)
        dec = in_ref[n, half:, :].astype(F32)
        carry = carry * (dec[0:1] + dec[1:2] + dec[2:3]) + in_ref[n, :half, :].astype(F32)


def scan_states(arrived):
    blocks, rows, width = arrived.shape
    return pl.pallas_call(
        scan_kernel,
        out_shape=jax.ShapeDtypeStruct((blocks, rows - DEC, width), BF),
        compiler_params=pltpu.CompilerParams(vmem_limit_bytes=48 * 2**20),
        name="state_prefix",
    )(arrived)


def carry_kernel(q_ref, inner_ref, cum_ref, state_ref, gain_ref, out_ref):
    shares, slice_len = out_ref.shape[0], out_ref.shape[2]
    heads = cum_ref.shape[2]
    grow = jnp.exp(cum_ref[0])
    for h in range(heads):
        sl = slice(h * HEAD, (h + 1) * HEAD)
        head = inner_ref[0, :, sl] + mm(q_ref[0, :, sl], state_ref[h]) * grow[:, h : h + 1]
        scale = lax.rsqrt(jnp.mean(head * head, -1, keepdims=True) + 1e-06)
        normed = (head * scale * gain_ref[:, sl]).astype(BF)
        for a in range(shares):
            out_ref[a, 0, :, sl] = normed[
                a * slice_len : (a + 1) * slice_len
            ]


def carried(q, inner, cum, state, gain, shares):
    seqs, steps, width = q.shape
    heads = width // HEAD
    block = pl.BlockSpec((1, steps, width), lambda s: (s, 0, 0))
    return pl.pallas_call(
        carry_kernel,
        grid=(seqs,),
        in_specs=[
            block,
            block,
            pl.BlockSpec((1, steps, heads), lambda s: (s, 0, 0)),
            pl.BlockSpec((heads, HEAD, HEAD), lambda s: (s, 0, 0)),
            pl.BlockSpec((1, width), lambda s: (0, 0)),
        ],
        out_specs=pl.BlockSpec((shares, 1, steps // shares, width), lambda s: (0, s, 0, 0)),
        out_shape=jax.ShapeDtypeStruct((shares, seqs, steps // shares, width), BF),
        compiler_params=pltpu.CompilerParams(vmem_limit_bytes=48 * 2**20),
        name="carried_norm",
    )(q, inner, cum, state, gain)


def route_kernel(cap, me_ref, routes_ref, place_ref, own_ref):
    flight, rows = routes_ref.shape[1] // 128, 128
    total = routes_ref.shape[1]
    me = me_ref[0]
    a = lax.broadcasted_iota(jnp.int32, (total, total), 0)
    b = lax.broadcasted_iota(jnp.int32, (total, total), 1)
    before = ((a < b) & (a // rows == b // rows)).astype(BF)
    first, second = routes_ref[0:1, :], routes_ref[1:2, :]
    home = lax.broadcasted_iota(jnp.int32, (1, total), 1) // rows
    slots = lax.broadcasted_iota(jnp.int32, (flight * cap, total), 0)
    for r, off in enumerate(OFFS):
        expert = lax.rem(me + off, flight)
        chosen = ((first == expert) | (second == expert)).astype(F32)
        rank = mm(jnp.broadcast_to(chosen, (8, total)).astype(BF), before)[0:1].astype(jnp.int32)
        start = jnp.zeros((1, total), jnp.int32)
        for delta in range(flight):
            start = jnp.where(home == delta, cap * JREL[(delta - off) % 4], start)
        target = jnp.where(chosen > 0.0, start + rank, -1)
        hits = (slots == target).astype(F32).astype(BF)
        span = slice(r * flight * cap, (r + 1) * flight * cap)
        own_ref[span, :] = hits[:, :rows]
        for delta in range(flight):
            at = pl.multiple_of(lax.rem(me + delta, flight) * rows, rows)
            place_ref[span, pl.ds(at, rows)] = hits[:, delta * rows : (delta + 1) * rows]


def call(kernel, name, outs, *args, **kw):
    limit = kw.pop("vmem", 40)
    return pl.pallas_call(
        kernel,
        out_shape=[jax.ShapeDtypeStruct(s, d) for s, d in outs],
        compiler_params=pltpu.CompilerParams(vmem_limit_bytes=limit * 2**20),
        name=name,
        **kw,
    )(*args)


VM = pl.BlockSpec(memory_space=pltpu.VMEM)
SM = pl.BlockSpec(memory_space=pltpu.SMEM)
ANY = pl.BlockSpec(memory_space=pl.ANY)


def route(me, routes, cap):
    total = routes.shape[1]
    flight = total // 128
    return call(
        functools.partial(route_kernel, cap),
        "route",
        [((flight * flight * cap, n), BF) for n in (total, 128)],
        me,
        routes,
        in_specs=[SM, VM],
        out_specs=[VM, VM],
    )


def nt(a, b):
    return lax.dot_general(a, b, (((1,), (1,)), ((), ())), preferred_element_type=F32)


def selected_kernel(place_ref, own_ref, normed_ref, weight_ref, res_ref, o0, o1, o2, o3, picked):

    @pl.when(pl.program_id(0) == 0)
    def _():
        picked[...] = mm(place_ref[...], normed_ref[...]).astype(BF)

    full = nt(picked[...], weight_ref[...]) + mm(own_ref[...], res_ref[...])
    full = full.astype(BF)
    size = o0.shape[0]
    for i, o in enumerate((o0, o1, o2, o3)):
        o[...] = full[i * size : (i + 1) * size]


def selected(place, own, normed, weight, res, tile=1024):
    picks, (model, width) = place.shape[0], weight.shape
    rows = res.shape[0]
    size = picks // 4
    whole = lambda a: pl.BlockSpec(a.shape, lambda n: (0, 0))
    return call(
        selected_kernel,
        "selected_projection",
        [((size, model), BF)] * 4,
        place,
        own,
        normed,
        weight,
        res,
        grid=(model // tile,),
        in_specs=[
            whole(place),
            whole(own),
            whole(normed),
            pl.BlockSpec((tile, width), lambda n: (n, 0)),
            pl.BlockSpec((rows, tile), lambda n: (0, n)),
        ],
        out_specs=[pl.BlockSpec((size, tile), lambda n: (0, n))] * 4,
        scratch_shapes=[pltpu.VMEM((picks, width), BF)],
    )


def whole_kernel(normed_ref, weight_ref, out_ref):
    out_ref[...] = nt(normed_ref[...], weight_ref[...]).astype(BF)


def whole_projection(normed, weight, tile=1024):
    total, (model, width) = normed.shape[0], weight.shape
    return call(
        whole_kernel,
        "whole_projection",
        [((total, model), BF)],
        normed,
        weight,
        grid=(model // tile,),
        in_specs=[
            pl.BlockSpec(normed.shape, lambda n: (0, 0)),
            pl.BlockSpec((tile, width), lambda n: (n, 0)),
        ],
        out_specs=[pl.BlockSpec((total, tile), lambda n: (0, n))],
        cost_estimate=pl.CostEstimate(
            flops=2 * total * model * width, bytes_accessed=4 * model * width, transcendentals=0
        ),
    )[0]


def norm_kernel(a, b, c, d, gain, held, o0, o1, same):
    x = a[...].astype(F32) + b[...].astype(F32) + c[...].astype(F32) + d[...].astype(F32)
    x = x * lax.rsqrt(jnp.mean(x * x, -1, keepdims=True) + 1e-06) * gain[...]
    half = o0.shape[1]
    o0[...] = x[:, :half].astype(BF)
    o1[...] = x[:, half:].astype(BF)


def stack_kernel(a0, a1, a2, a3, b0, b1, b2, b3, w0, w1, w2, o0, o1, *same):
    for i, (a, b) in enumerate(((a0, b0), (a1, b1), (a2, b2), (a3, b3))):
        o0[i] = a[...]
        o1[i] = b[...]


def expert_kernel(tile, *refs):
    xa, xb = refs[0:5], refs[5:10]
    gate, up, down = refs[10:13]
    oa, ob = refs[13:18], refs[18:23]
    x, gates, uppers, hidden = refs[23:]
    rows, half = xa[0].shape[1], xa[0].shape[2]

    def piece(refs, u, v):
        if u < 3:
            return refs[u], v
        return (refs[3], v) if v < 2 else (refs[4], v - 2)

    def pieces(refs, flip):
        for z in range(4):
            for y in range(4):
                ref, i = piece(refs, y, z) if flip else piece(refs, z, y)
                yield (z * 4 + y) * rows, ref, i

    gates[...] = jnp.zeros_like(gates)
    uppers[...] = jnp.zeros_like(uppers)
    for k, (refs_x, flip) in enumerate(((xa, False), (xb, True))):

        @pl.loop(0, half // tile)
        def _(c):
            at = pl.ds(pl.multiple_of(c * tile, tile), tile)
            wide = pl.ds(pl.multiple_of(k * half + c * tile, tile), tile)
            for row, ref, i in pieces(refs_x, flip):
                x[row : row + rows, :] = ref[i, :, at]
            gates[...] += nt(gate[:, wide], x[...])
            uppers[...] += nt(up[:, wide], x[...])

    g = gates[...]
    hidden[...] = (g / (1.0 + jnp.exp(-g)) * uppers[...]).T.astype(BF)
    for k, (refs_o, flip) in enumerate(((oa, False), (ob, True))):

        @pl.loop(0, half // tile)
        def _(c):
            at = pl.ds(pl.multiple_of(c * tile, tile), tile)
            wide = pl.ds(pl.multiple_of(k * half + c * tile, tile), tile)
            full = mm(hidden[...], down[:, wide]).astype(BF)
            for row, ref, i in pieces(refs_o, flip):
                ref[i, :, at] = full[row : row + rows]


def expert(xa, xb, gate, up, down, tile=1024):
    rows, half = xa[0].shape[1], xa[0].shape[2]
    units = gate.shape[0]
    total = 16 * rows
    outs = call(
        functools.partial(expert_kernel, tile),
        "expert",
        [((k, rows, half), BF) for k in (4, 4, 4, 2, 2)] * 2,
        *xa,
        *xb,
        gate,
        up,
        down,
        in_specs=[VM] * 13,
        out_specs=[VM] * 10,
        scratch_shapes=[
            pltpu.VMEM((total, tile), BF),
            pltpu.VMEM((units, total), F32),
            pltpu.VMEM((units, total), F32),
            pltpu.VMEM((total, units), BF),
        ],
        vmem=20,
    )
    return outs[:5], outs[5:]


def fold_kernel(bl0, ab0, up0, dn0, bl1, ab1, up1, dn1, ob0, oa0, ob1, oa1):
    for below, above, up, down, o_below, o_above in (
        (bl0, ab0, up0, dn0, ob0, oa0),
        (bl1, ab1, up1, dn1, ob1, oa1),
    ):
        o_above[0:2] = (above[0:2].astype(F32) + up[...].astype(F32)).astype(BF)
        o_above[2:4] = above[2:4]
        o_below[0:2] = below[0:2]
        o_below[2:4] = (below[2:4].astype(F32) + down[...].astype(F32)).astype(BF)


def phase_kernel(m0, u0, d0, m1, u1, d1, *outs):
    for k, (m, u, d) in enumerate(((m0, u0, d0), (m1, u1, d1))):
        total = m[...].astype(F32) + u[...].astype(F32) + d[...].astype(F32)
        for i in range(4):
            outs[4 * k + i][...] = total[i].astype(BF)


def served_kernel(cap, a0, a1, a2, a3, b0, b1, b2, b3, o0, o1, o2, o3):
    half = a0.shape[1]
    rows = a0.shape[0]
    padded = o0.shape[0]
    r = lax.broadcasted_iota(jnp.int32, (padded, rows), 0)
    c = lax.broadcasted_iota(jnp.int32, (padded, rows), 1)
    for k, parts in enumerate(((a0, a1, a2, a3), (b0, b1, b2, b3))):
        total = sum(p[...].astype(F32) for p in parts).astype(BF)
        for i, o in enumerate((o0, o1, o2, o3)):
            pick = ((c == r + i * cap) & (r < cap)).astype(F32).astype(BF)
            o[:, k * half : (k + 1) * half] = mm(pick, total).astype(BF)


def home_kernel(me_ref, routes_ref, res, mixed, gain, router, late, hidden_ref, hi_ref, lo_ref):
    x = res[...].astype(F32) + mixed[...].astype(F32)
    hidden_ref[...] = x
    normed = (x * lax.rsqrt(jnp.mean(x * x, -1, keepdims=True) + 1e-06) * gain[...]).astype(BF)
    logits = mm(normed, router[...])
    rows, experts = logits.shape
    labels = lax.broadcasted_iota(jnp.int32, (rows, experts), 1)
    one, two = routes_ref[:, 0:1], routes_ref[:, 1:2]
    first = jnp.sum(jnp.where(one == labels, logits, 0.0), -1, keepdims=True)
    second = jnp.sum(jnp.where(two == labels, logits, 0.0), -1, keepdims=True)
    gate0 = 1.0 / (1.0 + jnp.exp(second - first))
    gate1 = 1.0 / (1.0 + jnp.exp(first - second))
    cols = hi_ref.shape[1]
    place = lax.broadcasted_iota(jnp.int32, (rows, cols), 1)
    a = lax.broadcasted_iota(jnp.int32, (rows, rows), 0)
    b = lax.broadcasted_iota(jnp.int32, (rows, rows), 1)
    before = (b < a).astype(F32).astype(BF)
    total = jnp.zeros((rows, cols), F32)
    for j, off in enumerate((0, 1, 3, 2)):
        expert_id = lax.rem(me_ref[0] + off, 4)
        hit0, hit1 = (one == expert_id).astype(F32), (two == expert_id).astype(F32)
        chosen = hit0 + hit1
        rank = mm(before, jnp.broadcast_to(chosen, (rows, 128)).astype(BF))[:, 0:1].astype(jnp.int32)
        total = total + jnp.where(place == rank + 16 * j, hit0 * gate0 + hit1 * gate1, 0.0)
    hi, lo = split(total)
    hi_ref[...] = hi
    lo_ref[...] = lo


def final_kernel(hidden, hi, lo, b0, b1, b2, b3, out, back):
    for i, b in enumerate((b0, b1, b2, b3)):
        back[16 * i : 16 * i + 16, :] = b[...]
    moe = mm(hi[...], back[...]) + mm(lo[...], back[...])
    out[...] = (hidden[...] + moe).astype(BF)


def up_one(x, axis):
    return lax.ppermute(x, axis, ring(4, 1))


def down_one(x, axis):
    return lax.ppermute(x, axis, ring(4, -1))


def across(x, axis):
    return lax.ppermute(x, axis, ring(4, 2))


def far_sides(below, above, axis):
    return up_one(below[:2], axis), down_one(above[2:], axis)


def shards(
    queries,
    keys,
    payload_vectors,
    log_decay,
    attn_gain,
    out_weight,
    residual,
    norm_gain,
    router_weight,
    picks,
    gate_weight,
    up_weight,
    down_weight,
):
    seqs, positions, width = queries.shape
    slice_len, model = residual.shape[1], residual.shape[2]
    shares = positions // slice_len
    rows = seqs * slice_len
    cap = 3 * rows // 32
    half = model // 2
    me = lax.axis_index("x").astype(jnp.int32).reshape(1)

    weight_out = lax.all_gather(out_weight.T, SEQ, axis=0, tiled=True)
    gate, up, down = [
        lax.all_gather(w[0], "core", axis=0, tiled=True)
        for w in (gate_weight, up_weight, down_weight)
    ]
    routes = picks.reshape(rows, 2)
    turned = routes.T
    all_routes = jnp.concatenate(
        [turned] + [lax.ppermute(turned, "x", ring(4, -delta)) for delta in (1, 2, 3)], axis=1
    )

    inner, states, cum = local_part(queries, keys, payload_vectors, log_decay)
    arrived = lax.all_to_all(states, SEQ, 0, 0, tiled=True)
    prefix = lax.all_to_all(scan_states(arrived), SEQ, 0, 0, tiled=True)
    prefix = prefix.reshape(seqs * width // HEAD, HEAD, HEAD)
    normed = carried(
        queries, inner, cum, prefix, attn_gain.reshape(1, width), shares
    ).reshape(shares * rows, width)

    place, own_place = route(me, all_routes, cap)
    flat = residual.reshape(rows, model)
    gain = norm_gain.reshape(1, model)
    to_up, to_down, to_far, here = selected(place, own_place, normed, weight_out, flat)
    whole = whole_projection(normed, weight_out)

    size = here.shape[0]
    a0, b0, whole = call(
        norm_kernel,
        "selected_norm",
        [((size, half), BF)] * 2 + [(whole.shape, BF)],
        here,
        up_one(to_up, "x"),
        down_one(to_down, "x"),
        across(to_far, "x"),
        gain,
        whole,
        in_specs=[VM] * 5 + [ANY],
        out_specs=[VM] * 2 + [ANY],
        input_output_aliases={5: 2},
    )
    mixed = lax.psum_scatter(whole, "x", scatter_dimension=0, tiled=True)

    a4, b4, gate, up, down = call(
        stack_kernel,
        "stack",
        [((4, size, half), BF)] * 2 + [(w.shape, BF) for w in (gate, up, down)],
        a0,
        up_one(a0, "y"),
        down_one(a0, "y"),
        across(a0, "y"),
        b0,
        up_one(b0, "z"),
        down_one(b0, "z"),
        across(b0, "z"),
        gate,
        up,
        down,
        in_specs=[VM] * 8 + [ANY] * 3,
        out_specs=[VM] * 2 + [ANY] * 3,
        input_output_aliases={8: 2, 9: 3, 10: 4},
    )
    a_below, a_above = up_one(a4, "z"), down_one(a4, "z")
    b_below, b_above = up_one(b4, "y"), down_one(b4, "y")
    a_far, b_far = far_sides(a_below, a_above, "z"), far_sides(b_below, b_above, "y")

    oa, ob = expert(
        (a4, a_below, a_above, *a_far), (b4, b_below, b_above, *b_far), gate, up, down
    )
    a_below, a_above, b_below, b_above = call(
        fold_kernel,
        "fold",
        [((4, size, half), BF)] * 4,
        oa[1],
        oa[2],
        up_one(oa[3], "z"),
        down_one(oa[4], "z"),
        ob[1],
        ob[2],
        up_one(ob[3], "y"),
        down_one(ob[4], "y"),
        in_specs=[VM] * 8,
        out_specs=[VM] * 4,
    )
    parts = call(
        phase_kernel,
        "phase",
        [((size, half), BF)] * 8,
        oa[0],
        up_one(a_above, "z"),
        down_one(a_below, "z"),
        ob[0],
        up_one(b_above, "y"),
        down_one(b_below, "y"),
        in_specs=[VM] * 6,
        out_specs=[VM] * 8,
    )
    s0, s1, s2, s3 = call(
        functools.partial(served_kernel, cap),
        "served",
        [((16, model), BF)] * 4,
        parts[0],
        up_one(parts[2], "y"),
        down_one(parts[1], "y"),
        across(parts[3], "y"),
        parts[4],
        up_one(parts[6], "z"),
        down_one(parts[5], "z"),
        across(parts[7], "z"),
        in_specs=[VM] * 8,
        out_specs=[VM] * 4,
    )

    hidden, hi, lo = call(
        home_kernel,
        "home",
        [((rows, model), F32), ((rows, 64), BF), ((rows, 64), BF)],
        me,
        routes,
        flat,
        mixed,
        gain,
        router_weight,
        parts[0],
        in_specs=[SM] + [VM] * 5 + [ANY],
        out_specs=[VM] * 3,
        vmem=56,
    )
    out = call(
        final_kernel,
        "combine",
        [((rows, model), BF)],
        hidden,
        hi,
        lo,
        s0,
        down_one(s1, "x"),
        up_one(s2, "x"),
        across(s3, "x"),
        in_specs=[VM] * 7,
        out_specs=[VM],
        scratch_shapes=[pltpu.VMEM((64, model), BF)],
    )[0]
    return out.reshape(seqs, slice_len, model)


def solution(mesh):
    shape = dict(mesh.shape)
    grid = Mesh(mesh.devices.reshape(4, shape["seq"] // 8, 2, shape["exp"]), SEQ + ("x",))
    everyone = SEQ + ("x",)
    placed = (
        P(None, SEQ, "x"),
        P(None, SEQ, "x"),
        P(None, SEQ, "x"),
        P(None, SEQ, "x"),
        P("x"),
        P("x", SEQ),
        P(None, everyone, None),
        P(),
        P(),
        P(None, everyone, None),
        P("x", SEQ, None),
        P("x", SEQ, None),
        P("x", SEQ, None),
    )
    return jax.shard_map(
        shards, mesh=grid, in_specs=placed, out_specs=P(None, everyone, None), check_vma=False
    )
```

```python
import functools

import jax
import jax.numpy as jnp
from jax import lax
from jax.experimental import pallas as pl
from jax.experimental.pallas import tpu as pltpu
from jax.sharding import Mesh, PartitionSpec as P

HEAD = 128
BF = jnp.bfloat16
F32 = jnp.float32
HI = lax.Precision.HIGHEST
SEQ = ("z", "y", "core")
DEC = 16
OFFS = (1, 3, 2, 0)
JREL = {0: 0, 3: 1, 1: 2, 2: 3}


VM = pl.BlockSpec(memory_space=pltpu.VMEM)
SM = pl.BlockSpec(memory_space=pltpu.SMEM)
ANY = pl.BlockSpec(memory_space=pl.ANY)
HBM = pl.BlockSpec(memory_space=pltpu.HBM)


def ring(n, k):
    return [(i, (i + k) % n) for i in range(n)]


def mm(a, b):
    return jnp.dot(a, b, preferred_element_type=F32)


def mm0(a, b):
    return lax.dot_general(a, b, (((0,), (0,)), ((), ())), preferred_element_type=F32)


def split(a):
    hi = a.astype(BF)
    return hi, (a - hi.astype(F32)).astype(BF)


def local_kernel(q_ref, k_ref, v_ref, d_ref, inner_ref, state_ref, cum_ref):
    heads, steps = d_ref.shape[1], d_ref.shape[2]
    row = lax.broadcasted_iota(jnp.int32, (steps, steps), 0)
    col = lax.broadcasted_iota(jnp.int32, (steps, steps), 1)
    later = row >= col
    upto = (row <= col).astype(F32)
    turned = jnp.dot(d_ref[0], upto, precision=HI, preferred_element_type=F32)
    cum = turned.T
    cum_ref[0] = cum
    final = cum[steps - 1 : steps, :]
    tail = jnp.exp(final - cum)
    ends = jnp.exp(final)
    piece = lax.broadcasted_iota(jnp.int32, (DEC, HEAD), 0)
    half = HEAD // 2
    for h in range(heads):
        sl = slice(h * HEAD, (h + 1) * HEAD)
        q, k, v = q_ref[0, :, sl], k_ref[0, :, sl], v_ref[0, :, sl]
        scores = lax.dot_general(q, k, (((1,), (1,)), ((), ())), preferred_element_type=F32)
        spread = cum[:, h : h + 1] - turned[h : h + 1, :]
        weights = jnp.where(later, jnp.exp(jnp.minimum(spread, 0.0)), 0.0) * scores
        whi, wlo = split(weights)
        inner_ref[0, :, sl] = mm(whi, v) + mm(wlo, v)
        khi, klo = split(k.astype(F32) * tail[:, h : h + 1])
        update = (mm0(khi, v) + mm0(klo, v)).astype(BF)
        end = jnp.broadcast_to(ends[:, h : h + 1], (DEC, HEAD))
        e1 = end.astype(BF).astype(F32)
        e2 = (end - e1).astype(BF).astype(F32)
        e3 = end - e1 - e2
        rows = jnp.where(piece == 0, e1, jnp.where(piece == 1, e2, jnp.where(piece == 2, e3, 0.0)))
        for r in range(2):
            state_ref[2 * h + r, :half, :] = update[r * half : (r + 1) * half]
            state_ref[2 * h + r, half:, :] = rows.astype(BF)


def local_part(q, k, v, d):
    seqs, steps, width = q.shape
    heads = width // HEAD
    half = HEAD // 2
    block = pl.BlockSpec((1, steps, width), lambda s: (s, 0, 0))
    thin = pl.BlockSpec((1, steps, heads), lambda s: (s, 0, 0))
    return pl.pallas_call(
        local_kernel,
        grid=(seqs,),
        in_specs=[block, block, block, pl.BlockSpec((1, heads, steps), lambda s: (s, 0, 0))],
        out_specs=[block, pl.BlockSpec((2 * heads, half + DEC, HEAD), lambda s: (s, 0, 0)), thin],
        out_shape=[
            jax.ShapeDtypeStruct((seqs, steps, width), F32),
            jax.ShapeDtypeStruct((seqs * heads * 2, half + DEC, HEAD), BF),
            jax.ShapeDtypeStruct((seqs, steps, heads), F32),
        ],
        compiler_params=pltpu.CompilerParams(vmem_limit_bytes=32 * 2**20),
        name="local_attention",
    )(q, k, v, d)


def scan_kernel(in_ref, out_ref):
    blocks = in_ref.shape[0]
    half = out_ref.shape[1]
    carry = jnp.zeros(out_ref.shape[1:], F32)
    for n in range(blocks):
        out_ref[n] = carry.astype(BF)
        dec = in_ref[n, half:, :].astype(F32)
        carry = carry * (dec[0:1] + dec[1:2] + dec[2:3]) + in_ref[n, :half, :].astype(F32)


def scan_states(arrived):
    blocks, rows, width = arrived.shape
    return pl.pallas_call(
        scan_kernel,
        out_shape=jax.ShapeDtypeStruct((blocks, rows - DEC, width), BF),
        compiler_params=pltpu.CompilerParams(vmem_limit_bytes=32 * 2**20),
        name="state_prefix",
    )(arrived)


def carry_kernel(q_ref, inner_ref, cum_ref, state_ref, gain_ref, h0, h1, h2, out_ref, *same):
    shares, slice_len = out_ref.shape[0], out_ref.shape[2]
    heads = cum_ref.shape[2]
    grow = jnp.exp(cum_ref[0])
    for h in range(heads):
        sl = slice(h * HEAD, (h + 1) * HEAD)
        head = inner_ref[0, :, sl] + mm(q_ref[0, :, sl], state_ref[h]) * grow[:, h : h + 1]
        scale = lax.rsqrt(jnp.mean(head * head, -1, keepdims=True) + 1e-06)
        normed = (head * scale * gain_ref[:, sl]).astype(BF)
        for a in range(shares):
            out_ref[a, 0, :, sl] = normed[
                a * slice_len : (a + 1) * slice_len
            ]


def carried(q, inner, cum, state, gain, shares, held):
    seqs, steps, width = q.shape
    heads = width // HEAD
    block = pl.BlockSpec((1, steps, width), lambda s: (s, 0, 0))
    return pl.pallas_call(
        carry_kernel,
        grid=(seqs,),
        in_specs=[
            block,
            block,
            pl.BlockSpec((1, steps, heads), lambda s: (s, 0, 0)),
            pl.BlockSpec((heads, HEAD, HEAD), lambda s: (s, 0, 0)),
            pl.BlockSpec((1, width), lambda s: (0, 0)),
        ]
        + [ANY] * 3,
        out_specs=[pl.BlockSpec((shares, 1, steps // shares, width), lambda s: (0, s, 0, 0))]
        + [ANY] * 3,
        out_shape=[jax.ShapeDtypeStruct((shares, seqs, steps // shares, width), BF)]
        + [jax.ShapeDtypeStruct(h.shape, BF) for h in held],
        input_output_aliases={5: 1, 6: 2, 7: 3},
        compiler_params=pltpu.CompilerParams(vmem_limit_bytes=32 * 2**20),
        name="carried_norm",
    )(q, inner, cum, state, gain, *held)


def route_kernel(cap, me_ref, routes_ref, place_ref, own_ref):
    flight, rows = routes_ref.shape[1] // 128, 128
    total = routes_ref.shape[1]
    me = me_ref[0]
    a = lax.broadcasted_iota(jnp.int32, (total, total), 0)
    b = lax.broadcasted_iota(jnp.int32, (total, total), 1)
    before = ((a < b) & (a // rows == b // rows)).astype(BF)
    first, second = routes_ref[0:1, :], routes_ref[1:2, :]
    home = lax.broadcasted_iota(jnp.int32, (1, total), 1) // rows
    slots = lax.broadcasted_iota(jnp.int32, (flight * cap, total), 0)
    for r, off in enumerate(OFFS):
        expert = lax.rem(me + off, flight)
        chosen = ((first == expert) | (second == expert)).astype(F32)
        rank = mm(jnp.broadcast_to(chosen, (8, total)).astype(BF), before)[0:1].astype(jnp.int32)
        start = jnp.zeros((1, total), jnp.int32)
        for delta in range(flight):
            start = jnp.where(home == delta, cap * JREL[(delta - off) % 4], start)
        target = jnp.where(chosen > 0.0, start + rank, -1)
        hits = (slots == target).astype(F32).astype(BF)
        span = slice(r * flight * cap, (r + 1) * flight * cap)
        own_ref[span, :] = hits[:, :rows]
        for delta in range(flight):
            at = pl.multiple_of(lax.rem(me + delta, flight) * rows, rows)
            place_ref[span, pl.ds(at, rows)] = hits[:, delta * rows : (delta + 1) * rows]


def call(kernel, name, outs, *args, **kw):
    limit = kw.pop("vmem", 16)
    return pl.pallas_call(
        kernel,
        out_shape=[jax.ShapeDtypeStruct(s, d) for s, d in outs],
        compiler_params=pltpu.CompilerParams(vmem_limit_bytes=limit * 2**20),
        name=name,
        **kw,
    )(*args)


def route(me, routes, cap):
    total = routes.shape[1]
    flight = total // 128
    return call(
        functools.partial(route_kernel, cap),
        "route",
        [((flight * flight * cap, n), BF) for n in (total, 128)],
        me,
        routes,
        in_specs=[SM, VM],
        out_specs=[VM, VM],
    )


def nt(a, b):
    return lax.dot_general(a, b, (((1,), (1,)), ((), ())), preferred_element_type=F32)


def selected_kernel(place_ref, own_ref, normed_ref, weight_ref, res_ref, o0, o1, o2, o3, picked):

    @pl.when(pl.program_id(0) == 0)
    def _():
        picked[...] = mm(place_ref[...], normed_ref[...]).astype(BF)

    full = nt(picked[...], weight_ref[...]) + mm(own_ref[...], res_ref[...])
    full = full.astype(BF)
    size = o0.shape[0]
    for i, o in enumerate((o0, o1, o2, o3)):
        o[...] = full[i * size : (i + 1) * size]


def selected(place, own, normed, weight, res, tile=1024):
    picks, (model, width) = place.shape[0], weight.shape
    rows = res.shape[0]
    size = picks // 4
    whole = lambda a: pl.BlockSpec(a.shape, lambda n: (0, 0))
    return call(
        selected_kernel,
        "selected_projection",
        [((size, model), BF)] * 4,
        place,
        own,
        normed,
        weight,
        res,
        grid=(model // tile,),
        in_specs=[
            whole(place),
            whole(own),
            whole(normed),
            pl.BlockSpec((tile, width), lambda n: (n, 0)),
            pl.BlockSpec((rows, tile), lambda n: (0, n)),
        ],
        out_specs=[pl.BlockSpec((size, tile), lambda n: (0, n))] * 4,
        scratch_shapes=[pltpu.VMEM((picks, width), BF)],
        vmem=40,
    )


def whole_kernel(normed_ref, weight_ref, out_ref):
    out_ref[...] = nt(normed_ref[...], weight_ref[...]).astype(BF)


def whole_projection(normed, weight, tile=1024):
    total, (model, width) = normed.shape[0], weight.shape
    return call(
        whole_kernel,
        "whole_projection",
        [((total, model), BF)],
        normed,
        weight,
        grid=(model // tile,),
        in_specs=[
            pl.BlockSpec(normed.shape, lambda n: (0, 0)),
            pl.BlockSpec((tile, width), lambda n: (n, 0)),
        ],
        out_specs=[pl.BlockSpec((total, tile), lambda n: (0, n))],
        cost_estimate=pl.CostEstimate(
            flops=2 * total * model * width, bytes_accessed=4 * model * width, transcendentals=0
        ),
        vmem=24,
    )[0]


def norm_kernel(a, b, c, d, gain, held, w0, o0, o1, *same):
    x = a[...].astype(F32) + b[...].astype(F32) + c[...].astype(F32) + d[...].astype(F32)
    x = x * lax.rsqrt(jnp.mean(x * x, -1, keepdims=True) + 1e-06) * gain[...]
    half = o0.shape[1]
    o0[...] = x[:, :half].astype(BF)
    o1[...] = x[:, half:].astype(BF)


def stack_kernel(a0, a1, a2, a3, b0, b1, b2, b3, o0, o1):
    for i, (a, b) in enumerate(((a0, b0), (a1, b1), (a2, b2), (a3, b3))):
        o0[i] = a[...]
        o1[i] = b[...]


def pack_kernel(g0, g1, u0, u1, d0, d1, late, gu, down, sems):
    units = g0.shape[0]
    copies = []
    for i, part in enumerate((g0, g1, u0, u1)):
        copies.append((part, gu.at[pl.ds(i * units, units)]))
    for i, part in enumerate((d0, d1)):
        copies.append((part, down.at[pl.ds(i * units, units)]))
    copies = [pltpu.make_async_copy(a, b, sems.at[i]) for i, (a, b) in enumerate(copies)]
    for c in copies:
        c.start()
    for c in copies:
        c.wait()


def by_y(rows, y):
    return [((z * 4 + y) * rows, z) for z in range(4)]


def near_kernel(tile, a0, a1, a2, b0, b1, b2, gu, acc, x, part):
    rows, half = a0.shape[1], a0.shape[2]
    block = 4 * rows

    def fill(refs, at):
        for k, ref in enumerate(refs):
            for i in range(4):
                x[k * block + i * rows : k * block + (i + 1) * rows, :] = ref[i, :, at]

    acc[...] = jnp.zeros_like(acc)
    part[...] = jnp.zeros_like(part)

    @pl.loop(0, half // tile)
    def _(c):
        at = pl.ds(pl.multiple_of(c * tile, tile), tile)
        fill((a0, a1, a2), at)
        acc[0 : 3 * block, :] += nt(x[...], gu[:, at])

    @pl.loop(0, half // tile)
    def _(c):
        at = pl.ds(pl.multiple_of(c * tile, tile), tile)
        wide = pl.ds(pl.multiple_of(half + c * tile, tile), tile)
        fill((b0, b1, b2), at)
        part[...] += nt(x[...], gu[:, wide])

    for y in range(3):
        for row, z in by_y(rows, y):
            at = y * block + z * rows
            acc[row : row + rows, :] += part[at : at + rows, :]


def far_kernel(tile, acc, a3, a4, b3, b4, gu, down, hidden, oa3, oa4, ob3, ob4, x, part, own):
    rows, half = a3.shape[1], a3.shape[2]
    block = 4 * rows
    units = down.shape[0]

    def fill(refs, at):
        for k, ref in enumerate(refs):
            for i in range(2):
                x[(2 * k + i) * rows : (2 * k + i + 1) * rows, :] = ref[i, :, at]

    part[...] = jnp.zeros_like(part)

    @pl.loop(0, half // tile)
    def _(c):
        at = pl.ds(pl.multiple_of(c * tile, tile), tile)
        wide = pl.ds(pl.multiple_of(half + c * tile, tile), tile)
        fill((a3, a4), at)
        part[0:block, :] += nt(x[...], gu[:, at])
        fill((b3, b4), at)
        part[block : 2 * block, :] += nt(x[...], gu[:, wide])

    own[...] = acc[...]
    own[3 * block : 4 * block, :] += part[0:block, :]
    for row, z in by_y(rows, 3):
        own[row : row + rows, :] += part[block + z * rows : block + (z + 1) * rows, :]
    g = own[:, :units]
    hidden[...] = (g / (1.0 + jnp.exp(-g)) * own[:, units:]).astype(BF)
    by_z = hidden[3 * block : 4 * block, :]
    across_y = jnp.concatenate([hidden[row : row + rows, :] for row, _ in by_y(rows, 3)])

    @pl.loop(0, half // tile)
    def _(c):
        at = pl.ds(pl.multiple_of(c * tile, tile), tile)
        wide = pl.ds(pl.multiple_of(half + c * tile, tile), tile)
        for value, cols, outs in ((by_z, at, (oa3, oa4)), (across_y, wide, (ob3, ob4))):
            full = mm(value, down[:, cols]).astype(BF)
            for i in range(4):
                outs[i // 2][i % 2, :, at] = full[i * rows : (i + 1) * rows]


def rest_kernel(tile, hidden, down, oa0, oa1, oa2, ob0, ob1, ob2):
    rows, half = oa0.shape[1], oa0.shape[2]
    block = 4 * rows
    by_z = hidden[0 : 3 * block, :]
    across_y = jnp.concatenate(
        [hidden[row : row + rows, :] for y in range(3) for row, _ in by_y(rows, y)]
    )

    @pl.loop(0, half // tile)
    def _(c):
        at = pl.ds(pl.multiple_of(c * tile, tile), tile)
        wide = pl.ds(pl.multiple_of(half + c * tile, tile), tile)
        for value, cols, outs in ((by_z, at, (oa0, oa1, oa2)), (across_y, wide, (ob0, ob1, ob2))):
            full = mm(value, down[:, cols]).astype(BF)
            for k, out in enumerate(outs):
                for i in range(4):
                    out[i, :, at] = full[k * block + i * rows : k * block + (i + 1) * rows]


def cost(flops):
    return pl.CostEstimate(flops=flops, bytes_accessed=2**20, transcendentals=0)


def near(xs, gu, tile=1024):
    rows, half = xs[0].shape[1:]
    return call(
        functools.partial(near_kernel, tile),
        "near_rows",
        [((16 * rows, gu.shape[0]), F32)],
        *xs,
        gu,
        in_specs=[VM] * 7,
        out_specs=[VM],
        scratch_shapes=[
            pltpu.VMEM((12 * rows, tile), BF),
            pltpu.VMEM((12 * rows, gu.shape[0]), F32),
        ],
        cost_estimate=cost(2 * 12 * rows * gu.size),
        vmem=16,
    )[0]


def far(acc, xs, gu, down, tile=1024):
    rows, half = xs[0].shape[1:]
    return call(
        functools.partial(far_kernel, tile),
        "far_rows",
        [((16 * rows, down.shape[0]), BF)] + [((2, rows, half), BF)] * 4,
        acc,
        *xs,
        gu,
        down,
        in_specs=[VM] * 7,
        out_specs=[VM] * 5,
        scratch_shapes=[
            pltpu.VMEM((4 * rows, tile), BF),
            pltpu.VMEM((8 * rows, gu.shape[0]), F32),
            pltpu.VMEM(acc.shape, F32),
        ],
        vmem=20,
    )


def rest(hidden, down, rows, tile=1024):
    half = down.shape[1] // 2
    return call(
        functools.partial(rest_kernel, tile),
        "rest_rows",
        [((4, rows, half), BF)] * 6,
        hidden,
        down,
        in_specs=[VM] * 2,
        out_specs=[VM] * 6,
        cost_estimate=cost(2 * 12 * rows * down.size),
        vmem=16,
    )


def fold_kernel(bl0, ab0, up0, dn0, bl1, ab1, up1, dn1, ob0, oa0, ob1, oa1):
    for below, above, up, down, o_below, o_above in (
        (bl0, ab0, up0, dn0, ob0, oa0),
        (bl1, ab1, up1, dn1, ob1, oa1),
    ):
        o_above[0:2] = (above[0:2].astype(F32) + up[...].astype(F32)).astype(BF)
        o_above[2:4] = above[2:4]
        o_below[0:2] = below[0:2]
        o_below[2:4] = (below[2:4].astype(F32) + down[...].astype(F32)).astype(BF)


def phase_kernel(m0, u0, d0, m1, u1, d1, *outs):
    for k, (m, u, d) in enumerate(((m0, u0, d0), (m1, u1, d1))):
        total = m[...].astype(F32) + u[...].astype(F32) + d[...].astype(F32)
        for i in range(4):
            outs[4 * k + i][...] = total[i].astype(BF)


def served_kernel(cap, a0, a1, a2, a3, b0, b1, b2, b3, o0, o1, o2, o3):
    half = a0.shape[1]
    rows = a0.shape[0]
    padded = o0.shape[0]
    r = lax.broadcasted_iota(jnp.int32, (padded, rows), 0)
    c = lax.broadcasted_iota(jnp.int32, (padded, rows), 1)
    for k, parts in enumerate(((a0, a1, a2, a3), (b0, b1, b2, b3))):
        total = sum(p[...].astype(F32) for p in parts).astype(BF)
        for i, o in enumerate((o0, o1, o2, o3)):
            pick = ((c == r + i * cap) & (r < cap)).astype(F32).astype(BF)
            o[:, k * half : (k + 1) * half] = mm(pick, total).astype(BF)


def home_kernel(me_ref, routes_ref, res, mixed, gain, router, late, hidden_ref, coef_ref):
    x = res[...].astype(F32) + mixed[...].astype(F32)
    hidden_ref[...] = x
    normed = (x * lax.rsqrt(jnp.mean(x * x, -1, keepdims=True) + 1e-06) * gain[...]).astype(BF)
    logits = nt(normed, router[...])
    rows, experts = logits.shape
    labels = lax.broadcasted_iota(jnp.int32, (rows, experts), 1)
    one, two = routes_ref[:, 0:1], routes_ref[:, 1:2]
    first = jnp.sum(jnp.where(one == labels, logits, 0.0), -1, keepdims=True)
    second = jnp.sum(jnp.where(two == labels, logits, 0.0), -1, keepdims=True)
    gate0 = 1.0 / (1.0 + jnp.exp(second - first))
    gate1 = 1.0 / (1.0 + jnp.exp(first - second))
    cols = coef_ref.shape[1] // 2
    place = lax.broadcasted_iota(jnp.int32, (rows, cols), 1)
    a = lax.broadcasted_iota(jnp.int32, (rows, rows), 0)
    b = lax.broadcasted_iota(jnp.int32, (rows, rows), 1)
    before = (b < a).astype(F32).astype(BF)
    total = jnp.zeros((rows, cols), F32)
    for j, off in enumerate((0, 1, 3, 2)):
        expert_id = lax.rem(me_ref[0] + off, 4)
        hit0, hit1 = (one == expert_id).astype(F32), (two == expert_id).astype(F32)
        chosen = hit0 + hit1
        rank = mm(before, jnp.broadcast_to(chosen, (rows, 128)).astype(BF))[:, 0:1].astype(jnp.int32)
        total = total + jnp.where(place == rank + 16 * j, hit0 * gate0 + hit1 * gate1, 0.0)
    hi, lo = split(total)
    coef_ref[:, :cols] = hi
    coef_ref[:, cols:] = lo


def final_kernel(hidden, coef, b0, b1, b2, b3, out, back):
    for i, b in enumerate((b0, b1, b2, b3) * 2):
        back[16 * i : 16 * i + 16, :] = b[...]
    moe = mm(coef[...], back[...])
    out[...] = (hidden[...] + moe).astype(BF)


def up_one(x, axis):
    return lax.ppermute(x, axis, ring(4, 1))


def down_one(x, axis):
    return lax.ppermute(x, axis, ring(4, -1))


def across(x, axis):
    return lax.ppermute(x, axis, ring(4, 2))


def far_sides(below, above, axis):
    return up_one(below[:2], axis), down_one(above[2:], axis)


def shards(
    queries,
    keys,
    payload_vectors,
    log_decay,
    attn_gain,
    out_weight,
    residual,
    norm_gain,
    router_weight,
    picks,
    gate_weight,
    up_weight,
    down_weight,
):
    seqs, positions, width = queries.shape
    slice_len, model = residual.shape[1], residual.shape[2]
    shares = positions // slice_len
    rows = seqs * slice_len
    cap = 3 * rows // 32
    half = model // 2
    me = lax.axis_index("x").astype(jnp.int32).reshape(1)

    weight_out = lax.all_gather(out_weight.T, SEQ, axis=0, tiled=True)
    units = gate_weight.shape[1]
    weights = (gate_weight[0], up_weight[0], down_weight[0])
    swapped = [lax.ppermute(w, "core", ring(2, 1)) for w in weights]
    routes = picks.reshape(rows, 2)
    turned = routes.T
    all_routes = jnp.concatenate(
        [turned] + [lax.ppermute(turned, "x", ring(4, -delta)) for delta in (1, 2, 3)], axis=1
    )

    inner, states, cum = local_part(
        queries, keys, payload_vectors, log_decay.transpose(0, 2, 1)
    )
    arrived = lax.all_to_all(states, SEQ, 0, 0, tiled=True)
    prefix = lax.all_to_all(scan_states(arrived), SEQ, 0, 0, tiled=True)
    prefix = prefix.reshape(seqs * width // HEAD, HEAD, HEAD)
    normed, *swapped = carried(
        queries, inner, cum, prefix, attn_gain.reshape(1, width), shares, swapped
    )
    normed = normed.reshape(shares * rows, width)

    place, own_place = route(me, all_routes, cap)
    flat = residual.reshape(rows, model)
    gain = norm_gain.reshape(1, model)
    to_up, to_down, to_far, here = selected(place, own_place, normed, weight_out, flat)
    whole = whole_projection(normed, weight_out)

    size = here.shape[0]
    gu, down = call(
        pack_kernel,
        "pack",
        [((4 * units, model), BF), ((2 * units, model), BF)],
        *[w for pair in zip(weights, swapped) for w in pair],
        here,
        in_specs=[ANY] * 6 + [VM],
        out_specs=[VM, HBM],
        scratch_shapes=[pltpu.SemaphoreType.DMA((6,))],
        vmem=8,
    )
    a0, b0, whole, gu = call(
        norm_kernel,
        "selected_norm",
        [((size, half), BF)] * 2 + [(w.shape, BF) for w in (whole, gu)],
        here,
        up_one(to_up, "x"),
        down_one(to_down, "x"),
        across(to_far, "x"),
        gain,
        whole,
        gu,
        in_specs=[VM] * 5 + [HBM, VM],
        out_specs=[VM] * 2 + [HBM, VM],
        input_output_aliases={5: 2, 6: 3},
        vmem=16,
    )
    mixed = lax.psum_scatter(whole, "x", scatter_dimension=0, tiled=True)

    a4, b4 = call(
        stack_kernel,
        "stack",
        [((4, size, half), BF)] * 2,
        a0,
        up_one(a0, "y"),
        down_one(a0, "y"),
        across(a0, "y"),
        b0,
        up_one(b0, "z"),
        down_one(b0, "z"),
        across(b0, "z"),
        in_specs=[VM] * 8,
        out_specs=[VM] * 2,
        vmem=8,
    )
    a_below, a_above = up_one(a4, "z"), down_one(a4, "z")
    b_below, b_above = up_one(b4, "y"), down_one(b4, "y")
    a_far, b_far = far_sides(a_below, a_above, "z"), far_sides(b_below, b_above, "y")

    acc = near((a4, a_below, a_above, b4, b_below, b_above), gu)
    hidden, *ends = far(acc, (*a_far, *b_far), gu, down)
    body = rest(hidden, down, size)
    oa, ob = (*body[:3], *ends[:2]), (*body[3:], *ends[2:])
    a_below, a_above, b_below, b_above = call(
        fold_kernel,
        "fold",
        [((4, size, half), BF)] * 4,
        oa[1],
        oa[2],
        up_one(oa[3], "z"),
        down_one(oa[4], "z"),
        ob[1],
        ob[2],
        up_one(ob[3], "y"),
        down_one(ob[4], "y"),
        in_specs=[VM] * 8,
        out_specs=[VM] * 4,
        vmem=16,
    )
    parts = call(
        phase_kernel,
        "phase",
        [((size, half), BF)] * 8,
        oa[0],
        up_one(a_above, "z"),
        down_one(a_below, "z"),
        ob[0],
        up_one(b_above, "y"),
        down_one(b_below, "y"),
        in_specs=[VM] * 6,
        out_specs=[VM] * 8,
        vmem=16,
    )
    s0, s1, s2, s3 = call(
        functools.partial(served_kernel, cap),
        "served",
        [((16, model), BF)] * 4,
        parts[0],
        up_one(parts[2], "y"),
        down_one(parts[1], "y"),
        across(parts[3], "y"),
        parts[4],
        up_one(parts[6], "z"),
        down_one(parts[5], "z"),
        across(parts[7], "z"),
        in_specs=[VM] * 8,
        out_specs=[VM] * 4,
    )

    hidden, coef = call(
        home_kernel,
        "home",
        [((rows, model), F32), ((rows, 128), BF)],
        me,
        routes,
        flat,
        mixed,
        gain,
        router_weight.T,
        a_below,
        in_specs=[SM] + [VM] * 6,
        out_specs=[VM] * 2,
        vmem=20,
    )
    out = call(
        final_kernel,
        "combine",
        [((rows, model), BF)],
        hidden,
        coef,
        s0,
        down_one(s1, "x"),
        up_one(s2, "x"),
        across(s3, "x"),
        in_specs=[VM] * 6,
        out_specs=[VM],
        scratch_shapes=[pltpu.VMEM((128, model), BF)],
        vmem=16,
    )[0]
    return out.reshape(seqs, slice_len, model)


def solution(mesh):
    shape = dict(mesh.shape)
    grid = Mesh(mesh.devices.reshape(4, shape["seq"] // 8, 2, shape["exp"]), SEQ + ("x",))
    everyone = SEQ + ("x",)
    placed = (
        P(None, SEQ, "x"),
        P(None, SEQ, "x"),
        P(None, SEQ, "x"),
        P(None, SEQ, "x"),
        P("x"),
        P("x", SEQ),
        P(None, everyone, None),
        P(),
        P(),
        P(None, everyone, None),
        P("x", SEQ, None),
        P("x", SEQ, None),
        P("x", SEQ, None),
    )
    return jax.shard_map(
        shards, mesh=grid, in_specs=placed, out_specs=P(None, everyone, None), check_vma=False
    )
```

```python
import functools

import jax
import jax.numpy as jnp
from jax import lax
from jax.experimental import pallas as pl
from jax.experimental.pallas import tpu as pltpu
from jax.sharding import Mesh, PartitionSpec as P

HEAD = 128
BF = jnp.bfloat16
F32 = jnp.float32
HI = lax.Precision.HIGHEST
SEQ = ("z", "y", "core")
DEC = 16
OFFS = (1, 3, 2, 0)
JREL = {0: 0, 3: 1, 1: 2, 2: 3}


VM = pl.BlockSpec(memory_space=pltpu.VMEM)
SM = pl.BlockSpec(memory_space=pltpu.SMEM)
ANY = pl.BlockSpec(memory_space=pl.ANY)
HBM = pl.BlockSpec(memory_space=pltpu.HBM)


def ring(n, k):
    return [(i, (i + k) % n) for i in range(n)]


def mm(a, b):
    return jnp.dot(a, b, preferred_element_type=F32)


def mm0(a, b):
    return lax.dot_general(a, b, (((0,), (0,)), ((), ())), preferred_element_type=F32)


def split(a):
    hi = a.astype(BF)
    return hi, (a - hi.astype(F32)).astype(BF)


def local_kernel(q_ref, k_ref, v_ref, d_ref, inner_ref, state_ref, cum_ref):
    heads, steps = d_ref.shape[1], d_ref.shape[2]
    row = lax.broadcasted_iota(jnp.int32, (steps, steps), 0)
    col = lax.broadcasted_iota(jnp.int32, (steps, steps), 1)
    later = row >= col
    upto = (row <= col).astype(F32)
    turned = jnp.dot(d_ref[0], upto, precision=HI, preferred_element_type=F32)
    cum = turned.T
    cum_ref[0] = cum
    final = cum[steps - 1 : steps, :]
    tail = jnp.exp(final - cum)
    ends = jnp.exp(final)
    piece = lax.broadcasted_iota(jnp.int32, (DEC, HEAD), 0)
    half = HEAD // 2
    for h in range(heads):
        sl = slice(h * HEAD, (h + 1) * HEAD)
        q, k, v = q_ref[0, :, sl], k_ref[0, :, sl], v_ref[0, :, sl]
        scores = lax.dot_general(q, k, (((1,), (1,)), ((), ())), preferred_element_type=F32)
        spread = cum[:, h : h + 1] - turned[h : h + 1, :]
        weights = jnp.where(later, jnp.exp(jnp.minimum(spread, 0.0)), 0.0) * scores
        whi, wlo = split(weights)
        inner_ref[0, :, sl] = mm(whi, v) + mm(wlo, v)
        khi, klo = split(k.astype(F32) * tail[:, h : h + 1])
        update = (mm0(khi, v) + mm0(klo, v)).astype(BF)
        end = jnp.broadcast_to(ends[:, h : h + 1], (DEC, HEAD))
        e1 = end.astype(BF).astype(F32)
        e2 = (end - e1).astype(BF).astype(F32)
        e3 = end - e1 - e2
        rows = jnp.where(piece == 0, e1, jnp.where(piece == 1, e2, jnp.where(piece == 2, e3, 0.0)))
        for r in range(2):
            state_ref[2 * h + r, :half, :] = update[r * half : (r + 1) * half]
            state_ref[2 * h + r, half:, :] = rows.astype(BF)


def local_part(q, k, v, d):
    seqs, steps, width = q.shape
    heads = width // HEAD
    half = HEAD // 2
    block = pl.BlockSpec((1, steps, width), lambda s: (s, 0, 0))
    thin = pl.BlockSpec((1, steps, heads), lambda s: (s, 0, 0))
    return pl.pallas_call(
        local_kernel,
        grid=(seqs,),
        in_specs=[block, block, block, pl.BlockSpec((1, heads, steps), lambda s: (s, 0, 0))],
        out_specs=[block, pl.BlockSpec((2 * heads, half + DEC, HEAD), lambda s: (s, 0, 0)), thin],
        out_shape=[
            jax.ShapeDtypeStruct((seqs, steps, width), F32),
            jax.ShapeDtypeStruct((seqs * heads * 2, half + DEC, HEAD), BF),
            jax.ShapeDtypeStruct((seqs, steps, heads), F32),
        ],
        compiler_params=pltpu.CompilerParams(vmem_limit_bytes=60 * 2**20),
        name="local_attention",
    )(q, k, v, d)


def scan_kernel(in_ref, out_ref):
    blocks = in_ref.shape[0]
    half = out_ref.shape[1]
    carry = jnp.zeros(out_ref.shape[1:], F32)
    for n in range(blocks):
        out_ref[n] = carry.astype(BF)
        dec = in_ref[n, half:, :].astype(F32)
        carry = carry * (dec[0:1] + dec[1:2] + dec[2:3]) + in_ref[n, :half, :].astype(F32)


def scan_states(arrived):
    blocks, rows, width = arrived.shape
    return pl.pallas_call(
        scan_kernel,
        out_shape=jax.ShapeDtypeStruct((blocks, rows - DEC, width), BF),
        compiler_params=pltpu.CompilerParams(vmem_limit_bytes=32 * 2**20),
        name="state_prefix",
    )(arrived)


def carry_kernel(q_ref, inner_ref, cum_ref, state_ref, gain_ref, out_ref):
    shares, slice_len = out_ref.shape[0], out_ref.shape[2]
    heads = cum_ref.shape[2]
    grow = jnp.exp(cum_ref[0])
    for h in range(heads):
        sl = slice(h * HEAD, (h + 1) * HEAD)
        head = inner_ref[0, :, sl] + mm(q_ref[0, :, sl], state_ref[h]) * grow[:, h : h + 1]
        scale = lax.rsqrt(jnp.mean(head * head, -1, keepdims=True) + 1e-06)
        normed = (head * scale * gain_ref[:, sl]).astype(BF)
        for a in range(shares):
            out_ref[a, 0, :, sl] = normed[
                a * slice_len : (a + 1) * slice_len
            ]


def carried(q, inner, cum, state, gain, shares):
    seqs, steps, width = q.shape
    heads = width // HEAD
    block = pl.BlockSpec((1, steps, width), lambda s: (s, 0, 0))
    return pl.pallas_call(
        carry_kernel,
        grid=(seqs,),
        in_specs=[
            block,
            block,
            pl.BlockSpec((1, steps, heads), lambda s: (s, 0, 0)),
            pl.BlockSpec((heads, HEAD, HEAD), lambda s: (s, 0, 0)),
            pl.BlockSpec((1, width), lambda s: (0, 0)),
        ],
        out_specs=pl.BlockSpec((shares, 1, steps // shares, width), lambda s: (0, s, 0, 0)),
        out_shape=jax.ShapeDtypeStruct((shares, seqs, steps // shares, width), BF),
        compiler_params=pltpu.CompilerParams(vmem_limit_bytes=32 * 2**20),
        name="carried_norm",
    )(q, inner, cum, state, gain)


def call(kernel, name, outs, *args, **kw):
    limit = kw.pop("vmem", 16)
    return pl.pallas_call(
        kernel,
        out_shape=[jax.ShapeDtypeStruct(s, d) for s, d in outs],
        compiler_params=pltpu.CompilerParams(vmem_limit_bytes=limit * 2**20),
        name=name,
        **kw,
    )(*args)


def route_kernel(cap, me_ref, r0, r1, r2, r3, place_ref, own_ref):
    homes = (r0, r1, r2, r3)
    flight, rows = len(homes), r0.shape[1]
    me = me_ref[0]
    a = lax.broadcasted_iota(jnp.int32, (rows, rows), 0)
    b = lax.broadcasted_iota(jnp.int32, (rows, rows), 1)
    before = (a < b).astype(F32).astype(BF)
    slots = lax.broadcasted_iota(jnp.int32, (flight * cap, rows), 0)
    for r, off in enumerate(OFFS):
        expert = lax.rem(me + off, flight)
        span = slice(r * flight * cap, (r + 1) * flight * cap)
        for delta, home in enumerate(homes):
            hit = (home[0:1, :] == expert) | (home[1:2, :] == expert)
            chosen = hit.astype(F32)
            rank = mm(jnp.broadcast_to(chosen, (8, rows)).astype(BF), before)[0:1]
            start = cap * JREL[(delta - off) % 4]
            target = jnp.where(chosen > 0.0, rank.astype(jnp.int32) + start, -1)
            hits = (slots == target).astype(F32).astype(BF)
            at = pl.multiple_of(lax.rem(me + delta, flight) * rows, rows)
            place_ref[span, pl.ds(at, rows)] = hits
            if delta == 0:
                own_ref[span, :] = hits


def route(me, routes, cap):
    flight, rows = len(routes), routes[0].shape[1]
    return call(
        functools.partial(route_kernel, cap),
        "route",
        [((flight * flight * cap, n), BF) for n in (flight * rows, rows)],
        me,
        *routes,
        in_specs=[SM] + [VM] * flight,
        out_specs=[VM, VM],
    )


def nt(a, b):
    return lax.dot_general(a, b, (((1,), (1,)), ((), ())), preferred_element_type=F32)


def selected_kernel(place_ref, own_ref, normed_ref, weight_ref, res_ref, o0, o1, o2, o3, picked):

    @pl.when(pl.program_id(0) == 0)
    def _():
        picked[...] = mm(place_ref[...], normed_ref[...]).astype(BF)

    full = nt(weight_ref[...], picked[...]).T + mm(own_ref[...], res_ref[...])
    full = full.astype(BF)
    size = o0.shape[0]
    for i, o in enumerate((o0, o1, o2, o3)):
        o[...] = full[i * size : (i + 1) * size]


def selected(place, own, normed, weight, res, tile=1024):
    picks, (model, width) = place.shape[0], weight.shape
    rows = res.shape[0]
    size = picks // 4
    whole = lambda a: pl.BlockSpec(a.shape, lambda n: (0, 0))
    return call(
        selected_kernel,
        "selected_projection",
        [((size, model), BF)] * 4,
        place,
        own,
        normed,
        weight,
        res,
        grid=(model // tile,),
        in_specs=[
            whole(place),
            whole(own),
            whole(normed),
            pl.BlockSpec((tile, width), lambda n: (n, 0)),
            pl.BlockSpec((rows, tile), lambda n: (0, n)),
        ],
        out_specs=[pl.BlockSpec((size, tile), lambda n: (0, n))] * 4,
        scratch_shapes=[pltpu.VMEM((picks, width), BF)],
        vmem=54,
    )


def whole_kernel(normed_ref, weight_ref, late, out_ref):
    out_ref[...] = nt(normed_ref[...], weight_ref[...]).astype(BF)


def whole_projection(normed, weight, late, tile=1024):
    total, (model, width) = normed.shape[0], weight.shape
    return call(
        whole_kernel,
        "whole_projection",
        [((total, model), BF)],
        normed,
        weight,
        late,
        grid=(model // tile,),
        in_specs=[
            pl.BlockSpec(normed.shape, lambda n: (0, 0)),
            pl.BlockSpec((tile, width), lambda n: (n, 0)),
            VM,
        ],
        out_specs=[pl.BlockSpec((total, tile), lambda n: (0, n))],
        cost_estimate=pl.CostEstimate(
            flops=2 * total * model * width, bytes_accessed=4 * model * width, transcendentals=0
        ),
        vmem=58,
    )[0]


def norm_kernel(a, b, c, d, gain, o0, o1, ready):
    ready[...] = jnp.zeros_like(ready)
    x = a[...].astype(F32) + b[...].astype(F32) + c[...].astype(F32) + d[...].astype(F32)
    x = x * lax.rsqrt(jnp.mean(x * x, -1, keepdims=True) + 1e-06) * gain[...]
    half = o0.shape[1]
    o0[...] = x[:, :half].astype(BF)
    o1[...] = x[:, half:].astype(BF)


def hold_kernel(held, late, same):
    pass


def stack_kernel(a0, a1, a2, a3, b0, b1, b2, b3, o0, o1):
    for i, (a, b) in enumerate(((a0, b0), (a1, b1), (a2, b2), (a3, b3))):
        o0[i] = a[...]
        o1[i] = b[...]


def by_y(rows, y):
    return [((z * 4 + y) * rows, z) for z in range(4)]


def fetch(parts, buf, sems, chunk, slot):
    units, tile = parts[0].shape[0], buf.shape[2]
    cols = pl.ds(pl.multiple_of(chunk * tile, tile), tile)
    return [
        pltpu.make_async_copy(
            part.at[:, cols], buf.at[slot, pl.ds(i * units, units)], sems.at[slot, i]
        )
        for i, part in enumerate(parts)
    ]


def streamed(parts, buf, sems, chunks, body):
    @pl.loop(0, chunks)
    def _(c):
        slot = lax.rem(c, 2)

        @pl.when(c + 1 < chunks)
        def _():
            for copy in fetch(parts, buf, sems, c + 1, 1 - slot):
                copy.start()

        for copy in fetch(parts, buf, sems, c, slot):
            copy.wait()
        body(c, buf[slot])


def first_chunk(parts, buf, sems):
    for copy in fetch(parts, buf, sems, 0, 0):
        copy.start()


def gate_up(refs_a, refs_b, parts, x, part, buf, sems):
    tile = buf.shape[2]
    rows, half = refs_a[0].shape[1:]
    each = half // tile
    part[...] = jnp.zeros_like(part)

    def body(c, weights):
        for k, refs in enumerate((refs_a, refs_b)):

            @pl.when(c // each == k)
            def _():
                at = pl.ds(pl.multiple_of((c - k * each) * tile, tile), tile)
                row = 0
                for ref in refs:
                    for i in range(ref.shape[0]):
                        x[row : row + rows, :] = ref[i, :, at]
                        row += rows

        part[c // each] += nt(x[...], weights)

    streamed(parts, buf, sems, 2 * each, body)


def down_product(value, parts, buf, sems, outs_a, outs_b):
    tile = buf.shape[2]
    rows, half = outs_a[0].shape[1:]
    each = half // tile

    def body(c, weights):
        full = mm(value[c // each], weights).astype(BF)
        for k, outs in enumerate((outs_a, outs_b)):

            @pl.when(c // each == k)
            def _():
                at = pl.ds(pl.multiple_of((c - k * each) * tile, tile), tile)
                row = 0
                for out in outs:
                    for i in range(out.shape[0]):
                        out[i, :, at] = full[row : row + rows]
                        row += rows

    streamed(parts, buf, sems, 2 * each, body)


def near_kernel(*refs):
    a, b, parts = refs[0:3], refs[3:6], refs[6:8]
    acc, x, part, buf, sems = refs[8:]
    rows = a[0].shape[1]
    block = 4 * rows
    first_chunk(parts, buf, sems)
    gate_up(a, b, parts, x, part, buf, sems)
    acc[0 : 3 * block, :] = part[0]
    acc[3 * block :, :] = jnp.zeros((block, acc.shape[1]), F32)
    for y in range(3):
        for row, z in by_y(rows, y):
            at = y * block + z * rows
            acc[row : row + rows, :] += part[1, at : at + rows, :]


def far_kernel(*refs):
    acc, a, b, parts, downs = refs[0], refs[1:3], refs[3:5], refs[5:7], refs[7:8]
    hidden, oa, ob = refs[8], refs[9:11], refs[11:13]
    x, part, own, value, buf, sems, dbuf, dsems = refs[13:]
    rows = a[0].shape[1]
    block = 4 * rows
    units = own.shape[1] // 2
    first_chunk(parts, buf, sems)
    first_chunk(downs, dbuf, dsems)
    gate_up(a, b, parts, x, part, buf, sems)
    own[...] = acc[...]
    own[3 * block :, :] += part[0]
    for row, z in by_y(rows, 3):
        own[row : row + rows, :] += part[1, z * rows : (z + 1) * rows, :]
    g = own[:, :units]
    hidden[...] = (g / (1.0 + jnp.exp(-g)) * own[:, units:]).astype(BF)
    value[0] = hidden[3 * block :, :]
    for row, z in by_y(rows, 3):
        value[1, z * rows : (z + 1) * rows, :] = hidden[row : row + rows, :]
    down_product(value, downs, dbuf, dsems, oa, ob)


def rest_kernel(*refs):
    hidden, downs, oa, ob = refs[0], refs[1:2], refs[2:5], refs[5:8]
    value, dbuf, dsems = refs[8:]
    rows = oa[0].shape[1]
    block = 4 * rows
    first_chunk(downs, dbuf, dsems)
    value[0] = hidden[: 3 * block, :]
    for y in range(3):
        for row, z in by_y(rows, y):
            at = y * block + z * rows
            value[1, at : at + rows, :] = hidden[row : row + rows, :]
    down_product(value, downs, dbuf, dsems, oa, ob)


def cost(flops):
    return pl.CostEstimate(flops=flops, bytes_accessed=2**20, transcendentals=0)


TILE = 1024


def streams(parts):
    units, count = parts[0].shape[0], len(parts)
    return [
        pltpu.VMEM((2, count * units, TILE), BF),
        pltpu.SemaphoreType.DMA((2, count)),
    ]


def near(xs, parts):
    rows = xs[0].shape[1]
    units = len(parts) * parts[0].shape[0]
    return call(
        near_kernel,
        "near_rows",
        [((16 * rows, units), F32)],
        *xs,
        *parts,
        in_specs=[VM] * 6 + [HBM] * len(parts),
        out_specs=[VM],
        scratch_shapes=[
            pltpu.VMEM((12 * rows, TILE), BF),
            pltpu.VMEM((2, 12 * rows, units), F32),
            *streams(parts),
        ],
        cost_estimate=cost(2 * 12 * rows * len(parts) * parts[0].size),
        vmem=46,
    )[0]


def far(acc, xs, parts, downs):
    rows, half = xs[0].shape[1:]
    units = len(downs) * downs[0].shape[0]
    return call(
        far_kernel,
        "far_rows",
        [((16 * rows, units), BF)] + [((2, rows, half), BF)] * 4,
        acc,
        *xs,
        *parts,
        *downs,
        in_specs=[VM] * 5 + [HBM] * (len(parts) + len(downs)),
        out_specs=[VM] * 5,
        scratch_shapes=[
            pltpu.VMEM((4 * rows, TILE), BF),
            pltpu.VMEM((2, 4 * rows, 2 * units), F32),
            pltpu.VMEM(acc.shape, F32),
            pltpu.VMEM((2, 4 * rows, units), BF),
            *streams(parts),
            *streams(downs),
        ],
        vmem=48,
    )


def rest(hidden, downs, rows):
    half = downs[0].shape[1] // 2
    return call(
        rest_kernel,
        "rest_rows",
        [((4, rows, half), BF)] * 6,
        hidden,
        *downs,
        in_specs=[VM] + [HBM] * len(downs),
        out_specs=[VM] * 6,
        scratch_shapes=[pltpu.VMEM((2, 12 * rows, hidden.shape[1]), BF), *streams(downs)],
        cost_estimate=cost(2 * 12 * rows * len(downs) * downs[0].size),
        vmem=46,
    )


def fold_kernel(bl0, ab0, up0, dn0, bl1, ab1, up1, dn1, ob0, oa0, ob1, oa1):
    for below, above, up, down, o_below, o_above in (
        (bl0, ab0, up0, dn0, ob0, oa0),
        (bl1, ab1, up1, dn1, ob1, oa1),
    ):
        o_above[0:2] = (above[0:2].astype(F32) + up[...].astype(F32)).astype(BF)
        o_above[2:4] = above[2:4]
        o_below[0:2] = below[0:2]
        o_below[2:4] = (below[2:4].astype(F32) + down[...].astype(F32)).astype(BF)


def phase_kernel(m0, u0, d0, m1, u1, d1, *outs):
    for k, (m, u, d) in enumerate(((m0, u0, d0), (m1, u1, d1))):
        total = m[...].astype(F32) + u[...].astype(F32) + d[...].astype(F32)
        for i in range(4):
            outs[4 * k + i][...] = total[i].astype(BF)


def served_kernel(cap, a0, a1, a2, a3, b0, b1, b2, b3, o0, o1, o2, o3):
    half = a0.shape[1]
    rows = a0.shape[0]
    padded = o0.shape[0]
    r = lax.broadcasted_iota(jnp.int32, (padded, rows), 0)
    c = lax.broadcasted_iota(jnp.int32, (padded, rows), 1)
    for k, parts in enumerate(((a0, a1, a2, a3), (b0, b1, b2, b3))):
        total = sum(p[...].astype(F32) for p in parts).astype(BF)
        for i, o in enumerate((o0, o1, o2, o3)):
            pick = ((c == r + i * cap) & (r < cap)).astype(F32).astype(BF)
            o[:, k * half : (k + 1) * half] = mm(pick, total).astype(BF)


def home_kernel(me_ref, routes_ref, res, mixed, gain, router, late, hidden_ref, coef_ref):
    x = res[...].astype(F32) + mixed[...].astype(F32)
    hidden_ref[...] = x
    normed = (x * lax.rsqrt(jnp.mean(x * x, -1, keepdims=True) + 1e-06) * gain[...]).astype(BF)
    logits = nt(normed, router[...])
    rows, experts = logits.shape
    labels = lax.broadcasted_iota(jnp.int32, (rows, experts), 1)
    one, two = routes_ref[:, 0:1], routes_ref[:, 1:2]
    first = jnp.sum(jnp.where(one == labels, logits, 0.0), -1, keepdims=True)
    second = jnp.sum(jnp.where(two == labels, logits, 0.0), -1, keepdims=True)
    gate0 = 1.0 / (1.0 + jnp.exp(second - first))
    gate1 = 1.0 / (1.0 + jnp.exp(first - second))
    cols = coef_ref.shape[1] // 2
    place = lax.broadcasted_iota(jnp.int32, (rows, cols), 1)
    a = lax.broadcasted_iota(jnp.int32, (rows, rows), 0)
    b = lax.broadcasted_iota(jnp.int32, (rows, rows), 1)
    before = (b < a).astype(F32).astype(BF)
    total = jnp.zeros((rows, cols), F32)
    for j, off in enumerate((0, 1, 3, 2)):
        expert_id = lax.rem(me_ref[0] + off, 4)
        hit0, hit1 = (one == expert_id).astype(F32), (two == expert_id).astype(F32)
        chosen = hit0 + hit1
        rank = mm(before, jnp.broadcast_to(chosen, (rows, 128)).astype(BF))[:, 0:1].astype(jnp.int32)
        total = total + jnp.where(place == rank + 16 * j, hit0 * gate0 + hit1 * gate1, 0.0)
    hi, lo = split(total)
    coef_ref[:, :cols] = hi
    coef_ref[:, cols:] = lo


def final_kernel(hidden, coef, b0, b1, b2, b3, out, back):
    for i, b in enumerate((b0, b1, b2, b3) * 2):
        back[16 * i : 16 * i + 16, :] = b[...]
    moe = mm(coef[...], back[...])
    out[...] = (hidden[...] + moe).astype(BF)


def up_one(x, axis):
    return lax.ppermute(x, axis, ring(4, 1))


def down_one(x, axis):
    return lax.ppermute(x, axis, ring(4, -1))


def across(x, axis):
    return lax.ppermute(x, axis, ring(4, 2))


def far_sides(below, above, axis):
    return up_one(below[:2], axis), down_one(above[2:], axis)


def shards(
    queries,
    keys,
    payload_vectors,
    log_decay,
    attn_gain,
    out_weight,
    residual,
    norm_gain,
    router_weight,
    picks,
    gate_weight,
    up_weight,
    down_weight,
):
    seqs, positions, width = queries.shape
    slice_len, model = residual.shape[1], residual.shape[2]
    shares = positions // slice_len
    rows = seqs * slice_len
    cap = 3 * rows // 32
    half = model // 2
    me = lax.axis_index("x").astype(jnp.int32).reshape(1)

    weight_out = lax.all_gather(out_weight.T, SEQ, axis=0, tiled=True)
    gate, up, down = [
        lax.all_gather(w[0], "core", axis=0, tiled=True)
        for w in (gate_weight, up_weight, down_weight)
    ]
    routes = picks.reshape(rows, 2)
    turned = routes.T
    all_routes = [turned] + [lax.ppermute(turned, "x", ring(4, -delta)) for delta in (1, 2, 3)]

    inner, states, cum = local_part(
        queries, keys, payload_vectors, log_decay.transpose(0, 2, 1)
    )
    arrived = lax.all_to_all(states, SEQ, 0, 0, tiled=True)
    prefix = lax.all_to_all(scan_states(arrived), SEQ, 0, 0, tiled=True)
    prefix = prefix.reshape(seqs * width // HEAD, HEAD, HEAD)
    normed = carried(
        queries, inner, cum, prefix, attn_gain.reshape(1, width), shares
    )
    normed = normed.reshape(shares * rows, width)

    place, own_place = route(me, all_routes, cap)
    flat = residual.reshape(rows, model)
    gain = norm_gain.reshape(1, model)
    to_up, to_down, to_far, here = selected(place, own_place, normed, weight_out, flat)
    whole = whole_projection(normed, weight_out, here)

    size = here.shape[0]
    a0, b0, ready = call(
        norm_kernel,
        "selected_norm",
        [((size, half), BF)] * 2 + [((8, 128), F32)],
        here,
        up_one(to_up, "x"),
        down_one(to_down, "x"),
        across(to_far, "x"),
        gain,
        in_specs=[VM] * 5,
        out_specs=[VM] * 3,
    )

    whole = call(
        hold_kernel,
        "hold",
        [(whole.shape, BF)],
        whole,
        ready,
        in_specs=[ANY, VM],
        out_specs=[ANY],
        input_output_aliases={0: 0},
        vmem=61,
    )[0]
    mixed = lax.psum_scatter(whole, "x", scatter_dimension=0, tiled=True)

    a4, b4 = call(
        stack_kernel,
        "stack",
        [((4, size, half), BF)] * 2,
        a0,
        up_one(a0, "y"),
        down_one(a0, "y"),
        across(a0, "y"),
        b0,
        up_one(b0, "z"),
        down_one(b0, "z"),
        across(b0, "z"),
        in_specs=[VM] * 8,
        out_specs=[VM] * 2,
        vmem=16,
    )
    a_below, a_above = up_one(a4, "z"), down_one(a4, "z")
    b_below, b_above = up_one(b4, "y"), down_one(b4, "y")
    a_far, b_far = far_sides(a_below, a_above, "z"), far_sides(b_below, b_above, "y")

    gate_up_parts, downs = (gate, up), (down,)
    acc = near((a4, a_below, a_above, b4, b_below, b_above), gate_up_parts)
    hidden, *ends = far(acc, (*a_far, *b_far), gate_up_parts, downs)
    body = rest(hidden, downs, size)
    oa, ob = (*body[:3], *ends[:2]), (*body[3:], *ends[2:])
    a_below, a_above, b_below, b_above = call(
        fold_kernel,
        "fold",
        [((4, size, half), BF)] * 4,
        oa[1],
        oa[2],
        up_one(oa[3], "z"),
        down_one(oa[4], "z"),
        ob[1],
        ob[2],
        up_one(ob[3], "y"),
        down_one(ob[4], "y"),
        in_specs=[VM] * 8,
        out_specs=[VM] * 4,
        vmem=16,
    )
    parts = call(
        phase_kernel,
        "phase",
        [((size, half), BF)] * 8,
        oa[0],
        up_one(a_above, "z"),
        down_one(a_below, "z"),
        ob[0],
        up_one(b_above, "y"),
        down_one(b_below, "y"),
        in_specs=[VM] * 6,
        out_specs=[VM] * 8,
        vmem=16,
    )
    s0, s1, s2, s3 = call(
        functools.partial(served_kernel, cap),
        "served",
        [((16, model), BF)] * 4,
        parts[0],
        up_one(parts[2], "y"),
        down_one(parts[1], "y"),
        across(parts[3], "y"),
        parts[4],
        up_one(parts[6], "z"),
        down_one(parts[5], "z"),
        across(parts[7], "z"),
        in_specs=[VM] * 8,
        out_specs=[VM] * 4,
    )

    hidden, coef = call(
        home_kernel,
        "home",
        [((rows, model), F32), ((rows, 128), BF)],
        me,
        routes,
        flat,
        mixed,
        gain,
        router_weight.T,
        a_below,
        in_specs=[SM] + [VM] * 6,
        out_specs=[VM] * 2,
        vmem=20,
    )
    out = call(
        final_kernel,
        "combine",
        [((rows, model), BF)],
        hidden,
        coef,
        s0,
        down_one(s1, "x"),
        up_one(s2, "x"),
        across(s3, "x"),
        in_specs=[VM] * 6,
        out_specs=[VM],
        scratch_shapes=[pltpu.VMEM((128, model), BF)],
        vmem=16,
    )[0]
    return out.reshape(seqs, slice_len, model)


def solution(mesh):
    shape = dict(mesh.shape)
    grid = Mesh(mesh.devices.reshape(4, shape["seq"] // 8, 2, shape["exp"]), SEQ + ("x",))
    everyone = SEQ + ("x",)
    placed = (
        P(None, SEQ, "x"),
        P(None, SEQ, "x"),
        P(None, SEQ, "x"),
        P(None, SEQ, "x"),
        P("x"),
        P("x", SEQ),
        P(None, everyone, None),
        P(),
        P(),
        P(None, everyone, None),
        P("x", SEQ, None),
        P("x", SEQ, None),
        P("x", SEQ, None),
    )
    return jax.shard_map(
        shards, mesh=grid, in_specs=placed, out_specs=P(None, everyone, None), check_vma=False
    )
```

```python
import functools

import jax
import jax.numpy as jnp
from jax import lax
from jax.experimental import pallas as pl
from jax.experimental.pallas import tpu as pltpu
from jax.sharding import Mesh, PartitionSpec as P

HEAD = 128
BF = jnp.bfloat16
F32 = jnp.float32
HI = lax.Precision.HIGHEST
SEQ = ("z", "y", "core")
TILE = 1024
DEC = 16
OFFS = (1, 3, 2, 0)
JREL = {0: 0, 3: 1, 1: 2, 2: 3}


VM = pl.BlockSpec(memory_space=pltpu.VMEM)
SM = pl.BlockSpec(memory_space=pltpu.SMEM)
ANY = pl.BlockSpec(memory_space=pl.ANY)
HBM = pl.BlockSpec(memory_space=pltpu.HBM)


def ring(n, k):
    return [(i, (i + k) % n) for i in range(n)]


def mm(a, b):
    return jnp.dot(a, b, preferred_element_type=F32)


def mm0(a, b):
    return lax.dot_general(a, b, (((0,), (0,)), ((), ())), preferred_element_type=F32)


def split(a):
    hi = a.astype(BF)
    return hi, (a - hi.astype(F32)).astype(BF)


def local_kernel(q_ref, k_ref, v_ref, d_ref, inner_ref, state_ref, cum_ref):
    heads, steps = d_ref.shape[1], d_ref.shape[2]
    row = lax.broadcasted_iota(jnp.int32, (steps, steps), 0)
    col = lax.broadcasted_iota(jnp.int32, (steps, steps), 1)
    later = row >= col
    upto = (row <= col).astype(F32)
    turned = jnp.dot(d_ref[0], upto, precision=HI, preferred_element_type=F32)
    cum = turned.T
    cum_ref[0] = cum
    final = cum[steps - 1 : steps, :]
    tail = jnp.exp(final - cum)
    ends = jnp.exp(final)
    piece = lax.broadcasted_iota(jnp.int32, (DEC, HEAD), 0)
    half = HEAD // 2
    for h in range(heads):
        sl = slice(h * HEAD, (h + 1) * HEAD)
        q, k, v = q_ref[0, :, sl], k_ref[0, :, sl], v_ref[0, :, sl]
        scores = lax.dot_general(q, k, (((1,), (1,)), ((), ())), preferred_element_type=F32)
        spread = cum[:, h : h + 1] - turned[h : h + 1, :]
        weights = jnp.where(later, jnp.exp(jnp.minimum(spread, 0.0)), 0.0) * scores
        whi, wlo = split(weights)
        inner_ref[0, :, sl] = mm(whi, v) + mm(wlo, v)
        khi, klo = split(k.astype(F32) * tail[:, h : h + 1])
        update = (mm0(khi, v) + mm0(klo, v)).astype(BF)
        end = jnp.broadcast_to(ends[:, h : h + 1], (DEC, HEAD))
        e1 = end.astype(BF).astype(F32)
        e2 = (end - e1).astype(BF).astype(F32)
        e3 = end - e1 - e2
        rows = jnp.where(piece == 0, e1, jnp.where(piece == 1, e2, jnp.where(piece == 2, e3, 0.0)))
        for r in range(2):
            state_ref[2 * h + r, :half, :] = update[r * half : (r + 1) * half]
            state_ref[2 * h + r, half:, :] = rows.astype(BF)


def local_part(q, k, v, d):
    seqs, steps, width = q.shape
    heads = width // HEAD
    half = HEAD // 2
    block = pl.BlockSpec((1, steps, width), lambda s: (s, 0, 0))
    thin = pl.BlockSpec((1, steps, heads), lambda s: (s, 0, 0))
    return pl.pallas_call(
        local_kernel,
        grid=(seqs,),
        in_specs=[block, block, block, pl.BlockSpec((1, heads, steps), lambda s: (s, 0, 0))],
        out_specs=[block, pl.BlockSpec((2 * heads, half + DEC, HEAD), lambda s: (s, 0, 0)), thin],
        out_shape=[
            jax.ShapeDtypeStruct((seqs, steps, width), F32),
            jax.ShapeDtypeStruct((seqs * heads * 2, half + DEC, HEAD), BF),
            jax.ShapeDtypeStruct((seqs, steps, heads), F32),
        ],
        compiler_params=pltpu.CompilerParams(vmem_limit_bytes=60 * 2**20),
        name="local_attention",
    )(q, k, v, d)


def scan_kernel(in_ref, out_ref):
    blocks = in_ref.shape[0]
    half = out_ref.shape[1]
    carry = jnp.zeros(out_ref.shape[1:], F32)
    for n in range(blocks):
        out_ref[n] = carry.astype(BF)
        dec = in_ref[n, half:, :].astype(F32)
        carry = carry * (dec[0:1] + dec[1:2] + dec[2:3]) + in_ref[n, :half, :].astype(F32)


def scan_states(arrived):
    blocks, rows, width = arrived.shape
    return pl.pallas_call(
        scan_kernel,
        out_shape=jax.ShapeDtypeStruct((blocks, rows - DEC, width), BF),
        compiler_params=pltpu.CompilerParams(vmem_limit_bytes=32 * 2**20),
        name="state_prefix",
    )(arrived)


def carry_kernel(q_ref, inner_ref, cum_ref, state_ref, gain_ref, out_ref):
    shares, slice_len = out_ref.shape[0], out_ref.shape[2]
    heads = cum_ref.shape[2]
    grow = jnp.exp(cum_ref[0])
    for h in range(heads):
        sl = slice(h * HEAD, (h + 1) * HEAD)
        head = inner_ref[0, :, sl] + mm(q_ref[0, :, sl], state_ref[h]) * grow[:, h : h + 1]
        scale = lax.rsqrt(jnp.mean(head * head, -1, keepdims=True) + 1e-06)
        normed = (head * scale * gain_ref[:, sl]).astype(BF)
        for a in range(shares):
            out_ref[a, 0, :, sl] = normed[
                a * slice_len : (a + 1) * slice_len
            ]


def carried(q, inner, cum, state, gain, shares):
    seqs, steps, width = q.shape
    heads = width // HEAD
    block = pl.BlockSpec((1, steps, width), lambda s: (s, 0, 0))
    return pl.pallas_call(
        carry_kernel,
        grid=(seqs,),
        in_specs=[
            block,
            block,
            pl.BlockSpec((1, steps, heads), lambda s: (s, 0, 0)),
            pl.BlockSpec((heads, HEAD, HEAD), lambda s: (s, 0, 0)),
            pl.BlockSpec((1, width), lambda s: (0, 0)),
        ],
        out_specs=pl.BlockSpec((shares, 1, steps // shares, width), lambda s: (0, s, 0, 0)),
        out_shape=jax.ShapeDtypeStruct((shares, seqs, steps // shares, width), BF),
        compiler_params=pltpu.CompilerParams(vmem_limit_bytes=32 * 2**20),
        name="carried_norm",
    )(q, inner, cum, state, gain)


def call(kernel, name, outs, *args, **kw):
    limit = kw.pop("vmem", 16)
    return pl.pallas_call(
        kernel,
        out_shape=[jax.ShapeDtypeStruct(s, d) for s, d in outs],
        compiler_params=pltpu.CompilerParams(vmem_limit_bytes=limit * 2**20),
        name=name,
        **kw,
    )(*args)


def route_kernel(cap, me_ref, r0, r1, r2, r3, place_ref, own_ref):
    homes = (r0, r1, r2, r3)
    flight, rows = len(homes), r0.shape[1]
    me = me_ref[0]
    a = lax.broadcasted_iota(jnp.int32, (rows, rows), 0)
    b = lax.broadcasted_iota(jnp.int32, (rows, rows), 1)
    before = (a < b).astype(F32).astype(BF)
    slots = lax.broadcasted_iota(jnp.int32, (flight * cap, rows), 0)
    for r, off in enumerate(OFFS):
        expert = lax.rem(me + off, flight)
        span = slice(r * flight * cap, (r + 1) * flight * cap)
        for delta, home in enumerate(homes):
            hit = (home[0:1, :] == expert) | (home[1:2, :] == expert)
            chosen = hit.astype(F32)
            rank = mm(jnp.broadcast_to(chosen, (8, rows)).astype(BF), before)[0:1]
            start = cap * JREL[(delta - off) % 4]
            target = jnp.where(chosen > 0.0, rank.astype(jnp.int32) + start, -1)
            hits = (slots == target).astype(F32).astype(BF)
            at = pl.multiple_of(lax.rem(me + delta, flight) * rows, rows)
            place_ref[span, pl.ds(at, rows)] = hits
            if delta == 0:
                own_ref[span, :] = hits


def route(me, routes, cap):
    flight, rows = len(routes), routes[0].shape[1]
    return call(
        functools.partial(route_kernel, cap),
        "route",
        [((flight * flight * cap, n), BF) for n in (flight * rows, rows)],
        me,
        *routes,
        in_specs=[SM] + [VM] * flight,
        out_specs=[VM, VM],
    )


def nt(a, b):
    return lax.dot_general(a, b, (((1,), (1,)), ((), ())), preferred_element_type=F32)


def selected_kernel(place, own, normed, weight, res, o0, o1, o2, o3, w_here, r_here, sems):
    size = o0.shape[0]
    chunks = weight.shape[0] // TILE

    def copy(c):
        span = pl.ds(pl.multiple_of(c * TILE, TILE), TILE)
        return pltpu.make_async_copy(weight.at[span], w_here.at[span], sems.at[c])

    @pl.loop(0, chunks)
    def _(c):
        copy(c).start()

    rest = pltpu.make_async_copy(res, r_here, sems.at[chunks])
    rest.start()
    picked = mm(place[...], normed[...]).astype(BF)
    rest.wait()

    @pl.loop(0, chunks)
    def _(c):
        span = pl.ds(pl.multiple_of(c * TILE, TILE), TILE)
        copy(c).wait()
        full = (nt(picked, w_here[span, :]) + mm(own[...], r_here[:, span])).astype(BF)
        for i, o in enumerate((o0, o1, o2, o3)):
            o[:, span] = full[i * size : (i + 1) * size]


def selected(place, own, normed, weight, res):
    picks, model = place.shape[0], weight.shape[0]
    return call(
        selected_kernel,
        "selected_projection",
        [((picks // 4, model), BF)] * 4,
        place,
        own,
        normed,
        weight,
        res,
        in_specs=[VM] * 3 + [ANY] * 2,
        out_specs=[VM] * 4,
        scratch_shapes=[
            pltpu.VMEM(weight.shape, BF),
            pltpu.VMEM(res.shape, BF),
            pltpu.SemaphoreType.DMA((model // TILE + 1,)),
        ],
        vmem=54,
    )


def whole_kernel(normed_ref, weight_ref, late, out_ref):
    out_ref[...] = nt(normed_ref[...], weight_ref[...]).astype(BF)


def whole_projection(normed, weight, late, tile=1024):
    total, (model, width) = normed.shape[0], weight.shape
    return call(
        whole_kernel,
        "whole_projection",
        [((total, model), BF)],
        normed,
        weight,
        late,
        grid=(model // tile,),
        in_specs=[
            pl.BlockSpec(normed.shape, lambda n: (0, 0)),
            pl.BlockSpec((tile, width), lambda n: (n, 0)),
            VM,
        ],
        out_specs=[pl.BlockSpec((total, tile), lambda n: (0, n))],
        cost_estimate=pl.CostEstimate(
            flops=2 * total * model * width, bytes_accessed=4 * model * width, transcendentals=0
        ),
        vmem=58,
    )[0]


def norm_kernel(a, b, c, d, gain, o0, o1, ready):
    ready[...] = jnp.zeros_like(ready)
    x = a[...].astype(F32) + b[...].astype(F32) + c[...].astype(F32) + d[...].astype(F32)
    x = x * lax.rsqrt(jnp.mean(x * x, -1, keepdims=True) + 1e-06) * gain[...]
    half = o0.shape[1]
    o0[...] = x[:, :half].astype(BF)
    o1[...] = x[:, half:].astype(BF)


def hold_kernel(held, late, same):
    pass


def stack_kernel(a0, a1, a2, a3, b0, b1, b2, b3, o0, o1):
    for i, (a, b) in enumerate(((a0, b0), (a1, b1), (a2, b2), (a3, b3))):
        o0[i] = a[...]
        o1[i] = b[...]


def by_y(rows, y):
    return [((z * 4 + y) * rows, z) for z in range(4)]


def gate_up(refs_a, refs_b, gu, x, part, arrive):
    rows, half = refs_a[0].shape[1:]
    each = half // TILE
    part[...] = jnp.zeros_like(part)

    @pl.loop(0, 2 * each)
    def _(c):
        for k, refs in enumerate((refs_a, refs_b)):

            @pl.when(c // each == k)
            def _():
                at = pl.ds(pl.multiple_of((c - k * each) * TILE, TILE), TILE)
                row = 0
                for ref in refs:
                    for i in range(ref.shape[0]):
                        x[row : row + rows, :] = ref[i, :, at]
                        row += rows

        arrive(c)
        wide = pl.ds(pl.multiple_of(c * TILE, TILE), TILE)
        units = gu[0].shape[0]
        for i, w in enumerate(gu):
            part[c // each, :, i * units : (i + 1) * units] += nt(x[...], w[:, wide])


def down_product(value, down, outs_a, outs_b):
    rows, half = outs_a[0].shape[1:]
    each = half // TILE

    @pl.loop(0, 2 * each)
    def _(c):
        wide = pl.ds(pl.multiple_of(c * TILE, TILE), TILE)
        full = mm(value[c // each], down[:, wide]).astype(BF)
        for k, outs in enumerate((outs_a, outs_b)):

            @pl.when(c // each == k)
            def _():
                at = pl.ds(pl.multiple_of((c - k * each) * TILE, TILE), TILE)
                row = 0
                for out in outs:
                    for i in range(out.shape[0]):
                        out[i, :, at] = full[row : row + rows]
                        row += rows


def near_kernel(
    a0, a1, a2, b0, b1, b2, gate, up, down, acc, gate_here, up_here, down_here, x, part, sems, last
):
    rows = a0.shape[1]
    block = 4 * rows
    chunks = gate.shape[1] // TILE

    def copies(c):
        cols = pl.ds(pl.multiple_of(c * TILE, TILE), TILE)
        pairs = ((gate, gate_here), (up, up_here))
        return [
            pltpu.make_async_copy(a.at[:, cols], b.at[:, cols], sems.at[c, i])
            for i, (a, b) in enumerate(pairs)
        ]

    @pl.loop(0, chunks)
    def _(c):
        for copy in copies(c):
            copy.start()

    whole = pltpu.make_async_copy(down, down_here, last)
    whole.start()

    def arrive(c):
        for copy in copies(c):
            copy.wait()

    gate_up((a0, a1, a2), (b0, b1, b2), (gate_here, up_here), x, part, arrive)
    acc[0 : 3 * block, :] = part[0]
    acc[3 * block :, :] = jnp.zeros((block, acc.shape[1]), F32)
    for y in range(3):
        for row, z in by_y(rows, y):
            at = y * block + z * rows
            acc[row : row + rows, :] += part[1, at : at + rows, :]
    whole.wait()


def far_kernel(acc, a3, a4, b3, b4, gate, up, down, hidden, oa3, oa4, ob3, ob4, x, part, own, value):
    rows = a3.shape[1]
    block = 4 * rows
    units = down.shape[0]
    gate_up((a3, a4), (b3, b4), (gate, up), x, part, lambda c: None)
    own[...] = acc[...]
    own[3 * block :, :] += part[0]
    for row, z in by_y(rows, 3):
        own[row : row + rows, :] += part[1, z * rows : (z + 1) * rows, :]
    g = own[:, :units]
    hidden[...] = (g / (1.0 + jnp.exp(-g)) * own[:, units:]).astype(BF)
    value[0] = hidden[3 * block :, :]
    for row, z in by_y(rows, 3):
        value[1, z * rows : (z + 1) * rows, :] = hidden[row : row + rows, :]
    down_product(value, down, (oa3, oa4), (ob3, ob4))


def rest_kernel(hidden, down, oa0, oa1, oa2, ob0, ob1, ob2, value):
    rows = oa0.shape[1]
    block = 4 * rows
    value[0] = hidden[: 3 * block, :]
    for y in range(3):
        for row, z in by_y(rows, y):
            at = y * block + z * rows
            value[1, at : at + rows, :] = hidden[row : row + rows, :]
    down_product(value, down, (oa0, oa1, oa2), (ob0, ob1, ob2))


def cost(flops):
    return pl.CostEstimate(flops=flops, bytes_accessed=2**20, transcendentals=0)


def near(xs, gate, up, down):
    rows = xs[0].shape[1]
    units, model = gate.shape
    return call(
        near_kernel,
        "near_rows",
        [((16 * rows, 2 * units), F32)] + [((units, model), BF)] * 3,
        *xs,
        gate,
        up,
        down,
        in_specs=[VM] * 6 + [ANY] * 3,
        out_specs=[VM] * 4,
        scratch_shapes=[
            pltpu.VMEM((12 * rows, TILE), BF),
            pltpu.VMEM((2, 12 * rows, 2 * units), F32),
            pltpu.SemaphoreType.DMA((model // TILE, 2)),
            pltpu.SemaphoreType.DMA,
        ],
        cost_estimate=cost(4 * 12 * rows * gate.size),
        vmem=24,
    )


def far(acc, xs, gate, up, down):
    rows, half = xs[0].shape[1:]
    units = down.shape[0]
    return call(
        far_kernel,
        "far_rows",
        [((16 * rows, units), BF)] + [((2, rows, half), BF)] * 4,
        acc,
        *xs,
        gate,
        up,
        down,
        in_specs=[VM] * 8,
        out_specs=[VM] * 5,
        scratch_shapes=[
            pltpu.VMEM((4 * rows, TILE), BF),
            pltpu.VMEM((2, 4 * rows, 2 * units), F32),
            pltpu.VMEM(acc.shape, F32),
            pltpu.VMEM((2, 4 * rows, units), BF),
        ],
        vmem=16,
    )


def rest(hidden, down, rows):
    half = down.shape[1] // 2
    return call(
        rest_kernel,
        "rest_rows",
        [((4, rows, half), BF)] * 6,
        hidden,
        down,
        in_specs=[VM] * 2,
        out_specs=[VM] * 6,
        scratch_shapes=[pltpu.VMEM((2, 12 * rows, hidden.shape[1]), BF)],
        cost_estimate=cost(2 * 12 * rows * down.size),
        vmem=12,
    )


def fold_kernel(bl0, ab0, up0, dn0, bl1, ab1, up1, dn1, ob0, oa0, ob1, oa1):
    for below, above, up, down, o_below, o_above in (
        (bl0, ab0, up0, dn0, ob0, oa0),
        (bl1, ab1, up1, dn1, ob1, oa1),
    ):
        o_above[0:2] = (above[0:2].astype(F32) + up[...].astype(F32)).astype(BF)
        o_above[2:4] = above[2:4]
        o_below[0:2] = below[0:2]
        o_below[2:4] = (below[2:4].astype(F32) + down[...].astype(F32)).astype(BF)


def phase_kernel(m0, u0, d0, m1, u1, d1, *outs):
    for k, (m, u, d) in enumerate(((m0, u0, d0), (m1, u1, d1))):
        total = m[...].astype(F32) + u[...].astype(F32) + d[...].astype(F32)
        for i in range(4):
            outs[4 * k + i][...] = total[i].astype(BF)


def served_kernel(cap, a0, a1, a2, a3, b0, b1, b2, b3, o0, o1, o2, o3):
    half = a0.shape[1]
    rows = a0.shape[0]
    padded = o0.shape[0]
    r = lax.broadcasted_iota(jnp.int32, (padded, rows), 0)
    c = lax.broadcasted_iota(jnp.int32, (padded, rows), 1)
    for k, parts in enumerate(((a0, a1, a2, a3), (b0, b1, b2, b3))):
        total = sum(p[...].astype(F32) for p in parts).astype(BF)
        for i, o in enumerate((o0, o1, o2, o3)):
            pick = ((c == r + i * cap) & (r < cap)).astype(F32).astype(BF)
            o[:, k * half : (k + 1) * half] = mm(pick, total).astype(BF)


def home_kernel(me_ref, routes_ref, res, mixed, gain, router, late, hidden_ref, coef_ref):
    x = res[...].astype(F32) + mixed[...].astype(F32)
    hidden_ref[...] = x
    normed = (x * lax.rsqrt(jnp.mean(x * x, -1, keepdims=True) + 1e-06) * gain[...]).astype(BF)
    logits = nt(normed, router[...])
    rows, experts = logits.shape
    labels = lax.broadcasted_iota(jnp.int32, (rows, experts), 1)
    one, two = routes_ref[:, 0:1], routes_ref[:, 1:2]
    first = jnp.sum(jnp.where(one == labels, logits, 0.0), -1, keepdims=True)
    second = jnp.sum(jnp.where(two == labels, logits, 0.0), -1, keepdims=True)
    gate0 = 1.0 / (1.0 + jnp.exp(second - first))
    gate1 = 1.0 / (1.0 + jnp.exp(first - second))
    cols = coef_ref.shape[1] // 2
    place = lax.broadcasted_iota(jnp.int32, (rows, cols), 1)
    a = lax.broadcasted_iota(jnp.int32, (rows, rows), 0)
    b = lax.broadcasted_iota(jnp.int32, (rows, rows), 1)
    before = (b < a).astype(F32).astype(BF)
    total = jnp.zeros((rows, cols), F32)
    for j, off in enumerate((0, 1, 3, 2)):
        expert_id = lax.rem(me_ref[0] + off, 4)
        hit0, hit1 = (one == expert_id).astype(F32), (two == expert_id).astype(F32)
        chosen = hit0 + hit1
        rank = mm(before, jnp.broadcast_to(chosen, (rows, 128)).astype(BF))[:, 0:1].astype(jnp.int32)
        total = total + jnp.where(place == rank + 16 * j, hit0 * gate0 + hit1 * gate1, 0.0)
    hi, lo = split(total)
    coef_ref[:, :cols] = hi
    coef_ref[:, cols:] = lo


def final_kernel(hidden, coef, b0, b1, b2, b3, out, back):
    for i, b in enumerate((b0, b1, b2, b3) * 2):
        back[16 * i : 16 * i + 16, :] = b[...]
    moe = mm(coef[...], back[...])
    out[...] = (hidden[...] + moe).astype(BF)


def up_one(x, axis):
    return lax.ppermute(x, axis, ring(4, 1))


def down_one(x, axis):
    return lax.ppermute(x, axis, ring(4, -1))


def across(x, axis):
    return lax.ppermute(x, axis, ring(4, 2))


def far_sides(below, above, axis):
    return up_one(below[:2], axis), down_one(above[2:], axis)


def shards(
    queries,
    keys,
    payload_vectors,
    log_decay,
    attn_gain,
    out_weight,
    residual,
    norm_gain,
    router_weight,
    picks,
    gate_weight,
    up_weight,
    down_weight,
):
    seqs, positions, width = queries.shape
    slice_len, model = residual.shape[1], residual.shape[2]
    shares = positions // slice_len
    rows = seqs * slice_len
    cap = 3 * rows // 32
    half = model // 2
    me = lax.axis_index("x").astype(jnp.int32).reshape(1)

    weight_out = lax.all_gather(out_weight.T, SEQ, axis=0, tiled=True)
    gate, up, down = [
        lax.all_gather(w[0], "core", axis=0, tiled=True)
        for w in (gate_weight, up_weight, down_weight)
    ]
    routes = picks.reshape(rows, 2)
    turned = routes.T
    all_routes = [turned] + [lax.ppermute(turned, "x", ring(4, -delta)) for delta in (1, 2, 3)]

    inner, states, cum = local_part(
        queries, keys, payload_vectors, log_decay.transpose(0, 2, 1)
    )
    arrived = lax.all_to_all(states, SEQ, 0, 0, tiled=True)
    prefix = lax.all_to_all(scan_states(arrived), SEQ, 0, 0, tiled=True)
    prefix = prefix.reshape(seqs * width // HEAD, HEAD, HEAD)
    normed = carried(
        queries, inner, cum, prefix, attn_gain.reshape(1, width), shares
    )
    normed = normed.reshape(shares * rows, width)

    place, own_place = route(me, all_routes, cap)
    flat = residual.reshape(rows, model)
    gain = norm_gain.reshape(1, model)
    to_up, to_down, to_far, here = selected(place, own_place, normed, weight_out, flat)
    whole = whole_projection(normed, weight_out, here)

    size = here.shape[0]
    a0, b0, ready = call(
        norm_kernel,
        "selected_norm",
        [((size, half), BF)] * 2 + [((8, 128), F32)],
        here,
        up_one(to_up, "x"),
        down_one(to_down, "x"),
        across(to_far, "x"),
        gain,
        in_specs=[VM] * 5,
        out_specs=[VM] * 3,
    )

    whole = call(
        hold_kernel,
        "hold",
        [(whole.shape, BF)],
        whole,
        ready,
        in_specs=[ANY, VM],
        out_specs=[ANY],
        input_output_aliases={0: 0},
        vmem=61,
    )[0]
    mixed = lax.psum_scatter(whole, "x", scatter_dimension=0, tiled=True)

    a4, b4 = call(
        stack_kernel,
        "stack",
        [((4, size, half), BF)] * 2,
        a0,
        up_one(a0, "y"),
        down_one(a0, "y"),
        across(a0, "y"),
        b0,
        up_one(b0, "z"),
        down_one(b0, "z"),
        across(b0, "z"),
        in_specs=[VM] * 8,
        out_specs=[VM] * 2,
        vmem=16,
    )
    a_below, a_above = up_one(a4, "z"), down_one(a4, "z")
    b_below, b_above = up_one(b4, "y"), down_one(b4, "y")
    a_far, b_far = far_sides(a_below, a_above, "z"), far_sides(b_below, b_above, "y")

    acc, gate, up, down = near((a4, a_below, a_above, b4, b_below, b_above), gate, up, down)
    hidden, *ends = far(acc, (*a_far, *b_far), gate, up, down)
    body = rest(hidden, down, size)
    oa, ob = (*body[:3], *ends[:2]), (*body[3:], *ends[2:])
    a_below, a_above, b_below, b_above = call(
        fold_kernel,
        "fold",
        [((4, size, half), BF)] * 4,
        oa[1],
        oa[2],
        up_one(oa[3], "z"),
        down_one(oa[4], "z"),
        ob[1],
        ob[2],
        up_one(ob[3], "y"),
        down_one(ob[4], "y"),
        in_specs=[VM] * 8,
        out_specs=[VM] * 4,
        vmem=16,
    )
    parts = call(
        phase_kernel,
        "phase",
        [((size, half), BF)] * 8,
        oa[0],
        up_one(a_above, "z"),
        down_one(a_below, "z"),
        ob[0],
        up_one(b_above, "y"),
        down_one(b_below, "y"),
        in_specs=[VM] * 6,
        out_specs=[VM] * 8,
        vmem=16,
    )
    s0, s1, s2, s3 = call(
        functools.partial(served_kernel, cap),
        "served",
        [((16, model), BF)] * 4,
        parts[0],
        up_one(parts[2], "y"),
        down_one(parts[1], "y"),
        across(parts[3], "y"),
        parts[4],
        up_one(parts[6], "z"),
        down_one(parts[5], "z"),
        across(parts[7], "z"),
        in_specs=[VM] * 8,
        out_specs=[VM] * 4,
    )

    hidden, coef = call(
        home_kernel,
        "home",
        [((rows, model), F32), ((rows, 128), BF)],
        me,
        routes,
        flat,
        mixed,
        gain,
        router_weight.T,
        a_below,
        in_specs=[SM] + [VM] * 6,
        out_specs=[VM] * 2,
        vmem=20,
    )
    out = call(
        final_kernel,
        "combine",
        [((rows, model), BF)],
        hidden,
        coef,
        s0,
        down_one(s1, "x"),
        up_one(s2, "x"),
        across(s3, "x"),
        in_specs=[VM] * 6,
        out_specs=[VM],
        scratch_shapes=[pltpu.VMEM((128, model), BF)],
        vmem=16,
    )[0]
    return out.reshape(seqs, slice_len, model)


def solution(mesh):
    shape = dict(mesh.shape)
    grid = Mesh(mesh.devices.reshape(4, shape["seq"] // 8, 2, shape["exp"]), SEQ + ("x",))
    everyone = SEQ + ("x",)
    placed = (
        P(None, SEQ, "x"),
        P(None, SEQ, "x"),
        P(None, SEQ, "x"),
        P(None, SEQ, "x"),
        P("x"),
        P("x", SEQ),
        P(None, everyone, None),
        P(),
        P(),
        P(None, everyone, None),
        P("x", SEQ, None),
        P("x", SEQ, None),
        P("x", SEQ, None),
    )
    return jax.shard_map(
        shards, mesh=grid, in_specs=placed, out_specs=P(None, everyone, None), check_vma=False
    )
```

```python
import functools

import jax
import jax.numpy as jnp
from jax import lax
from jax.experimental import pallas as pl
from jax.experimental.pallas import tpu as pltpu
from jax.sharding import Mesh, PartitionSpec as P

HEAD = 128
BF = jnp.bfloat16
F32 = jnp.float32
HI = lax.Precision.HIGHEST
SEQ = ("z", "y", "core")
TILE = 1024
DEC = 16
OFFS = (1, 3, 2, 0)
JREL = {0: 0, 3: 1, 1: 2, 2: 3}


VM = pl.BlockSpec(memory_space=pltpu.VMEM)
SM = pl.BlockSpec(memory_space=pltpu.SMEM)
ANY = pl.BlockSpec(memory_space=pl.ANY)
HBM = pl.BlockSpec(memory_space=pltpu.HBM)


def ring(n, k):
    return [(i, (i + k) % n) for i in range(n)]


def mm(a, b):
    return jnp.dot(a, b, preferred_element_type=F32)


def mm0(a, b):
    return lax.dot_general(a, b, (((0,), (0,)), ((), ())), preferred_element_type=F32)


def split(a):
    hi = a.astype(BF)
    return hi, (a - hi.astype(F32)).astype(BF)


def local_kernel(q_ref, k_ref, v_ref, d_ref, inner_ref, state_ref, cum_ref):
    heads, steps = d_ref.shape[1], d_ref.shape[2]
    row = lax.broadcasted_iota(jnp.int32, (steps, steps), 0)
    col = lax.broadcasted_iota(jnp.int32, (steps, steps), 1)
    later = row >= col
    upto = (row <= col).astype(F32)
    turned = jnp.dot(d_ref[0], upto, precision=HI, preferred_element_type=F32)
    cum = turned.T
    cum_ref[0] = cum
    final = cum[steps - 1 : steps, :]
    tail = jnp.exp(final - cum)
    ends = jnp.exp(final)
    piece = lax.broadcasted_iota(jnp.int32, (DEC, HEAD), 0)
    half = HEAD // 2
    for h in range(heads):
        sl = slice(h * HEAD, (h + 1) * HEAD)
        q, k, v = q_ref[0, :, sl], k_ref[0, :, sl], v_ref[0, :, sl]
        scores = lax.dot_general(q, k, (((1,), (1,)), ((), ())), preferred_element_type=F32)
        spread = cum[:, h : h + 1] - turned[h : h + 1, :]
        weights = jnp.where(later, jnp.exp(jnp.minimum(spread, 0.0)), 0.0) * scores
        whi, wlo = split(weights)
        inner_ref[0, :, sl] = mm(whi, v) + mm(wlo, v)
        khi, klo = split(k.astype(F32) * tail[:, h : h + 1])
        update = (mm0(khi, v) + mm0(klo, v)).astype(BF)
        end = jnp.broadcast_to(ends[:, h : h + 1], (DEC, HEAD))
        e1 = end.astype(BF).astype(F32)
        e2 = (end - e1).astype(BF).astype(F32)
        e3 = end - e1 - e2
        rows = jnp.where(piece == 0, e1, jnp.where(piece == 1, e2, jnp.where(piece == 2, e3, 0.0)))
        for r in range(2):
            state_ref[2 * h + r, :half, :] = update[r * half : (r + 1) * half]
            state_ref[2 * h + r, half:, :] = rows.astype(BF)


def local_part(q, k, v, d):
    seqs, steps, width = q.shape
    heads = width // HEAD
    half = HEAD // 2
    block = pl.BlockSpec((1, steps, width), lambda s: (s, 0, 0))
    thin = pl.BlockSpec((1, steps, heads), lambda s: (s, 0, 0))
    return pl.pallas_call(
        local_kernel,
        grid=(seqs,),
        in_specs=[block, block, block, pl.BlockSpec((1, heads, steps), lambda s: (s, 0, 0))],
        out_specs=[block, pl.BlockSpec((2 * heads, half + DEC, HEAD), lambda s: (s, 0, 0)), thin],
        out_shape=[
            jax.ShapeDtypeStruct((seqs, steps, width), F32),
            jax.ShapeDtypeStruct((seqs * heads * 2, half + DEC, HEAD), BF),
            jax.ShapeDtypeStruct((seqs, steps, heads), F32),
        ],
        compiler_params=pltpu.CompilerParams(vmem_limit_bytes=60 * 2**20),
        name="local_attention",
    )(q, k, v, d)


def scan_kernel(in_ref, out_ref):
    blocks = in_ref.shape[0]
    half = out_ref.shape[1]
    carry = jnp.zeros(out_ref.shape[1:], F32)
    for n in range(blocks):
        out_ref[n] = carry.astype(BF)
        dec = in_ref[n, half:, :].astype(F32)
        carry = carry * (dec[0:1] + dec[1:2] + dec[2:3]) + in_ref[n, :half, :].astype(F32)


def scan_states(arrived):
    blocks, rows, width = arrived.shape
    return pl.pallas_call(
        scan_kernel,
        out_shape=jax.ShapeDtypeStruct((blocks, rows - DEC, width), BF),
        compiler_params=pltpu.CompilerParams(vmem_limit_bytes=32 * 2**20),
        name="state_prefix",
    )(arrived)


def carry_kernel(q_ref, inner_ref, cum_ref, state_ref, gain_ref, out_ref):
    shares, slice_len = out_ref.shape[0], out_ref.shape[2]
    heads = cum_ref.shape[2]
    grow = jnp.exp(cum_ref[0])
    for h in range(heads):
        sl = slice(h * HEAD, (h + 1) * HEAD)
        head = inner_ref[0, :, sl] + mm(q_ref[0, :, sl], state_ref[h]) * grow[:, h : h + 1]
        scale = lax.rsqrt(jnp.mean(head * head, -1, keepdims=True) + 1e-06)
        normed = (head * scale * gain_ref[:, sl]).astype(BF)
        for a in range(shares):
            out_ref[a, 0, :, sl] = normed[
                a * slice_len : (a + 1) * slice_len
            ]


def carried(q, inner, cum, state, gain, shares):
    seqs, steps, width = q.shape
    heads = width // HEAD
    block = pl.BlockSpec((1, steps, width), lambda s: (s, 0, 0))
    return pl.pallas_call(
        carry_kernel,
        grid=(seqs,),
        in_specs=[
            block,
            block,
            pl.BlockSpec((1, steps, heads), lambda s: (s, 0, 0)),
            pl.BlockSpec((heads, HEAD, HEAD), lambda s: (s, 0, 0)),
            pl.BlockSpec((1, width), lambda s: (0, 0)),
        ],
        out_specs=pl.BlockSpec((shares, 1, steps // shares, width), lambda s: (0, s, 0, 0)),
        out_shape=jax.ShapeDtypeStruct((shares, seqs, steps // shares, width), BF),
        compiler_params=pltpu.CompilerParams(vmem_limit_bytes=32 * 2**20),
        name="carried_norm",
    )(q, inner, cum, state, gain)


def call(kernel, name, outs, *args, **kw):
    limit = kw.pop("vmem", 16)
    return pl.pallas_call(
        kernel,
        out_shape=[jax.ShapeDtypeStruct(s, d) for s, d in outs],
        compiler_params=pltpu.CompilerParams(vmem_limit_bytes=limit * 2**20),
        name=name,
        **kw,
    )(*args)


def route_kernel(cap, me_ref, r0, r1, r2, r3, place_ref, own_ref):
    homes = (r0, r1, r2, r3)
    flight, rows = len(homes), r0.shape[1]
    me = me_ref[0]
    a = lax.broadcasted_iota(jnp.int32, (rows, rows), 0)
    b = lax.broadcasted_iota(jnp.int32, (rows, rows), 1)
    before = (a < b).astype(F32).astype(BF)
    slots = lax.broadcasted_iota(jnp.int32, (flight * cap, rows), 0)
    for r, off in enumerate(OFFS):
        expert = lax.rem(me + off, flight)
        span = slice(r * flight * cap, (r + 1) * flight * cap)
        for delta, home in enumerate(homes):
            hit = (home[0:1, :] == expert) | (home[1:2, :] == expert)
            chosen = hit.astype(F32)
            rank = mm(jnp.broadcast_to(chosen, (8, rows)).astype(BF), before)[0:1]
            start = cap * JREL[(delta - off) % 4]
            target = jnp.where(chosen > 0.0, rank.astype(jnp.int32) + start, -1)
            hits = (slots == target).astype(F32).astype(BF)
            at = pl.multiple_of(lax.rem(me + delta, flight) * rows, rows)
            place_ref[span, pl.ds(at, rows)] = hits
            if delta == 0:
                own_ref[span, :] = hits


def route(me, routes, cap):
    flight, rows = len(routes), routes[0].shape[1]
    return call(
        functools.partial(route_kernel, cap),
        "route",
        [((flight * flight * cap, n), BF) for n in (flight * rows, rows)],
        me,
        *routes,
        in_specs=[SM] + [VM] * flight,
        out_specs=[VM, VM],
    )


def nt(a, b):
    return lax.dot_general(a, b, (((1,), (1,)), ((), ())), preferred_element_type=F32)


def selected_kernel(place, own, normed, weight, res, o0, o1, o2, o3, w_here, sems):
    size = o0.shape[0]
    chunks = weight.shape[0] // TILE

    def copy(c):
        slot = lax.rem(c, AHEAD + 1)
        span = pl.ds(pl.multiple_of(c * TILE, TILE), TILE)
        return pltpu.make_async_copy(weight.at[span], w_here.at[slot], sems.at[slot])

    for c in range(AHEAD):
        copy(c).start()
    picked = mm(place[...], normed[...]).astype(BF)

    @pl.loop(0, chunks)
    def _(c):
        @pl.when(c + AHEAD < chunks)
        def _():
            copy(c + AHEAD).start()

        span = pl.ds(pl.multiple_of(c * TILE, TILE), TILE)
        copy(c).wait()
        full = nt(picked, w_here[lax.rem(c, AHEAD + 1)]) + mm(own[...], res[:, span])
        full = full.astype(BF)
        for i, o in enumerate((o0, o1, o2, o3)):
            o[:, span] = full[i * size : (i + 1) * size]


def selected(place, own, normed, weight, res):
    picks, (model, width) = place.shape[0], weight.shape
    return call(
        selected_kernel,
        "selected_projection",
        [((picks // 4, model), BF)] * 4,
        place,
        own,
        normed,
        weight,
        res,
        in_specs=[VM] * 3 + [ANY, VM],
        out_specs=[VM] * 4,
        scratch_shapes=[
            pltpu.VMEM((AHEAD + 1, TILE, width), BF),
            pltpu.SemaphoreType.DMA((AHEAD + 1,)),
        ],
        vmem=48,
    )


def whole_kernel(normed_ref, weight_ref, late, out_ref):
    out_ref[...] = nt(normed_ref[...], weight_ref[...]).astype(BF)


def whole_projection(normed, weight, late, tile=1024):
    total, (model, width) = normed.shape[0], weight.shape
    return call(
        whole_kernel,
        "whole_projection",
        [((total, model), BF)],
        normed,
        weight,
        late,
        grid=(model // tile,),
        in_specs=[
            pl.BlockSpec(normed.shape, lambda n: (0, 0)),
            pl.BlockSpec((tile, width), lambda n: (n, 0)),
            VM,
        ],
        out_specs=[pl.BlockSpec((total, tile), lambda n: (0, n))],
        cost_estimate=pl.CostEstimate(
            flops=2 * total * model * width, bytes_accessed=4 * model * width, transcendentals=0
        ),
        vmem=58,
    )[0]


def norm_kernel(a, b, c, d, gain, o0, o1, ready):
    ready[...] = jnp.zeros_like(ready)
    x = a[...].astype(F32) + b[...].astype(F32) + c[...].astype(F32) + d[...].astype(F32)
    x = x * lax.rsqrt(jnp.mean(x * x, -1, keepdims=True) + 1e-06) * gain[...]
    half = o0.shape[1]
    o0[...] = x[:, :half].astype(BF)
    o1[...] = x[:, half:].astype(BF)


def hold_kernel(held, late, same):
    pass


def stack_kernel(a0, a1, a2, a3, b0, b1, b2, b3, o0, o1):
    for i, (a, b) in enumerate(((a0, b0), (a1, b1), (a2, b2), (a3, b3))):
        o0[i] = a[...]
        o1[i] = b[...]


def by_y(rows, y):
    return [((z * 4 + y) * rows, z) for z in range(4)]


AHEAD = 2


class Stream:
    def __init__(self, source, spans, buf, sems):
        self.source, self.spans, self.buf, self.sems = source, spans, buf, sems
        self.chunks = source.shape[1] // TILE

    def copies(self, c):
        slot = lax.rem(c, AHEAD + 1)
        cols = pl.ds(pl.multiple_of(c * TILE, TILE), TILE)
        made, at = [], 0
        for i, (start, size) in enumerate(self.spans):
            made.append(
                pltpu.make_async_copy(
                    self.source.at[pl.ds(start, size), cols],
                    self.buf.at[slot, pl.ds(at, size)],
                    self.sems.at[slot, i],
                )
            )
            at += size
        return made

    def start(self, c):
        for copy in self.copies(c):
            copy.start()

    def begin(self):
        for c in range(AHEAD):
            self.start(c)

    def run(self, body, then=None):
        @pl.loop(0, self.chunks)
        def _(c):
            @pl.when(c + AHEAD < self.chunks)
            def _():
                self.start(c + AHEAD)

            if then is not None:

                @pl.when(c + AHEAD >= self.chunks)
                def _():
                    then.start(c + AHEAD - self.chunks)

            for copy in self.copies(c):
                copy.wait()
            body(c, self.buf[lax.rem(c, AHEAD + 1)])


def gate_up_spans(units):
    return ((0, 2 * units), (3 * units, 2 * units))


def down_spans(units):
    return ((2 * units, units), (5 * units, units))


def gate_up(refs_a, refs_b, x, part, stream, then=None):
    rows, half = refs_a[0].shape[1:]
    each = half // TILE
    part[...] = jnp.zeros_like(part)

    def body(c, weights):
        for k, refs in enumerate((refs_a, refs_b)):

            @pl.when(c // each == k)
            def _():
                at = pl.ds(pl.multiple_of((c - k * each) * TILE, TILE), TILE)
                row = 0
                for ref in refs:
                    for i in range(ref.shape[0]):
                        x[row : row + rows, :] = ref[i, :, at]
                        row += rows

        part[c // each] += nt(x[...], weights)

    stream.run(body, then)


def down_product(value, stream, outs_a, outs_b):
    rows, half = outs_a[0].shape[1:]
    each = half // TILE

    def body(c, weights):
        full = mm(value[c // each], weights).astype(BF)
        for k, outs in enumerate((outs_a, outs_b)):

            @pl.when(c // each == k)
            def _():
                at = pl.ds(pl.multiple_of((c - k * each) * TILE, TILE), TILE)
                row = 0
                for out in outs:
                    for i in range(out.shape[0]):
                        out[i, :, at] = full[row : row + rows]
                        row += rows

    stream.run(body)


def near_kernel(a0, a1, a2, b0, b1, b2, weights, acc, x, part, buf, sems):
    rows = a0.shape[1]
    block = 4 * rows
    stream = Stream(weights, gate_up_spans(weights.shape[0] // 6), buf, sems)
    stream.begin()
    gate_up((a0, a1, a2), (b0, b1, b2), x, part, stream)
    acc[0 : 3 * block, :] = part[0]
    acc[3 * block :, :] = jnp.zeros((block, acc.shape[1]), F32)
    for y in range(3):
        for row, z in by_y(rows, y):
            at = y * block + z * rows
            acc[row : row + rows, :] += part[1, at : at + rows, :]


def far_kernel(
    acc, a3, a4, b3, b4, weights, hidden, oa3, oa4, ob3, ob4, x, part, own, value, buf, sems, dbuf, dsems
):
    rows = a3.shape[1]
    block = 4 * rows
    units = weights.shape[0] // 6
    stream = Stream(weights, gate_up_spans(units), buf, sems)
    downs = Stream(weights, down_spans(units), dbuf, dsems)
    stream.begin()
    gate_up((a3, a4), (b3, b4), x, part, stream, downs)
    own[...] = acc[...]
    own[3 * block :, :] += part[0]
    for row, z in by_y(rows, 3):
        own[row : row + rows, :] += part[1, z * rows : (z + 1) * rows, :]
    for core in range(2):
        g = own[:, 2 * core * units : (2 * core + 1) * units]
        u = own[:, (2 * core + 1) * units : (2 * core + 2) * units]
        hidden[:, core * units : (core + 1) * units] = (g / (1.0 + jnp.exp(-g)) * u).astype(BF)
    value[0] = hidden[3 * block :, :]
    for row, z in by_y(rows, 3):
        value[1, z * rows : (z + 1) * rows, :] = hidden[row : row + rows, :]
    down_product(value, downs, (oa3, oa4), (ob3, ob4))


def rest_kernel(hidden, weights, oa0, oa1, oa2, ob0, ob1, ob2, value, dbuf, dsems):
    rows = oa0.shape[1]
    block = 4 * rows
    downs = Stream(weights, down_spans(weights.shape[0] // 6), dbuf, dsems)
    downs.begin()
    value[0] = hidden[: 3 * block, :]
    for y in range(3):
        for row, z in by_y(rows, y):
            at = y * block + z * rows
            value[1, at : at + rows, :] = hidden[row : row + rows, :]
    down_product(value, downs, (oa0, oa1, oa2), (ob0, ob1, ob2))


def cost(flops):
    return pl.CostEstimate(flops=flops, bytes_accessed=2**20, transcendentals=0)


def slots(rows, parts):
    return [
        pltpu.VMEM((AHEAD + 1, rows, TILE), BF),
        pltpu.SemaphoreType.DMA((AHEAD + 1, parts)),
    ]


def near(xs, weights):
    rows = xs[0].shape[1]
    wide = weights.shape[0] * 2 // 3
    return call(
        near_kernel,
        "near_rows",
        [((16 * rows, wide), F32)],
        *xs,
        weights,
        in_specs=[VM] * 6 + [ANY],
        out_specs=[VM],
        scratch_shapes=[
            pltpu.VMEM((12 * rows, TILE), BF),
            pltpu.VMEM((2, 12 * rows, wide), F32),
            *slots(wide, 2),
        ],
        cost_estimate=cost(2 * 12 * rows * wide * weights.shape[1]),
        vmem=30,
    )[0]


def far(acc, xs, weights):
    rows, half = xs[0].shape[1:]
    wide = acc.shape[1]
    return call(
        far_kernel,
        "far_rows",
        [((16 * rows, wide // 2), BF)] + [((2, rows, half), BF)] * 4,
        acc,
        *xs,
        weights,
        in_specs=[VM] * 5 + [ANY],
        out_specs=[VM] * 5,
        scratch_shapes=[
            pltpu.VMEM((4 * rows, TILE), BF),
            pltpu.VMEM((2, 4 * rows, wide), F32),
            pltpu.VMEM(acc.shape, F32),
            pltpu.VMEM((2, 4 * rows, wide // 2), BF),
            *slots(wide, 2),
            *slots(wide // 2, 2),
        ],
        vmem=36,
    )


def rest(hidden, weights, rows):
    wide, half = hidden.shape[1], weights.shape[1] // 2
    return call(
        rest_kernel,
        "rest_rows",
        [((4, rows, half), BF)] * 6,
        hidden,
        weights,
        in_specs=[VM, ANY],
        out_specs=[VM] * 6,
        scratch_shapes=[pltpu.VMEM((2, 12 * rows, wide), BF), *slots(wide, 2)],
        cost_estimate=cost(2 * 12 * rows * wide * weights.shape[1]),
        vmem=36,
    )


def fold_kernel(bl0, ab0, up0, dn0, bl1, ab1, up1, dn1, ob0, oa0, ob1, oa1):
    for below, above, up, down, o_below, o_above in (
        (bl0, ab0, up0, dn0, ob0, oa0),
        (bl1, ab1, up1, dn1, ob1, oa1),
    ):
        o_above[0:2] = (above[0:2].astype(F32) + up[...].astype(F32)).astype(BF)
        o_above[2:4] = above[2:4]
        o_below[0:2] = below[0:2]
        o_below[2:4] = (below[2:4].astype(F32) + down[...].astype(F32)).astype(BF)


def phase_kernel(m0, u0, d0, m1, u1, d1, *outs):
    for k, (m, u, d) in enumerate(((m0, u0, d0), (m1, u1, d1))):
        total = m[...].astype(F32) + u[...].astype(F32) + d[...].astype(F32)
        for i in range(4):
            outs[4 * k + i][...] = total[i].astype(BF)


def served_kernel(cap, a0, a1, a2, a3, b0, b1, b2, b3, o0, o1, o2, o3):
    half = a0.shape[1]
    rows = a0.shape[0]
    padded = o0.shape[0]
    r = lax.broadcasted_iota(jnp.int32, (padded, rows), 0)
    c = lax.broadcasted_iota(jnp.int32, (padded, rows), 1)
    for k, parts in enumerate(((a0, a1, a2, a3), (b0, b1, b2, b3))):
        total = sum(p[...].astype(F32) for p in parts).astype(BF)
        for i, o in enumerate((o0, o1, o2, o3)):
            pick = ((c == r + i * cap) & (r < cap)).astype(F32).astype(BF)
            o[:, k * half : (k + 1) * half] = mm(pick, total).astype(BF)


def home_kernel(me_ref, routes_ref, res, mixed, gain, router, late, hidden_ref, coef_ref):
    x = res[...].astype(F32) + mixed[...].astype(F32)
    hidden_ref[...] = x
    normed = (x * lax.rsqrt(jnp.mean(x * x, -1, keepdims=True) + 1e-06) * gain[...]).astype(BF)
    logits = nt(normed, router[...])
    rows, experts = logits.shape
    labels = lax.broadcasted_iota(jnp.int32, (rows, experts), 1)
    one, two = routes_ref[:, 0:1], routes_ref[:, 1:2]
    first = jnp.sum(jnp.where(one == labels, logits, 0.0), -1, keepdims=True)
    second = jnp.sum(jnp.where(two == labels, logits, 0.0), -1, keepdims=True)
    gate0 = 1.0 / (1.0 + jnp.exp(second - first))
    gate1 = 1.0 / (1.0 + jnp.exp(first - second))
    cols = coef_ref.shape[1] // 2
    place = lax.broadcasted_iota(jnp.int32, (rows, cols), 1)
    a = lax.broadcasted_iota(jnp.int32, (rows, rows), 0)
    b = lax.broadcasted_iota(jnp.int32, (rows, rows), 1)
    before = (b < a).astype(F32).astype(BF)
    total = jnp.zeros((rows, cols), F32)
    for j, off in enumerate((0, 1, 3, 2)):
        expert_id = lax.rem(me_ref[0] + off, 4)
        hit0, hit1 = (one == expert_id).astype(F32), (two == expert_id).astype(F32)
        chosen = hit0 + hit1
        rank = mm(before, jnp.broadcast_to(chosen, (rows, 128)).astype(BF))[:, 0:1].astype(jnp.int32)
        total = total + jnp.where(place == rank + 16 * j, hit0 * gate0 + hit1 * gate1, 0.0)
    hi, lo = split(total)
    coef_ref[:, :cols] = hi
    coef_ref[:, cols:] = lo


def final_kernel(hidden, coef, b0, b1, b2, b3, out, back):
    for i, b in enumerate((b0, b1, b2, b3) * 2):
        back[16 * i : 16 * i + 16, :] = b[...]
    moe = mm(coef[...], back[...])
    out[...] = (hidden[...] + moe).astype(BF)


def up_one(x, axis):
    return lax.ppermute(x, axis, ring(4, 1))


def down_one(x, axis):
    return lax.ppermute(x, axis, ring(4, -1))


def across(x, axis):
    return lax.ppermute(x, axis, ring(4, 2))


def far_sides(below, above, axis):
    return up_one(below[:2], axis), down_one(above[2:], axis)


def shards(
    queries,
    keys,
    payload_vectors,
    log_decay,
    attn_gain,
    out_weight,
    residual,
    norm_gain,
    router_weight,
    picks,
    gate_weight,
    up_weight,
    down_weight,
):
    seqs, positions, width = queries.shape
    slice_len, model = residual.shape[1], residual.shape[2]
    shares = positions // slice_len
    rows = seqs * slice_len
    cap = 3 * rows // 32
    half = model // 2
    me = lax.axis_index("x").astype(jnp.int32).reshape(1)

    weight_out = lax.all_gather(out_weight.T, SEQ, axis=0, tiled=True)
    weights = jnp.concatenate([gate_weight[0], up_weight[0], down_weight[0]])
    weights = lax.all_gather(weights, "core", axis=0, tiled=True)
    routes = picks.reshape(rows, 2)
    turned = routes.T
    all_routes = [turned] + [lax.ppermute(turned, "x", ring(4, -delta)) for delta in (1, 2, 3)]

    inner, states, cum = local_part(
        queries, keys, payload_vectors, log_decay.transpose(0, 2, 1)
    )
    arrived = lax.all_to_all(states, SEQ, 0, 0, tiled=True)
    prefix = lax.all_to_all(scan_states(arrived), SEQ, 0, 0, tiled=True)
    prefix = prefix.reshape(seqs * width // HEAD, HEAD, HEAD)
    normed = carried(
        queries, inner, cum, prefix, attn_gain.reshape(1, width), shares
    )
    normed = normed.reshape(shares * rows, width)

    place, own_place = route(me, all_routes, cap)
    flat = residual.reshape(rows, model)
    gain = norm_gain.reshape(1, model)
    to_up, to_down, to_far, here = selected(place, own_place, normed, weight_out, flat)
    whole = whole_projection(normed, weight_out, here)

    size = here.shape[0]
    a0, b0, ready = call(
        norm_kernel,
        "selected_norm",
        [((size, half), BF)] * 2 + [((8, 128), F32)],
        here,
        up_one(to_up, "x"),
        down_one(to_down, "x"),
        across(to_far, "x"),
        gain,
        in_specs=[VM] * 5,
        out_specs=[VM] * 3,
    )

    whole = call(
        hold_kernel,
        "hold",
        [(whole.shape, BF)],
        whole,
        ready,
        in_specs=[ANY, VM],
        out_specs=[ANY],
        input_output_aliases={0: 0},
        vmem=61,
    )[0]
    mixed = lax.psum_scatter(whole, "x", scatter_dimension=0, tiled=True)

    a_across, b_across = across(a0, "y"), across(b0, "z")
    a4, b4 = call(
        stack_kernel,
        "stack",
        [((4, size, half), BF)] * 2,
        a0,
        up_one(a0, "y"),
        down_one(a0, "y"),
        a_across,
        b0,
        up_one(b0, "z"),
        down_one(b0, "z"),
        b_across,
        in_specs=[VM] * 8,
        out_specs=[VM] * 2,
        vmem=16,
    )
    a_below, a_above = up_one(a4, "z"), down_one(a4, "z")
    b_below, b_above = up_one(b4, "y"), down_one(b4, "y")
    a_far, b_far = far_sides(a_below, a_above, "z"), far_sides(b_below, b_above, "y")

    acc = near((a4, a_below, a_above, b4, b_below, b_above), weights)
    hidden, *ends = far(acc, (*a_far, *b_far), weights)
    body = rest(hidden, weights, size)
    oa, ob = (*body[:3], *ends[:2]), (*body[3:], *ends[2:])
    a_below, a_above, b_below, b_above = call(
        fold_kernel,
        "fold",
        [((4, size, half), BF)] * 4,
        oa[1],
        oa[2],
        up_one(oa[3], "z"),
        down_one(oa[4], "z"),
        ob[1],
        ob[2],
        up_one(ob[3], "y"),
        down_one(ob[4], "y"),
        in_specs=[VM] * 8,
        out_specs=[VM] * 4,
        vmem=16,
    )
    parts = call(
        phase_kernel,
        "phase",
        [((size, half), BF)] * 8,
        oa[0],
        up_one(a_above, "z"),
        down_one(a_below, "z"),
        ob[0],
        up_one(b_above, "y"),
        down_one(b_below, "y"),
        in_specs=[VM] * 6,
        out_specs=[VM] * 8,
        vmem=16,
    )
    s0, s1, s2, s3 = call(
        functools.partial(served_kernel, cap),
        "served",
        [((16, model), BF)] * 4,
        parts[0],
        up_one(parts[2], "y"),
        down_one(parts[1], "y"),
        across(parts[3], "y"),
        parts[4],
        up_one(parts[6], "z"),
        down_one(parts[5], "z"),
        across(parts[7], "z"),
        in_specs=[VM] * 8,
        out_specs=[VM] * 4,
    )

    hidden, coef = call(
        home_kernel,
        "home",
        [((rows, model), F32), ((rows, 128), BF)],
        me,
        routes,
        flat,
        mixed,
        gain,
        router_weight.T,
        a_below,
        in_specs=[SM] + [VM] * 6,
        out_specs=[VM] * 2,
        vmem=20,
    )
    out = call(
        final_kernel,
        "combine",
        [((rows, model), BF)],
        hidden,
        coef,
        s0,
        down_one(s1, "x"),
        up_one(s2, "x"),
        across(s3, "x"),
        in_specs=[VM] * 6,
        out_specs=[VM],
        scratch_shapes=[pltpu.VMEM((128, model), BF)],
        vmem=16,
    )[0]
    return out.reshape(seqs, slice_len, model)


def solution(mesh):
    shape = dict(mesh.shape)
    grid = Mesh(mesh.devices.reshape(4, shape["seq"] // 8, 2, shape["exp"]), SEQ + ("x",))
    everyone = SEQ + ("x",)
    placed = (
        P(None, SEQ, "x"),
        P(None, SEQ, "x"),
        P(None, SEQ, "x"),
        P(None, SEQ, "x"),
        P("x"),
        P("x", SEQ),
        P(None, everyone, None),
        P(),
        P(),
        P(None, everyone, None),
        P("x", SEQ, None),
        P("x", SEQ, None),
        P("x", SEQ, None),
    )
    return jax.shard_map(
        shards, mesh=grid, in_specs=placed, out_specs=P(None, everyone, None), check_vma=False
    )
```

```python
import functools

import jax
import jax.numpy as jnp
from jax import lax
from jax.experimental import pallas as pl
from jax.experimental.pallas import tpu as pltpu
from jax.sharding import Mesh, PartitionSpec as P

HEAD = 128
BF = jnp.bfloat16
F32 = jnp.float32
HI = lax.Precision.HIGHEST
SEQ = ("z", "y", "core")
TILE = 1024
DEC = 16
OFFS = (1, 3, 2, 0)
JREL = {0: 0, 3: 1, 1: 2, 2: 3}


VM = pl.BlockSpec(memory_space=pltpu.VMEM)
SM = pl.BlockSpec(memory_space=pltpu.SMEM)
ANY = pl.BlockSpec(memory_space=pl.ANY)
HBM = pl.BlockSpec(memory_space=pltpu.HBM)


def ring(n, k):
    return [(i, (i + k) % n) for i in range(n)]


def mm(a, b):
    return jnp.dot(a, b, preferred_element_type=F32)


def mm0(a, b):
    return lax.dot_general(a, b, (((0,), (0,)), ((), ())), preferred_element_type=F32)


def split(a):
    hi = a.astype(BF)
    return hi, (a - hi.astype(F32)).astype(BF)


def local_kernel(q_ref, k_ref, v_ref, d_ref, inner_ref, state_ref, cum_ref):
    heads, steps = d_ref.shape[1], d_ref.shape[2]
    row = lax.broadcasted_iota(jnp.int32, (steps, steps), 0)
    col = lax.broadcasted_iota(jnp.int32, (steps, steps), 1)
    later = row >= col
    upto = (row <= col).astype(F32)
    turned = jnp.dot(d_ref[0], upto, precision=HI, preferred_element_type=F32)
    cum = turned.T
    cum_ref[0] = cum
    final = cum[steps - 1 : steps, :]
    tail = jnp.exp(final - cum)
    ends = jnp.exp(final)
    piece = lax.broadcasted_iota(jnp.int32, (DEC, HEAD), 0)
    half = HEAD // 2
    for h in range(heads):
        sl = slice(h * HEAD, (h + 1) * HEAD)
        q, k, v = q_ref[0, :, sl], k_ref[0, :, sl], v_ref[0, :, sl]
        scores = lax.dot_general(q, k, (((1,), (1,)), ((), ())), preferred_element_type=F32)
        spread = cum[:, h : h + 1] - turned[h : h + 1, :]
        weights = jnp.where(later, jnp.exp(jnp.minimum(spread, 0.0)), 0.0) * scores
        whi, wlo = split(weights)
        inner_ref[0, :, sl] = mm(whi, v) + mm(wlo, v)
        khi, klo = split(k.astype(F32) * tail[:, h : h + 1])
        update = (mm0(khi, v) + mm0(klo, v)).astype(BF)
        end = jnp.broadcast_to(ends[:, h : h + 1], (DEC, HEAD))
        e1 = end.astype(BF).astype(F32)
        e2 = (end - e1).astype(BF).astype(F32)
        e3 = end - e1 - e2
        rows = jnp.where(piece == 0, e1, jnp.where(piece == 1, e2, jnp.where(piece == 2, e3, 0.0)))
        for r in range(2):
            state_ref[2 * h + r, :half, :] = update[r * half : (r + 1) * half]
            state_ref[2 * h + r, half:, :] = rows.astype(BF)


def local_part(q, k, v, d):
    seqs, steps, width = q.shape
    heads = width // HEAD
    half = HEAD // 2
    block = pl.BlockSpec((1, steps, width), lambda s: (s, 0, 0))
    thin = pl.BlockSpec((1, steps, heads), lambda s: (s, 0, 0))
    return pl.pallas_call(
        local_kernel,
        grid=(seqs,),
        in_specs=[block, block, block, pl.BlockSpec((1, heads, steps), lambda s: (s, 0, 0))],
        out_specs=[block, pl.BlockSpec((2 * heads, half + DEC, HEAD), lambda s: (s, 0, 0)), thin],
        out_shape=[
            jax.ShapeDtypeStruct((seqs, steps, width), F32),
            jax.ShapeDtypeStruct((seqs * heads * 2, half + DEC, HEAD), BF),
            jax.ShapeDtypeStruct((seqs, steps, heads), F32),
        ],
        compiler_params=pltpu.CompilerParams(vmem_limit_bytes=60 * 2**20),
        name="local_attention",
    )(q, k, v, d)


def scan_kernel(in_ref, out_ref):
    blocks = in_ref.shape[0]
    half = out_ref.shape[1]
    carry = jnp.zeros(out_ref.shape[1:], F32)
    for n in range(blocks):
        out_ref[n] = carry.astype(BF)
        dec = in_ref[n, half:, :].astype(F32)
        carry = carry * (dec[0:1] + dec[1:2] + dec[2:3]) + in_ref[n, :half, :].astype(F32)


def scan_states(arrived):
    blocks, rows, width = arrived.shape
    return pl.pallas_call(
        scan_kernel,
        out_shape=jax.ShapeDtypeStruct((blocks, rows - DEC, width), BF),
        compiler_params=pltpu.CompilerParams(vmem_limit_bytes=32 * 2**20),
        name="state_prefix",
    )(arrived)


def carry_kernel(q_ref, inner_ref, cum_ref, state_ref, gain_ref, out_ref):
    shares, slice_len = out_ref.shape[0], out_ref.shape[2]
    heads = cum_ref.shape[2]
    grow = jnp.exp(cum_ref[0])
    for h in range(heads):
        sl = slice(h * HEAD, (h + 1) * HEAD)
        head = inner_ref[0, :, sl] + mm(q_ref[0, :, sl], state_ref[h]) * grow[:, h : h + 1]
        scale = lax.rsqrt(jnp.mean(head * head, -1, keepdims=True) + 1e-06)
        normed = (head * scale * gain_ref[:, sl]).astype(BF)
        for a in range(shares):
            out_ref[a, 0, :, sl] = normed[
                a * slice_len : (a + 1) * slice_len
            ]


def carried(q, inner, cum, state, gain, shares):
    seqs, steps, width = q.shape
    heads = width // HEAD
    block = pl.BlockSpec((1, steps, width), lambda s: (s, 0, 0))
    return pl.pallas_call(
        carry_kernel,
        grid=(seqs,),
        in_specs=[
            block,
            block,
            pl.BlockSpec((1, steps, heads), lambda s: (s, 0, 0)),
            pl.BlockSpec((heads, HEAD, HEAD), lambda s: (s, 0, 0)),
            pl.BlockSpec((1, width), lambda s: (0, 0)),
        ],
        out_specs=pl.BlockSpec((shares, 1, steps // shares, width), lambda s: (0, s, 0, 0)),
        out_shape=jax.ShapeDtypeStruct((shares, seqs, steps // shares, width), BF),
        compiler_params=pltpu.CompilerParams(vmem_limit_bytes=32 * 2**20),
        name="carried_norm",
    )(q, inner, cum, state, gain)


def call(kernel, name, outs, *args, **kw):
    limit = kw.pop("vmem", 16)
    return pl.pallas_call(
        kernel,
        out_shape=[jax.ShapeDtypeStruct(s, d) for s, d in outs],
        compiler_params=pltpu.CompilerParams(vmem_limit_bytes=limit * 2**20),
        name=name,
        **kw,
    )(*args)


def route_kernel(cap, me_ref, r0, r1, r2, r3, place_ref, own_ref):
    homes = (r0, r1, r2, r3)
    flight, rows = len(homes), r0.shape[1]
    me = me_ref[0]
    a = lax.broadcasted_iota(jnp.int32, (rows, rows), 0)
    b = lax.broadcasted_iota(jnp.int32, (rows, rows), 1)
    before = (a < b).astype(F32).astype(BF)
    slots = lax.broadcasted_iota(jnp.int32, (flight * cap, rows), 0)
    for r, off in enumerate(OFFS):
        expert = lax.rem(me + off, flight)
        span = slice(r * flight * cap, (r + 1) * flight * cap)
        for delta, home in enumerate(homes):
            hit = (home[0:1, :] == expert) | (home[1:2, :] == expert)
            chosen = hit.astype(F32)
            rank = mm(jnp.broadcast_to(chosen, (8, rows)).astype(BF), before)[0:1]
            start = cap * JREL[(delta - off) % 4]
            target = jnp.where(chosen > 0.0, rank.astype(jnp.int32) + start, -1)
            hits = (slots == target).astype(F32).astype(BF)
            at = pl.multiple_of(lax.rem(me + delta, flight) * rows, rows)
            place_ref[span, pl.ds(at, rows)] = hits
            if delta == 0:
                own_ref[span, :] = hits


def route(me, routes, cap):
    flight, rows = len(routes), routes[0].shape[1]
    return call(
        functools.partial(route_kernel, cap),
        "route",
        [((flight * flight * cap, n), BF) for n in (flight * rows, rows)],
        me,
        *routes,
        in_specs=[SM] + [VM] * flight,
        out_specs=[VM, VM],
    )


def nt(a, b):
    return lax.dot_general(a, b, (((1,), (1,)), ((), ())), preferred_element_type=F32)


def selected_kernel(place, own, normed, weight, res, o0, o1, o2, o3, w_here, r_here, sems, last):
    size = o0.shape[0]
    chunks = weight.shape[0] // TILE

    def copy(c):
        slot = lax.rem(c, AHEAD + 1)
        span = pl.ds(pl.multiple_of(c * TILE, TILE), TILE)
        return pltpu.make_async_copy(weight.at[span], w_here.at[slot], sems.at[slot])

    rest = pltpu.make_async_copy(res, r_here, last)
    copy(0).start()
    rest.start()
    for c in range(1, AHEAD):
        copy(c).start()
    picked = mm(place[...], normed[...]).astype(BF)
    rest.wait()

    @pl.loop(0, chunks)
    def _(c):
        @pl.when(c + AHEAD < chunks)
        def _():
            copy(c + AHEAD).start()

        span = pl.ds(pl.multiple_of(c * TILE, TILE), TILE)
        copy(c).wait()
        full = nt(picked, w_here[lax.rem(c, AHEAD + 1)]) + mm(own[...], r_here[:, span])
        full = full.astype(BF)
        for i, o in enumerate((o0, o1, o2, o3)):
            o[:, span] = full[i * size : (i + 1) * size]


def selected(place, own, normed, weight, res):
    picks, (model, width) = place.shape[0], weight.shape
    return call(
        selected_kernel,
        "selected_projection",
        [((picks // 4, model), BF)] * 4,
        place,
        own,
        normed,
        weight,
        res,
        in_specs=[VM] * 3 + [ANY] * 2,
        out_specs=[VM] * 4,
        scratch_shapes=[
            pltpu.VMEM((AHEAD + 1, TILE, width), BF),
            pltpu.VMEM(res.shape, BF),
            pltpu.SemaphoreType.DMA((AHEAD + 1,)),
            pltpu.SemaphoreType.DMA,
        ],
        vmem=48,
    )


def whole_kernel(normed_ref, weight_ref, late, out_ref):
    out_ref[...] = nt(normed_ref[...], weight_ref[...]).astype(BF)


def whole_projection(normed, weight, late, tile=1024):
    total, (model, width) = normed.shape[0], weight.shape
    return call(
        whole_kernel,
        "whole_projection",
        [((total, model), BF)],
        normed,
        weight,
        late,
        grid=(model // tile,),
        in_specs=[
            pl.BlockSpec(normed.shape, lambda n: (0, 0)),
            pl.BlockSpec((tile, width), lambda n: (n, 0)),
            VM,
        ],
        out_specs=[pl.BlockSpec((total, tile), lambda n: (0, n))],
        cost_estimate=pl.CostEstimate(
            flops=2 * total * model * width, bytes_accessed=4 * model * width, transcendentals=0
        ),
        vmem=58,
    )[0]


def norm_kernel(a, b, c, d, gain, held, o0, o1, same):
    x = a[...].astype(F32) + b[...].astype(F32) + c[...].astype(F32) + d[...].astype(F32)
    x = x * lax.rsqrt(jnp.mean(x * x, -1, keepdims=True) + 1e-06) * gain[...]
    half = o0.shape[1]
    o0[...] = x[:, :half].astype(BF)
    o1[...] = x[:, half:].astype(BF)


def forward_kernel(a_below, b_below, a_above, b_above, a_up, b_up, a_down, b_down):
    a_up[...] = a_below[0:2]
    b_up[...] = b_below[0:2]
    a_down[...] = a_above[2:4]
    b_down[...] = b_above[2:4]


def stack_kernel(a0, b0, a3, b3, a1, b1, a2, b2, held, o0, o1, same):
    for i, (a, b) in enumerate(((a0, b0), (a1, b1), (a2, b2), (a3, b3))):
        o0[i] = a[...]
        o1[i] = b[...]


def by_y(rows, y):
    return [((z * 4 + y) * rows, z) for z in range(4)]


AHEAD = 2


class Stream:
    def __init__(self, source, spans, buf, sems):
        self.source, self.spans, self.buf, self.sems = source, spans, buf, sems
        self.chunks = source.shape[1] // TILE

    def copies(self, c):
        slot = lax.rem(c, AHEAD + 1)
        cols = pl.ds(pl.multiple_of(c * TILE, TILE), TILE)
        made, at = [], 0
        for i, (start, size) in enumerate(self.spans):
            made.append(
                pltpu.make_async_copy(
                    self.source.at[pl.ds(start, size), cols],
                    self.buf.at[slot, pl.ds(at, size)],
                    self.sems.at[slot, i],
                )
            )
            at += size
        return made

    def start(self, c):
        for copy in self.copies(c):
            copy.start()

    def begin(self):
        for c in range(AHEAD):
            self.start(c)

    def run(self, body, then=None):
        @pl.loop(0, self.chunks)
        def _(c):
            @pl.when(c + AHEAD < self.chunks)
            def _():
                self.start(c + AHEAD)

            if then is not None:

                @pl.when(c + AHEAD >= self.chunks)
                def _():
                    then.start(c + AHEAD - self.chunks)

            for copy in self.copies(c):
                copy.wait()
            body(c, self.buf[lax.rem(c, AHEAD + 1)])


def gate_up_spans(units):
    return ((0, 2 * units), (3 * units, 2 * units))


def down_spans(units):
    return ((2 * units, units), (5 * units, units))


def gate_up(refs_a, refs_b, x, part_a, part_b, stream, then=None):
    rows, half = refs_a[0].shape[1:]
    each = half // TILE
    part_a[...] = jnp.zeros_like(part_a)
    part_b[...] = jnp.zeros_like(part_b)

    def body(c, weights):
        for k, (refs, part) in enumerate(((refs_a, part_a), (refs_b, part_b))):

            @pl.when(c // each == k)
            def _():
                at = pl.ds(pl.multiple_of((c - k * each) * TILE, TILE), TILE)
                row = 0
                for ref in refs:
                    for i in range(ref.shape[0]):
                        x[row : row + rows, :] = ref[i, :, at]
                        row += rows
                part[...] += nt(x[...], weights)

    stream.run(body, then)


def down_product(value, stream, outs_a, outs_b):
    rows, half = outs_a[0].shape[1:]
    each = half // TILE

    def body(c, weights):
        full = mm(value[c // each], weights).astype(BF)
        for k, outs in enumerate((outs_a, outs_b)):

            @pl.when(c // each == k)
            def _():
                at = pl.ds(pl.multiple_of((c - k * each) * TILE, TILE), TILE)
                row = 0
                for out in outs:
                    for i in range(out.shape[0]):
                        out[i, :, at] = full[row : row + rows]
                        row += rows

    stream.run(body)


def near_kernel(a0, b0, a1, b1, a2, b2, weights, acc, x, part, buf, sems):
    rows = a0.shape[1]
    block = 4 * rows
    stream = Stream(weights, gate_up_spans(weights.shape[0] // 6), buf, sems)
    stream.begin()
    gate_up((a0, a1, a2), (b0, b1, b2), x, acc.at[pl.ds(0, 3 * block)], part, stream)
    acc[3 * block :, :] = jnp.zeros((block, acc.shape[1]), F32)
    for y in range(3):
        for row, z in by_y(rows, y):
            at = y * block + z * rows
            acc[row : row + rows, :] += part[at : at + rows, :]


def far_kernel(
    acc, a3, b3, a4, b4, weights, hidden, oa3, oa4, ob3, ob4, x, part, own, value, buf, sems, dbuf, dsems
):
    rows = a3.shape[1]
    block = 4 * rows
    units = weights.shape[0] // 6
    stream = Stream(weights, gate_up_spans(units), buf, sems)
    downs = Stream(weights, down_spans(units), dbuf, dsems)
    stream.begin()
    gate_up((a3, a4), (b3, b4), x, part.at[0], part.at[1], stream, downs)
    own[...] = acc[...]
    own[3 * block :, :] += part[0]
    for row, z in by_y(rows, 3):
        own[row : row + rows, :] += part[1, z * rows : (z + 1) * rows, :]
    for core in range(2):
        g = own[:, 2 * core * units : (2 * core + 1) * units]
        u = own[:, (2 * core + 1) * units : (2 * core + 2) * units]
        hidden[:, core * units : (core + 1) * units] = (g / (1.0 + jnp.exp(-g)) * u).astype(BF)
    value[0] = hidden[3 * block :, :]
    for row, z in by_y(rows, 3):
        value[1, z * rows : (z + 1) * rows, :] = hidden[row : row + rows, :]
    down_product(value, downs, (oa3, oa4), (ob3, ob4))


def rest_kernel(hidden, weights, oa0, oa1, oa2, ob0, ob1, ob2, value, dbuf, dsems):
    rows = oa0.shape[1]
    block = 4 * rows
    downs = Stream(weights, down_spans(weights.shape[0] // 6), dbuf, dsems)
    downs.begin()
    value[0] = hidden[: 3 * block, :]
    for y in range(3):
        for row, z in by_y(rows, y):
            at = y * block + z * rows
            value[1, at : at + rows, :] = hidden[row : row + rows, :]
    down_product(value, downs, (oa0, oa1, oa2), (ob0, ob1, ob2))


def cost(flops):
    return pl.CostEstimate(flops=flops, bytes_accessed=2**20, transcendentals=0)


def slots(rows, parts):
    return [
        pltpu.VMEM((AHEAD + 1, rows, TILE), BF),
        pltpu.SemaphoreType.DMA((AHEAD + 1, parts)),
    ]


def near(xs, weights):
    rows = xs[0].shape[1]
    wide = weights.shape[0] * 2 // 3
    return call(
        near_kernel,
        "near_rows",
        [((16 * rows, wide), F32)],
        *xs,
        weights,
        in_specs=[VM] * 6 + [ANY],
        out_specs=[VM],
        scratch_shapes=[
            pltpu.VMEM((12 * rows, TILE), BF),
            pltpu.VMEM((12 * rows, wide), F32),
            *slots(wide, 2),
        ],
        cost_estimate=cost(2 * 12 * rows * wide * weights.shape[1]),
        vmem=30,
    )[0]


def far(acc, xs, weights):
    rows, half = xs[0].shape[1:]
    wide = acc.shape[1]
    return call(
        far_kernel,
        "far_rows",
        [((16 * rows, wide // 2), BF)] + [((2, rows, half), BF)] * 4,
        acc,
        *xs,
        weights,
        in_specs=[VM] * 5 + [ANY],
        out_specs=[VM] * 5,
        scratch_shapes=[
            pltpu.VMEM((4 * rows, TILE), BF),
            pltpu.VMEM((2, 4 * rows, wide), F32),
            pltpu.VMEM(acc.shape, F32),
            pltpu.VMEM((2, 4 * rows, wide // 2), BF),
            *slots(wide, 2),
            *slots(wide // 2, 2),
        ],
        vmem=32,
    )


def rest(hidden, weights, rows):
    wide, half = hidden.shape[1], weights.shape[1] // 2
    return call(
        rest_kernel,
        "rest_rows",
        [((4, rows, half), BF)] * 6,
        hidden,
        weights,
        in_specs=[VM, ANY],
        out_specs=[VM] * 6,
        scratch_shapes=[pltpu.VMEM((2, 12 * rows, wide), BF), *slots(wide, 2)],
        cost_estimate=cost(2 * 12 * rows * wide * weights.shape[1]),
        vmem=32,
    )


def fold_kernel(bl0, ab0, bl1, ab1, up0, up1, dn0, dn1, ob0, oa0, ob1, oa1):
    for below, above, up, down, o_below, o_above in (
        (bl0, ab0, up0, dn0, ob0, oa0),
        (bl1, ab1, up1, dn1, ob1, oa1),
    ):
        o_above[0:2] = (above[0:2].astype(F32) + up[...].astype(F32)).astype(BF)
        o_above[2:4] = above[2:4]
        o_below[0:2] = below[0:2]
        o_below[2:4] = (below[2:4].astype(F32) + down[...].astype(F32)).astype(BF)


def phase_kernel(m0, m1, u0, u1, d0, d1, *outs):
    for k, (m, u, d) in enumerate(((m0, u0, d0), (m1, u1, d1))):
        total = m[...].astype(F32) + u[...].astype(F32) + d[...].astype(F32)
        for i in range(4):
            outs[4 * k + i][...] = total[i].astype(BF)


def served_kernel(cap, a0, b0, a3, b3, a1, b1, a2, b2, o0, o1, o2, o3):
    half = a0.shape[1]
    rows = a0.shape[0]
    padded = o0.shape[0]
    r = lax.broadcasted_iota(jnp.int32, (padded, rows), 0)
    c = lax.broadcasted_iota(jnp.int32, (padded, rows), 1)
    for k, parts in enumerate(((a0, a1, a2, a3), (b0, b1, b2, b3))):
        total = sum(p[...].astype(F32) for p in parts).astype(BF)
        for i, o in enumerate((o0, o1, o2, o3)):
            pick = ((c == r + i * cap) & (r < cap)).astype(F32).astype(BF)
            o[:, k * half : (k + 1) * half] = mm(pick, total).astype(BF)


def home_kernel(me_ref, routes_ref, res, mixed, gain, router, late, hidden_ref, coef_ref):
    x = res[...].astype(F32) + mixed[...].astype(F32)
    hidden_ref[...] = x
    normed = (x * lax.rsqrt(jnp.mean(x * x, -1, keepdims=True) + 1e-06) * gain[...]).astype(BF)
    logits = nt(normed, router[...])
    rows, experts = logits.shape
    labels = lax.broadcasted_iota(jnp.int32, (rows, experts), 1)
    one, two = routes_ref[:, 0:1], routes_ref[:, 1:2]
    first = jnp.sum(jnp.where(one == labels, logits, 0.0), -1, keepdims=True)
    second = jnp.sum(jnp.where(two == labels, logits, 0.0), -1, keepdims=True)
    gate0 = 1.0 / (1.0 + jnp.exp(second - first))
    gate1 = 1.0 / (1.0 + jnp.exp(first - second))
    cols = coef_ref.shape[1] // 2
    place = lax.broadcasted_iota(jnp.int32, (rows, cols), 1)
    a = lax.broadcasted_iota(jnp.int32, (rows, rows), 0)
    b = lax.broadcasted_iota(jnp.int32, (rows, rows), 1)
    before = (b < a).astype(F32).astype(BF)
    total = jnp.zeros((rows, cols), F32)
    for j, off in enumerate((0, 1, 3, 2)):
        expert_id = lax.rem(me_ref[0] + off, 4)
        hit0, hit1 = (one == expert_id).astype(F32), (two == expert_id).astype(F32)
        chosen = hit0 + hit1
        rank = mm(before, jnp.broadcast_to(chosen, (rows, 128)).astype(BF))[:, 0:1].astype(jnp.int32)
        total = total + jnp.where(place == rank + 16 * j, hit0 * gate0 + hit1 * gate1, 0.0)
    hi, lo = split(total)
    coef_ref[:, :cols] = hi
    coef_ref[:, cols:] = lo


def final_kernel(hidden, coef, b0, b1, b2, b3, out, back):
    for i, b in enumerate((b0, b1, b2, b3) * 2):
        back[16 * i : 16 * i + 16, :] = b[...]
    moe = mm(coef[...], back[...])
    out[...] = (hidden[...] + moe).astype(BF)


def up_one(x, axis):
    return lax.ppermute(x, axis, ring(4, 1))


def down_one(x, axis):
    return lax.ppermute(x, axis, ring(4, -1))


def across(x, axis):
    return lax.ppermute(x, axis, ring(4, 2))


def shards(
    queries,
    keys,
    payload_vectors,
    log_decay,
    attn_gain,
    out_weight,
    residual,
    norm_gain,
    router_weight,
    picks,
    gate_weight,
    up_weight,
    down_weight,
):
    seqs, positions, width = queries.shape
    slice_len, model = residual.shape[1], residual.shape[2]
    shares = positions // slice_len
    rows = seqs * slice_len
    cap = 3 * rows // 32
    half = model // 2
    me = lax.axis_index("x").astype(jnp.int32).reshape(1)

    weight_out = lax.all_gather(out_weight.T, SEQ, axis=0, tiled=True)
    weights = jnp.concatenate([gate_weight[0], up_weight[0], down_weight[0]])
    weights = lax.all_gather(weights, "core", axis=0, tiled=True)
    routes = picks.reshape(rows, 2)
    turned = routes.T
    all_routes = [turned] + [lax.ppermute(turned, "x", ring(4, -delta)) for delta in (1, 2, 3)]

    inner, states, cum = local_part(
        queries, keys, payload_vectors, log_decay.transpose(0, 2, 1)
    )
    arrived = lax.all_to_all(states, SEQ, 0, 0, tiled=True)
    prefix = lax.all_to_all(scan_states(arrived), SEQ, 0, 0, tiled=True)
    prefix = prefix.reshape(seqs * width // HEAD, HEAD, HEAD)
    normed = carried(
        queries, inner, cum, prefix, attn_gain.reshape(1, width), shares
    )
    normed = normed.reshape(shares * rows, width)

    place, own_place = route(me, all_routes, cap)
    flat = residual.reshape(rows, model)
    gain = norm_gain.reshape(1, model)
    to_up, to_down, to_far, here = selected(place, own_place, normed, weight_out, flat)
    whole = whole_projection(normed, weight_out, here)

    size = here.shape[0]
    a0, b0, whole = call(
        norm_kernel,
        "selected_norm",
        [((size, half), BF)] * 2 + [(whole.shape, BF)],
        here,
        up_one(to_up, "x"),
        down_one(to_down, "x"),
        across(to_far, "x"),
        gain,
        whole,
        in_specs=[VM] * 5 + [ANY],
        out_specs=[VM] * 2 + [ANY],
        input_output_aliases={5: 2},
        vmem=58,
    )

    mixed = lax.psum_scatter(whole, "x", scatter_dimension=0, tiled=True)

    a4, b4, weights = call(
        stack_kernel,
        "stack",
        [((4, size, half), BF)] * 2 + [(weights.shape, BF)],
        a0,
        b0,
        across(a0, "y"),
        across(b0, "z"),
        up_one(a0, "y"),
        up_one(b0, "z"),
        down_one(a0, "y"),
        down_one(b0, "z"),
        weights,
        in_specs=[VM] * 8 + [ANY],
        out_specs=[VM] * 2 + [ANY],
        input_output_aliases={8: 2},
        vmem=50,
    )
    a_below, b_below = up_one(a4, "z"), up_one(b4, "y")
    a_above, b_above = down_one(a4, "z"), down_one(b4, "y")
    a_up, b_up, a_down, b_down = call(
        forward_kernel,
        "forward",
        [((2, size, half), BF)] * 4,
        a_below,
        b_below,
        a_above,
        b_above,
        in_specs=[VM] * 4,
        out_specs=[VM] * 4,
        vmem=8,
    )
    ends_in = (up_one(a_up, "z"), up_one(b_up, "y"), down_one(a_down, "z"), down_one(b_down, "y"))

    acc = near((a4, b4, a_below, b_below, a_above, b_above), weights)
    hidden, *ends = far(acc, ends_in, weights)
    body = rest(hidden, weights, size)
    oa, ob = (*body[:3], *ends[:2]), (*body[3:], *ends[2:])
    a_below, a_above, b_below, b_above = call(
        fold_kernel,
        "fold",
        [((4, size, half), BF)] * 4,
        oa[1],
        oa[2],
        ob[1],
        ob[2],
        up_one(oa[3], "z"),
        up_one(ob[3], "y"),
        down_one(oa[4], "z"),
        down_one(ob[4], "y"),
        in_specs=[VM] * 8,
        out_specs=[VM] * 4,
        vmem=16,
    )
    parts = call(
        phase_kernel,
        "phase",
        [((size, half), BF)] * 8,
        oa[0],
        ob[0],
        up_one(a_above, "z"),
        up_one(b_above, "y"),
        down_one(a_below, "z"),
        down_one(b_below, "y"),
        in_specs=[VM] * 6,
        out_specs=[VM] * 8,
        vmem=16,
    )
    s0, s1, s2, s3 = call(
        functools.partial(served_kernel, cap),
        "served",
        [((16, model), BF)] * 4,
        parts[0],
        parts[4],
        across(parts[3], "y"),
        across(parts[7], "z"),
        up_one(parts[2], "y"),
        up_one(parts[6], "z"),
        down_one(parts[1], "y"),
        down_one(parts[5], "z"),
        in_specs=[VM] * 8,
        out_specs=[VM] * 4,
    )

    hidden, coef = call(
        home_kernel,
        "home",
        [((rows, model), F32), ((rows, 128), BF)],
        me,
        routes,
        flat,
        mixed,
        gain,
        router_weight.T,
        a_below,
        in_specs=[SM] + [VM] * 6,
        out_specs=[VM] * 2,
        vmem=20,
    )
    out = call(
        final_kernel,
        "combine",
        [((rows, model), BF)],
        hidden,
        coef,
        s0,
        down_one(s1, "x"),
        up_one(s2, "x"),
        across(s3, "x"),
        in_specs=[VM] * 6,
        out_specs=[VM],
        scratch_shapes=[pltpu.VMEM((128, model), BF)],
        vmem=16,
    )[0]
    return out.reshape(seqs, slice_len, model)


def solution(mesh):
    shape = dict(mesh.shape)
    grid = Mesh(mesh.devices.reshape(4, shape["seq"] // 8, 2, shape["exp"]), SEQ + ("x",))
    everyone = SEQ + ("x",)
    placed = (
        P(None, SEQ, "x"),
        P(None, SEQ, "x"),
        P(None, SEQ, "x"),
        P(None, SEQ, "x"),
        P("x"),
        P("x", SEQ),
        P(None, everyone, None),
        P(),
        P(),
        P(None, everyone, None),
        P("x", SEQ, None),
        P("x", SEQ, None),
        P("x", SEQ, None),
    )
    return jax.shard_map(
        shards, mesh=grid, in_specs=placed, out_specs=P(None, everyone, None), check_vma=False
    )
```

```python
import functools

import jax
import jax.numpy as jnp
from jax import lax
from jax.experimental import pallas as pl
from jax.experimental.pallas import tpu as pltpu
from jax.sharding import Mesh, PartitionSpec as P

HEAD = 128
BF = jnp.bfloat16
F32 = jnp.float32
HI = lax.Precision.HIGHEST
SEQ = ("z", "y", "core")
TILE = 1024
DEC = 16
OFFS = (1, 3, 2, 0)
JREL = {0: 0, 3: 1, 1: 2, 2: 3}


VM = pl.BlockSpec(memory_space=pltpu.VMEM)
SM = pl.BlockSpec(memory_space=pltpu.SMEM)
ANY = pl.BlockSpec(memory_space=pl.ANY)
HBM = pl.BlockSpec(memory_space=pltpu.HBM)


def ring(n, k):
    return [(i, (i + k) % n) for i in range(n)]


def mm(a, b):
    return jnp.dot(a, b, preferred_element_type=F32)


def mm0(a, b):
    return lax.dot_general(a, b, (((0,), (0,)), ((), ())), preferred_element_type=F32)


def split(a):
    hi = a.astype(BF)
    return hi, (a - hi.astype(F32)).astype(BF)


def local_kernel(q_ref, k_ref, v_ref, d_ref, inner_ref, state_ref, cum_ref):
    heads, steps = d_ref.shape[1], d_ref.shape[2]
    row = lax.broadcasted_iota(jnp.int32, (steps, steps), 0)
    col = lax.broadcasted_iota(jnp.int32, (steps, steps), 1)
    later = row >= col
    upto = (row <= col).astype(F32)
    turned = jnp.dot(d_ref[0], upto, precision=HI, preferred_element_type=F32)
    cum = turned.T
    cum_ref[0] = cum
    final = cum[steps - 1 : steps, :]
    tail = jnp.exp(final - cum)
    ends = jnp.exp(final)
    piece = lax.broadcasted_iota(jnp.int32, (DEC, HEAD), 0)
    half = HEAD // 2
    for h in range(heads):
        sl = slice(h * HEAD, (h + 1) * HEAD)
        q, k, v = q_ref[0, :, sl], k_ref[0, :, sl], v_ref[0, :, sl]
        scores = lax.dot_general(q, k, (((1,), (1,)), ((), ())), preferred_element_type=F32)
        spread = cum[:, h : h + 1] - turned[h : h + 1, :]
        weights = jnp.where(later, jnp.exp(jnp.minimum(spread, 0.0)), 0.0) * scores
        whi, wlo = split(weights)
        inner_ref[0, :, sl] = mm(whi, v) + mm(wlo, v)
        khi, klo = split(k.astype(F32) * tail[:, h : h + 1])
        update = (mm0(khi, v) + mm0(klo, v)).astype(BF)
        end = jnp.broadcast_to(ends[:, h : h + 1], (DEC, HEAD))
        e1 = end.astype(BF).astype(F32)
        e2 = (end - e1).astype(BF).astype(F32)
        e3 = end - e1 - e2
        rows = jnp.where(piece == 0, e1, jnp.where(piece == 1, e2, jnp.where(piece == 2, e3, 0.0)))
        for r in range(2):
            state_ref[2 * h + r, :half, :] = update[r * half : (r + 1) * half]
            state_ref[2 * h + r, half:, :] = rows.astype(BF)


def local_part(q, k, v, d):
    seqs, steps, width = q.shape
    heads = width // HEAD
    half = HEAD // 2
    block = pl.BlockSpec((1, steps, width), lambda s: (s, 0, 0))
    thin = pl.BlockSpec((1, steps, heads), lambda s: (s, 0, 0))
    return pl.pallas_call(
        local_kernel,
        grid=(seqs,),
        in_specs=[block, block, block, pl.BlockSpec((1, heads, steps), lambda s: (s, 0, 0))],
        out_specs=[block, pl.BlockSpec((2 * heads, half + DEC, HEAD), lambda s: (s, 0, 0)), thin],
        out_shape=[
            jax.ShapeDtypeStruct((seqs, steps, width), F32),
            jax.ShapeDtypeStruct((seqs * heads * 2, half + DEC, HEAD), BF),
            jax.ShapeDtypeStruct((seqs, steps, heads), F32),
        ],
        compiler_params=pltpu.CompilerParams(vmem_limit_bytes=60 * 2**20),
        name="local_attention",
    )(q, k, v, d)


def scan_kernel(in_ref, out_ref):
    blocks = in_ref.shape[0]
    half = out_ref.shape[1]
    carry = jnp.zeros(out_ref.shape[1:], F32)
    for n in range(blocks):
        out_ref[n] = carry.astype(BF)
        dec = in_ref[n, half:, :].astype(F32)
        carry = carry * (dec[0:1] + dec[1:2] + dec[2:3]) + in_ref[n, :half, :].astype(F32)


def scan_states(arrived):
    blocks, rows, width = arrived.shape
    return pl.pallas_call(
        scan_kernel,
        out_shape=jax.ShapeDtypeStruct((blocks, rows - DEC, width), BF),
        compiler_params=pltpu.CompilerParams(vmem_limit_bytes=32 * 2**20),
        name="state_prefix",
    )(arrived)


def carry_kernel(q_ref, inner_ref, cum_ref, state_ref, gain_ref, out_ref):
    shares, slice_len = out_ref.shape[0], out_ref.shape[2]
    heads = cum_ref.shape[2]
    grow = jnp.exp(cum_ref[0])
    for h in range(heads):
        sl = slice(h * HEAD, (h + 1) * HEAD)
        head = inner_ref[0, :, sl] + mm(q_ref[0, :, sl], state_ref[h]) * grow[:, h : h + 1]
        scale = lax.rsqrt(jnp.mean(head * head, -1, keepdims=True) + 1e-06)
        normed = (head * scale * gain_ref[:, sl]).astype(BF)
        for a in range(shares):
            out_ref[a, 0, :, sl] = normed[
                a * slice_len : (a + 1) * slice_len
            ]


def carried(q, inner, cum, state, gain, shares):
    seqs, steps, width = q.shape
    heads = width // HEAD
    block = pl.BlockSpec((1, steps, width), lambda s: (s, 0, 0))
    return pl.pallas_call(
        carry_kernel,
        grid=(seqs,),
        in_specs=[
            block,
            block,
            pl.BlockSpec((1, steps, heads), lambda s: (s, 0, 0)),
            pl.BlockSpec((heads, HEAD, HEAD), lambda s: (s, 0, 0)),
            pl.BlockSpec((1, width), lambda s: (0, 0)),
        ],
        out_specs=pl.BlockSpec((shares, 1, steps // shares, width), lambda s: (0, s, 0, 0)),
        out_shape=jax.ShapeDtypeStruct((shares, seqs, steps // shares, width), BF),
        compiler_params=pltpu.CompilerParams(vmem_limit_bytes=32 * 2**20),
        name="carried_norm",
    )(q, inner, cum, state, gain)


def call(kernel, name, outs, *args, **kw):
    limit = kw.pop("vmem", 16)
    return pl.pallas_call(
        kernel,
        out_shape=[jax.ShapeDtypeStruct(s, d) for s, d in outs],
        compiler_params=pltpu.CompilerParams(vmem_limit_bytes=limit * 2**20),
        name=name,
        **kw,
    )(*args)


def route_kernel(cap, me_ref, r0, r1, r2, r3, place_ref, own_ref):
    homes = (r0, r1, r2, r3)
    flight, rows = len(homes), r0.shape[1]
    me = me_ref[0]
    a = lax.broadcasted_iota(jnp.int32, (rows, rows), 0)
    b = lax.broadcasted_iota(jnp.int32, (rows, rows), 1)
    before = (a < b).astype(F32).astype(BF)
    slots = lax.broadcasted_iota(jnp.int32, (flight * cap, rows), 0)
    for r, off in enumerate(OFFS):
        expert = lax.rem(me + off, flight)
        span = slice(r * flight * cap, (r + 1) * flight * cap)
        for delta, home in enumerate(homes):
            hit = (home[0:1, :] == expert) | (home[1:2, :] == expert)
            chosen = hit.astype(F32)
            rank = mm(jnp.broadcast_to(chosen, (8, rows)).astype(BF), before)[0:1]
            start = cap * JREL[(delta - off) % 4]
            target = jnp.where(chosen > 0.0, rank.astype(jnp.int32) + start, -1)
            hits = (slots == target).astype(F32).astype(BF)
            at = pl.multiple_of(lax.rem(me + delta, flight) * rows, rows)
            place_ref[span, pl.ds(at, rows)] = hits
            if delta == 0:
                own_ref[span, :] = hits


def route(me, routes, cap):
    flight, rows = len(routes), routes[0].shape[1]
    return call(
        functools.partial(route_kernel, cap),
        "route",
        [((flight * flight * cap, n), BF) for n in (flight * rows, rows)],
        me,
        *routes,
        in_specs=[SM] + [VM] * flight,
        out_specs=[VM, VM],
    )


def nt(a, b):
    return lax.dot_general(a, b, (((1,), (1,)), ((), ())), preferred_element_type=F32)


def pick_kernel(place, normed, out):
    out[...] = mm(place[...], normed[...]).astype(BF)


def selected_kernel(picked, own, weight, res, o0, o1, o2, o3, w_here, r_here, sems, last):
    size = o0.shape[0]
    chunks = weight.shape[0] // TILE

    def copy(c):
        slot = lax.rem(c, AHEAD + 1)
        span = pl.ds(pl.multiple_of(c * TILE, TILE), TILE)
        return pltpu.make_async_copy(weight.at[span], w_here.at[slot], sems.at[slot])

    rest = pltpu.make_async_copy(res, r_here, last)
    copy(0).start()
    rest.start()
    for c in range(1, AHEAD):
        copy(c).start()
    rest.wait()

    @pl.loop(0, chunks)
    def _(c):
        @pl.when(c + AHEAD < chunks)
        def _():
            copy(c + AHEAD).start()

        span = pl.ds(pl.multiple_of(c * TILE, TILE), TILE)
        copy(c).wait()
        full = nt(picked[...], w_here[lax.rem(c, AHEAD + 1)]) + mm(own[...], r_here[:, span])
        full = full.astype(BF)
        for i, o in enumerate((o0, o1, o2, o3)):
            o[:, span] = full[i * size : (i + 1) * size]


def selected(picked, own, weight, res):
    picks, (model, width) = picked.shape[0], weight.shape
    return call(
        selected_kernel,
        "selected_projection",
        [((picks // 4, model), BF)] * 4,
        picked,
        own,
        weight,
        res,
        in_specs=[VM] * 2 + [ANY] * 2,
        out_specs=[VM] * 4,
        scratch_shapes=[
            pltpu.VMEM((AHEAD + 1, TILE, width), BF),
            pltpu.VMEM(res.shape, BF),
            pltpu.SemaphoreType.DMA((AHEAD + 1,)),
            pltpu.SemaphoreType.DMA,
        ],
        vmem=48,
    )


def whole_kernel(normed_ref, weight_ref, out_ref, done_ref):
    out_ref[...] = nt(normed_ref[...], weight_ref[...]).astype(BF)
    done_ref[...] = jnp.zeros_like(done_ref)


def whole_projection(normed, weight, tile=1024):
    total, (model, width) = normed.shape[0], weight.shape
    return call(
        whole_kernel,
        "whole_projection",
        [((total, model), BF), ((8, 128), F32)],
        normed,
        weight,
        grid=(model // tile,),
        in_specs=[
            pl.BlockSpec(normed.shape, lambda n: (0, 0)),
            pl.BlockSpec((tile, width), lambda n: (n, 0)),
        ],
        out_specs=[
            pl.BlockSpec((total, tile), lambda n: (0, n)),
            pl.BlockSpec((8, 128), lambda n: (0, 0)),
        ],
        cost_estimate=pl.CostEstimate(
            flops=2 * total * model * width, bytes_accessed=4 * model * width, transcendentals=0
        ),
        vmem=58,
    )


def norm_kernel(a, b, c, d, gain, done, o0, o1):
    x = a[...].astype(F32) + b[...].astype(F32) + c[...].astype(F32) + d[...].astype(F32)
    x = x * lax.rsqrt(jnp.mean(x * x, -1, keepdims=True) + 1e-06) * gain[...]
    half = o0.shape[1]
    o0[...] = x[:, :half].astype(BF)
    o1[...] = x[:, half:].astype(BF)


def forward_kernel(a_below, b_below, a_above, b_above, a_up, b_up, a_down, b_down):
    a_up[...] = a_below[0:2]
    b_up[...] = b_below[0:2]
    a_down[...] = a_above[2:4]
    b_down[...] = b_above[2:4]


def stack_kernel(a0, b0, a3, b3, a1, b1, a2, b2, h0, h1, o0, o1, *same):
    for i, (a, b) in enumerate(((a0, b0), (a1, b1), (a2, b2), (a3, b3))):
        o0[i] = a[...]
        o1[i] = b[...]


def by_y(rows, y):
    return [((z * 4 + y) * rows, z) for z in range(4)]


AHEAD = 2


class Stream:
    def __init__(self, source, spans, buf, sems):
        self.source, self.spans, self.buf, self.sems = source, spans, buf, sems
        self.chunks = source.shape[1] // TILE

    def copies(self, c):
        slot = lax.rem(c, AHEAD + 1)
        cols = pl.ds(pl.multiple_of(c * TILE, TILE), TILE)
        made, at = [], 0
        for i, (start, size) in enumerate(self.spans):
            made.append(
                pltpu.make_async_copy(
                    self.source.at[pl.ds(start, size), cols],
                    self.buf.at[slot, pl.ds(at, size)],
                    self.sems.at[slot, i],
                )
            )
            at += size
        return made

    def start(self, c):
        for copy in self.copies(c):
            copy.start()

    def begin(self):
        for c in range(AHEAD):
            self.start(c)

    def run(self, body, then=None):
        @pl.loop(0, self.chunks)
        def _(c):
            @pl.when(c + AHEAD < self.chunks)
            def _():
                self.start(c + AHEAD)

            if then is not None:

                @pl.when(c + AHEAD >= self.chunks)
                def _():
                    then.start(c + AHEAD - self.chunks)

            for copy in self.copies(c):
                copy.wait()
            body(c, self.buf[lax.rem(c, AHEAD + 1)])


def gate_up_spans(units):
    return ((0, 2 * units), (3 * units, 2 * units))


def down_spans(units):
    return ((2 * units, units), (5 * units, units))


def gate_up(refs_a, refs_b, x, part_a, part_b, stream, then=None):
    rows, half = refs_a[0].shape[1:]
    each = half // TILE
    part_a[...] = jnp.zeros_like(part_a)
    part_b[...] = jnp.zeros_like(part_b)

    def body(c, weights):
        for k, (refs, part) in enumerate(((refs_a, part_a), (refs_b, part_b))):

            @pl.when(c // each == k)
            def _():
                at = pl.ds(pl.multiple_of((c - k * each) * TILE, TILE), TILE)
                row = 0
                for ref in refs:
                    for i in range(ref.shape[0]):
                        x[row : row + rows, :] = ref[i, :, at]
                        row += rows
                part[...] += nt(x[...], weights)

    stream.run(body, then)


def down_product(value, stream, outs_a, outs_b):
    rows, half = outs_a[0].shape[1:]
    each = half // TILE

    def body(c, weights):
        full = mm(value[c // each], weights).astype(BF)
        for k, outs in enumerate((outs_a, outs_b)):

            @pl.when(c // each == k)
            def _():
                at = pl.ds(pl.multiple_of((c - k * each) * TILE, TILE), TILE)
                row = 0
                for out in outs:
                    for i in range(out.shape[0]):
                        out[i, :, at] = full[row : row + rows]
                        row += rows

    stream.run(body)


def near_kernel(a0, b0, a1, b1, a2, b2, weights, acc, x, part, buf, sems):
    rows = a0.shape[1]
    block = 4 * rows
    stream = Stream(weights, gate_up_spans(weights.shape[0] // 6), buf, sems)
    stream.begin()
    gate_up((a0, a1, a2), (b0, b1, b2), x, acc.at[pl.ds(0, 3 * block)], part, stream)
    acc[3 * block :, :] = jnp.zeros((block, acc.shape[1]), F32)
    for y in range(3):
        for row, z in by_y(rows, y):
            at = y * block + z * rows
            acc[row : row + rows, :] += part[at : at + rows, :]


def far_kernel(
    acc, a3, b3, a4, b4, weights, hidden, oa3, oa4, ob3, ob4, x, part, own, value, buf, sems, dbuf, dsems
):
    rows = a3.shape[1]
    block = 4 * rows
    units = weights.shape[0] // 6
    stream = Stream(weights, gate_up_spans(units), buf, sems)
    downs = Stream(weights, down_spans(units), dbuf, dsems)
    stream.begin()
    gate_up((a3, a4), (b3, b4), x, part.at[0], part.at[1], stream, downs)
    own[...] = acc[...]
    own[3 * block :, :] += part[0]
    for row, z in by_y(rows, 3):
        own[row : row + rows, :] += part[1, z * rows : (z + 1) * rows, :]
    for core in range(2):
        g = own[:, 2 * core * units : (2 * core + 1) * units]
        u = own[:, (2 * core + 1) * units : (2 * core + 2) * units]
        hidden[:, core * units : (core + 1) * units] = (g / (1.0 + jnp.exp(-g)) * u).astype(BF)
    value[0] = hidden[3 * block :, :]
    for row, z in by_y(rows, 3):
        value[1, z * rows : (z + 1) * rows, :] = hidden[row : row + rows, :]
    down_product(value, downs, (oa3, oa4), (ob3, ob4))


def rest_kernel(hidden, weights, oa0, oa1, oa2, ob0, ob1, ob2, value, dbuf, dsems):
    rows = oa0.shape[1]
    block = 4 * rows
    downs = Stream(weights, down_spans(weights.shape[0] // 6), dbuf, dsems)
    downs.begin()
    value[0] = hidden[: 3 * block, :]
    for y in range(3):
        for row, z in by_y(rows, y):
            at = y * block + z * rows
            value[1, at : at + rows, :] = hidden[row : row + rows, :]
    down_product(value, downs, (oa0, oa1, oa2), (ob0, ob1, ob2))


def cost(flops):
    return pl.CostEstimate(flops=flops, bytes_accessed=2**20, transcendentals=0)


def slots(rows, parts):
    return [
        pltpu.VMEM((AHEAD + 1, rows, TILE), BF),
        pltpu.SemaphoreType.DMA((AHEAD + 1, parts)),
    ]


def near(xs, weights):
    rows = xs[0].shape[1]
    wide = weights.shape[0] * 2 // 3
    return call(
        near_kernel,
        "near_rows",
        [((16 * rows, wide), F32)],
        *xs,
        weights,
        in_specs=[VM] * 6 + [ANY],
        out_specs=[VM],
        scratch_shapes=[
            pltpu.VMEM((12 * rows, TILE), BF),
            pltpu.VMEM((12 * rows, wide), F32),
            *slots(wide, 2),
        ],
        cost_estimate=cost(2 * 12 * rows * wide * weights.shape[1]),
        vmem=30,
    )[0]


def far(acc, xs, weights):
    rows, half = xs[0].shape[1:]
    wide = acc.shape[1]
    return call(
        far_kernel,
        "far_rows",
        [((16 * rows, wide // 2), BF)] + [((2, rows, half), BF)] * 4,
        acc,
        *xs,
        weights,
        in_specs=[VM] * 5 + [ANY],
        out_specs=[VM] * 5,
        scratch_shapes=[
            pltpu.VMEM((4 * rows, TILE), BF),
            pltpu.VMEM((2, 4 * rows, wide), F32),
            pltpu.VMEM(acc.shape, F32),
            pltpu.VMEM((2, 4 * rows, wide // 2), BF),
            *slots(wide, 2),
            *slots(wide // 2, 2),
        ],
        vmem=32,
    )


def rest(hidden, weights, rows):
    wide, half = hidden.shape[1], weights.shape[1] // 2
    return call(
        rest_kernel,
        "rest_rows",
        [((4, rows, half), BF)] * 6,
        hidden,
        weights,
        in_specs=[VM, ANY],
        out_specs=[VM] * 6,
        scratch_shapes=[pltpu.VMEM((2, 12 * rows, wide), BF), *slots(wide, 2)],
        cost_estimate=cost(2 * 12 * rows * wide * weights.shape[1]),
        vmem=32,
    )


def fold_kernel(bl0, ab0, bl1, ab1, up0, up1, dn0, dn1, ob0, oa0, ob1, oa1):
    for below, above, up, down, o_below, o_above in (
        (bl0, ab0, up0, dn0, ob0, oa0),
        (bl1, ab1, up1, dn1, ob1, oa1),
    ):
        o_above[0:2] = (above[0:2].astype(F32) + up[...].astype(F32)).astype(BF)
        o_above[2:4] = above[2:4]
        o_below[0:2] = below[0:2]
        o_below[2:4] = (below[2:4].astype(F32) + down[...].astype(F32)).astype(BF)


def phase_kernel(m0, m1, u0, u1, d0, d1, *outs):
    for k, (m, u, d) in enumerate(((m0, u0, d0), (m1, u1, d1))):
        total = m[...].astype(F32) + u[...].astype(F32) + d[...].astype(F32)
        for i in range(4):
            outs[4 * k + i][...] = total[i].astype(BF)


def served_kernel(cap, a0, b0, a3, b3, a1, b1, a2, b2, o0, o1, o2, o3):
    half = a0.shape[1]
    rows = a0.shape[0]
    padded = o0.shape[0]
    r = lax.broadcasted_iota(jnp.int32, (padded, rows), 0)
    c = lax.broadcasted_iota(jnp.int32, (padded, rows), 1)
    for k, parts in enumerate(((a0, a1, a2, a3), (b0, b1, b2, b3))):
        total = sum(p[...].astype(F32) for p in parts).astype(BF)
        for i, o in enumerate((o0, o1, o2, o3)):
            pick = ((c == r + i * cap) & (r < cap)).astype(F32).astype(BF)
            o[:, k * half : (k + 1) * half] = mm(pick, total).astype(BF)


def home_kernel(me_ref, routes_ref, res, mixed, gain, router, late, hidden_ref, coef_ref):
    x = res[...].astype(F32) + mixed[...].astype(F32)
    hidden_ref[...] = x
    normed = (x * lax.rsqrt(jnp.mean(x * x, -1, keepdims=True) + 1e-06) * gain[...]).astype(BF)
    logits = nt(normed, router[...])
    rows, experts = logits.shape
    labels = lax.broadcasted_iota(jnp.int32, (rows, experts), 1)
    one, two = routes_ref[:, 0:1], routes_ref[:, 1:2]
    first = jnp.sum(jnp.where(one == labels, logits, 0.0), -1, keepdims=True)
    second = jnp.sum(jnp.where(two == labels, logits, 0.0), -1, keepdims=True)
    gate0 = 1.0 / (1.0 + jnp.exp(second - first))
    gate1 = 1.0 / (1.0 + jnp.exp(first - second))
    cols = coef_ref.shape[1] // 2
    place = lax.broadcasted_iota(jnp.int32, (rows, cols), 1)
    a = lax.broadcasted_iota(jnp.int32, (rows, rows), 0)
    b = lax.broadcasted_iota(jnp.int32, (rows, rows), 1)
    before = (b < a).astype(F32).astype(BF)
    total = jnp.zeros((rows, cols), F32)
    for j, off in enumerate((0, 1, 3, 2)):
        expert_id = lax.rem(me_ref[0] + off, 4)
        hit0, hit1 = (one == expert_id).astype(F32), (two == expert_id).astype(F32)
        chosen = hit0 + hit1
        rank = mm(before, jnp.broadcast_to(chosen, (rows, 128)).astype(BF))[:, 0:1].astype(jnp.int32)
        total = total + jnp.where(place == rank + 16 * j, hit0 * gate0 + hit1 * gate1, 0.0)
    hi, lo = split(total)
    coef_ref[:, :cols] = hi
    coef_ref[:, cols:] = lo


def final_kernel(hidden, coef, b0, b1, b2, b3, out, back):
    for i, b in enumerate((b0, b1, b2, b3) * 2):
        back[16 * i : 16 * i + 16, :] = b[...]
    moe = mm(coef[...], back[...])
    out[...] = (hidden[...] + moe).astype(BF)


def up_one(x, axis):
    return lax.ppermute(x, axis, ring(4, 1))


def down_one(x, axis):
    return lax.ppermute(x, axis, ring(4, -1))


def across(x, axis):
    return lax.ppermute(x, axis, ring(4, 2))


def shards(
    queries,
    keys,
    payload_vectors,
    log_decay,
    attn_gain,
    out_weight,
    residual,
    norm_gain,
    router_weight,
    picks,
    gate_weight,
    up_weight,
    down_weight,
):
    seqs, positions, width = queries.shape
    slice_len, model = residual.shape[1], residual.shape[2]
    shares = positions // slice_len
    rows = seqs * slice_len
    cap = 3 * rows // 32
    half = model // 2
    me = lax.axis_index("x").astype(jnp.int32).reshape(1)

    weight_out = lax.all_gather(out_weight.T, SEQ, axis=0, tiled=True)
    weights = jnp.concatenate([gate_weight[0], up_weight[0], down_weight[0]])
    weights = lax.all_gather(weights, "core", axis=0, tiled=True)
    routes = picks.reshape(rows, 2)
    turned = routes.T
    all_routes = [turned] + [lax.ppermute(turned, "x", ring(4, -delta)) for delta in (1, 2, 3)]

    inner, states, cum = local_part(
        queries, keys, payload_vectors, log_decay.transpose(0, 2, 1)
    )
    arrived = lax.all_to_all(states, SEQ, 0, 0, tiled=True)
    prefix = lax.all_to_all(scan_states(arrived), SEQ, 0, 0, tiled=True)
    prefix = prefix.reshape(seqs * width // HEAD, HEAD, HEAD)
    normed = carried(
        queries, inner, cum, prefix, attn_gain.reshape(1, width), shares
    )
    normed = normed.reshape(shares * rows, width)

    place, own_place = route(me, all_routes, cap)
    flat = residual.reshape(rows, model)
    gain = norm_gain.reshape(1, model)
    picked = call(
        pick_kernel,
        "pick",
        [((place.shape[0], width), BF)],
        place,
        normed,
        in_specs=[VM] * 2,
        out_specs=[VM],
        vmem=8,
    )[0]
    to_up, to_down, to_far, here = selected(picked, own_place, weight_out, flat)
    whole, done = whole_projection(normed, weight_out)

    size = here.shape[0]
    a0, b0 = call(
        norm_kernel,
        "selected_norm",
        [((size, half), BF)] * 2,
        here,
        across(to_far, "x"),
        up_one(to_up, "x"),
        down_one(to_down, "x"),
        gain,
        done,
        in_specs=[VM] * 6,
        out_specs=[VM] * 2,
    )

    a4, b4, weights, whole = call(
        stack_kernel,
        "stack",
        [((4, size, half), BF)] * 2 + [(weights.shape, BF), (whole.shape, BF)],
        a0,
        b0,
        across(a0, "y"),
        across(b0, "z"),
        up_one(a0, "y"),
        up_one(b0, "z"),
        down_one(a0, "y"),
        down_one(b0, "z"),
        weights,
        whole,
        in_specs=[VM] * 8 + [ANY] * 2,
        out_specs=[VM] * 2 + [ANY] * 2,
        input_output_aliases={8: 2, 9: 3},
        vmem=54,
    )
    mixed = lax.psum_scatter(whole, "x", scatter_dimension=0, tiled=True)
    a_below, b_below = up_one(a4, "z"), up_one(b4, "y")
    a_above, b_above = down_one(a4, "z"), down_one(b4, "y")
    a_up, b_up, a_down, b_down = call(
        forward_kernel,
        "forward",
        [((2, size, half), BF)] * 4,
        a_below,
        b_below,
        a_above,
        b_above,
        in_specs=[VM] * 4,
        out_specs=[VM] * 4,
        vmem=8,
    )
    ends_in = (up_one(a_up, "z"), up_one(b_up, "y"), down_one(a_down, "z"), down_one(b_down, "y"))

    acc = near((a4, b4, a_below, b_below, a_above, b_above), weights)
    hidden, *ends = far(acc, ends_in, weights)
    body = rest(hidden, weights, size)
    oa, ob = (*body[:3], *ends[:2]), (*body[3:], *ends[2:])
    a_below, a_above, b_below, b_above = call(
        fold_kernel,
        "fold",
        [((4, size, half), BF)] * 4,
        oa[1],
        oa[2],
        ob[1],
        ob[2],
        up_one(oa[3], "z"),
        up_one(ob[3], "y"),
        down_one(oa[4], "z"),
        down_one(ob[4], "y"),
        in_specs=[VM] * 8,
        out_specs=[VM] * 4,
        vmem=16,
    )
    parts = call(
        phase_kernel,
        "phase",
        [((size, half), BF)] * 8,
        oa[0],
        ob[0],
        up_one(a_above, "z"),
        up_one(b_above, "y"),
        down_one(a_below, "z"),
        down_one(b_below, "y"),
        in_specs=[VM] * 6,
        out_specs=[VM] * 8,
        vmem=16,
    )
    s0, s1, s2, s3 = call(
        functools.partial(served_kernel, cap),
        "served",
        [((16, model), BF)] * 4,
        parts[0],
        parts[4],
        across(parts[3], "y"),
        across(parts[7], "z"),
        up_one(parts[2], "y"),
        up_one(parts[6], "z"),
        down_one(parts[1], "y"),
        down_one(parts[5], "z"),
        in_specs=[VM] * 8,
        out_specs=[VM] * 4,
    )

    hidden, coef = call(
        home_kernel,
        "home",
        [((rows, model), F32), ((rows, 128), BF)],
        me,
        routes,
        flat,
        mixed,
        gain,
        router_weight.T,
        a_below,
        in_specs=[SM] + [VM] * 6,
        out_specs=[VM] * 2,
        vmem=20,
    )
    out = call(
        final_kernel,
        "combine",
        [((rows, model), BF)],
        hidden,
        coef,
        s0,
        down_one(s1, "x"),
        up_one(s2, "x"),
        across(s3, "x"),
        in_specs=[VM] * 6,
        out_specs=[VM],
        scratch_shapes=[pltpu.VMEM((128, model), BF)],
        vmem=16,
    )[0]
    return out.reshape(seqs, slice_len, model)


def solution(mesh):
    shape = dict(mesh.shape)
    grid = Mesh(mesh.devices.reshape(4, shape["seq"] // 8, 2, shape["exp"]), SEQ + ("x",))
    everyone = SEQ + ("x",)
    placed = (
        P(None, SEQ, "x"),
        P(None, SEQ, "x"),
        P(None, SEQ, "x"),
        P(None, SEQ, "x"),
        P("x"),
        P("x", SEQ),
        P(None, everyone, None),
        P(),
        P(),
        P(None, everyone, None),
        P("x", SEQ, None),
        P("x", SEQ, None),
        P("x", SEQ, None),
    )
    return jax.shard_map(
        shards, mesh=grid, in_specs=placed, out_specs=P(None, everyone, None), check_vma=False
    )
```

```python
import functools

import jax
import jax.numpy as jnp
from jax import lax
from jax.experimental import pallas as pl
from jax.experimental.pallas import tpu as pltpu
from jax.sharding import Mesh, PartitionSpec as P

HEAD = 128
BF = jnp.bfloat16
F32 = jnp.float32
HI = lax.Precision.HIGHEST
SEQ = ("z", "y", "core")
TILE = 1024
DEC = 16
OFFS = (1, 3, 2, 0)
JREL = {0: 0, 3: 1, 1: 2, 2: 3}


VM = pl.BlockSpec(memory_space=pltpu.VMEM)
SM = pl.BlockSpec(memory_space=pltpu.SMEM)
ANY = pl.BlockSpec(memory_space=pl.ANY)
HBM = pl.BlockSpec(memory_space=pltpu.HBM)


def ring(n, k):
    return [(i, (i + k) % n) for i in range(n)]


def mm(a, b):
    return jnp.dot(a, b, preferred_element_type=F32)


def mm0(a, b):
    return lax.dot_general(a, b, (((0,), (0,)), ((), ())), preferred_element_type=F32)


def split(a):
    hi = a.astype(BF)
    return hi, (a - hi.astype(F32)).astype(BF)


def local_kernel(q_ref, k_ref, v_ref, d_ref, inner_ref, state_ref, cum_ref):
    heads, steps = d_ref.shape[1], d_ref.shape[2]
    row = lax.broadcasted_iota(jnp.int32, (steps, steps), 0)
    col = lax.broadcasted_iota(jnp.int32, (steps, steps), 1)
    later = row >= col
    upto = (row <= col).astype(F32)
    turned = jnp.dot(d_ref[0], upto, precision=HI, preferred_element_type=F32)
    cum = turned.T
    cum_ref[0] = cum
    final = cum[steps - 1 : steps, :]
    tail = jnp.exp(final - cum)
    ends = jnp.exp(final)
    piece = lax.broadcasted_iota(jnp.int32, (DEC, HEAD), 0)
    half = HEAD // 2
    for h in range(heads):
        sl = slice(h * HEAD, (h + 1) * HEAD)
        q, k, v = q_ref[0, :, sl], k_ref[0, :, sl], v_ref[0, :, sl]
        scores = lax.dot_general(q, k, (((1,), (1,)), ((), ())), preferred_element_type=F32)
        spread = cum[:, h : h + 1] - turned[h : h + 1, :]
        weights = jnp.where(later, jnp.exp(jnp.minimum(spread, 0.0)), 0.0) * scores
        whi, wlo = split(weights)
        inner_ref[0, :, sl] = mm(whi, v) + mm(wlo, v)
        khi, klo = split(k.astype(F32) * tail[:, h : h + 1])
        update = (mm0(khi, v) + mm0(klo, v)).astype(BF)
        end = jnp.broadcast_to(ends[:, h : h + 1], (DEC, HEAD))
        e1 = end.astype(BF).astype(F32)
        e2 = (end - e1).astype(BF).astype(F32)
        e3 = end - e1 - e2
        rows = jnp.where(piece == 0, e1, jnp.where(piece == 1, e2, jnp.where(piece == 2, e3, 0.0)))
        for r in range(2):
            state_ref[2 * h + r, :half, :] = update[r * half : (r + 1) * half]
            state_ref[2 * h + r, half:, :] = rows.astype(BF)


def local_part(q, k, v, d):
    seqs, steps, width = q.shape
    heads = width // HEAD
    half = HEAD // 2
    block = pl.BlockSpec((1, steps, width), lambda s: (s, 0, 0))
    thin = pl.BlockSpec((1, steps, heads), lambda s: (s, 0, 0))
    return pl.pallas_call(
        local_kernel,
        grid=(seqs,),
        in_specs=[block, block, block, pl.BlockSpec((1, heads, steps), lambda s: (s, 0, 0))],
        out_specs=[block, pl.BlockSpec((2 * heads, half + DEC, HEAD), lambda s: (s, 0, 0)), thin],
        out_shape=[
            jax.ShapeDtypeStruct((seqs, steps, width), F32),
            jax.ShapeDtypeStruct((seqs * heads * 2, half + DEC, HEAD), BF),
            jax.ShapeDtypeStruct((seqs, steps, heads), F32),
        ],
        compiler_params=pltpu.CompilerParams(vmem_limit_bytes=60 * 2**20),
        name="local_attention",
    )(q, k, v, d)


def scan_kernel(in_ref, out_ref):
    blocks = in_ref.shape[0]
    half = out_ref.shape[1]
    carry = jnp.zeros(out_ref.shape[1:], F32)
    for n in range(blocks):
        out_ref[n] = carry.astype(BF)
        dec = in_ref[n, half:, :].astype(F32)
        carry = carry * (dec[0:1] + dec[1:2] + dec[2:3]) + in_ref[n, :half, :].astype(F32)


def scan_states(arrived):
    blocks, rows, width = arrived.shape
    return pl.pallas_call(
        scan_kernel,
        out_shape=jax.ShapeDtypeStruct((blocks, rows - DEC, width), BF),
        compiler_params=pltpu.CompilerParams(vmem_limit_bytes=32 * 2**20),
        name="state_prefix",
    )(arrived)


def carry_kernel(q_ref, inner_ref, cum_ref, state_ref, gain_ref, held, out_ref, same):
    shares, slice_len = out_ref.shape[0], out_ref.shape[2]
    heads = cum_ref.shape[2]
    grow = jnp.exp(cum_ref[0])
    for h in range(heads):
        sl = slice(h * HEAD, (h + 1) * HEAD)
        head = inner_ref[0, :, sl] + mm(q_ref[0, :, sl], state_ref[h]) * grow[:, h : h + 1]
        scale = lax.rsqrt(jnp.mean(head * head, -1, keepdims=True) + 1e-06)
        normed = (head * scale * gain_ref[:, sl]).astype(BF)
        for a in range(shares):
            out_ref[a, 0, :, sl] = normed[
                a * slice_len : (a + 1) * slice_len
            ]


def carried(q, inner, cum, state, gain, shares, held):
    seqs, steps, width = q.shape
    heads = width // HEAD
    block = pl.BlockSpec((1, steps, width), lambda s: (s, 0, 0))
    return pl.pallas_call(
        carry_kernel,
        grid=(seqs,),
        in_specs=[
            block,
            block,
            pl.BlockSpec((1, steps, heads), lambda s: (s, 0, 0)),
            pl.BlockSpec((heads, HEAD, HEAD), lambda s: (s, 0, 0)),
            pl.BlockSpec((1, width), lambda s: (0, 0)),
            ANY,
        ],
        out_specs=[
            pl.BlockSpec((shares, 1, steps // shares, width), lambda s: (0, s, 0, 0)),
            ANY,
        ],
        out_shape=[
            jax.ShapeDtypeStruct((shares, seqs, steps // shares, width), BF),
            jax.ShapeDtypeStruct(held.shape, BF),
        ],
        input_output_aliases={5: 1},
        compiler_params=pltpu.CompilerParams(vmem_limit_bytes=56 * 2**20),
        name="carried_norm",
    )(q, inner, cum, state, gain, held)


def call(kernel, name, outs, *args, **kw):
    limit = kw.pop("vmem", 16)
    return pl.pallas_call(
        kernel,
        out_shape=[jax.ShapeDtypeStruct(s, d) for s, d in outs],
        compiler_params=pltpu.CompilerParams(vmem_limit_bytes=limit * 2**20),
        name=name,
        **kw,
    )(*args)


def route_kernel(cap, me_ref, r0, r1, r2, r3, place_ref, own_ref):
    homes = (r0, r1, r2, r3)
    flight, rows = len(homes), r0.shape[1]
    me = me_ref[0]
    a = lax.broadcasted_iota(jnp.int32, (rows, rows), 0)
    b = lax.broadcasted_iota(jnp.int32, (rows, rows), 1)
    before = (a < b).astype(F32).astype(BF)
    slots = lax.broadcasted_iota(jnp.int32, (flight * cap, rows), 0)
    for r, off in enumerate(OFFS):
        expert = lax.rem(me + off, flight)
        span = slice(r * flight * cap, (r + 1) * flight * cap)
        for delta, home in enumerate(homes):
            hit = (home[0:1, :] == expert) | (home[1:2, :] == expert)
            chosen = hit.astype(F32)
            rank = mm(jnp.broadcast_to(chosen, (8, rows)).astype(BF), before)[0:1]
            start = cap * JREL[(delta - off) % 4]
            target = jnp.where(chosen > 0.0, rank.astype(jnp.int32) + start, -1)
            hits = (slots == target).astype(F32).astype(BF)
            at = pl.multiple_of(lax.rem(me + delta, flight) * rows, rows)
            place_ref[span, pl.ds(at, rows)] = hits
            if delta == 0:
                own_ref[span, :] = hits


def route(me, routes, cap):
    flight, rows = len(routes), routes[0].shape[1]
    return call(
        functools.partial(route_kernel, cap),
        "route",
        [((flight * flight * cap, n), BF) for n in (flight * rows, rows)],
        me,
        *routes,
        in_specs=[SM] + [VM] * flight,
        out_specs=[VM, VM],
    )


def nt(a, b):
    return lax.dot_general(a, b, (((1,), (1,)), ((), ())), preferred_element_type=F32)


def pick_kernel(place, normed, out):
    out[...] = mm(place[...], normed[...]).astype(BF)


def selected_kernel(picked, own, weight, res, o0, o1, o2, o3, w_here, r_here, sems, last):
    size = o0.shape[0]
    chunks = weight.shape[0] // TILE

    def copy(c):
        slot = lax.rem(c, AHEAD + 1)
        span = pl.ds(pl.multiple_of(c * TILE, TILE), TILE)
        return pltpu.make_async_copy(weight.at[span], w_here.at[slot], sems.at[slot])

    rest = pltpu.make_async_copy(res, r_here, last)
    copy(0).start()
    rest.start()
    for c in range(1, AHEAD):
        copy(c).start()
    rest.wait()

    @pl.loop(0, chunks)
    def _(c):
        @pl.when(c + AHEAD < chunks)
        def _():
            copy(c + AHEAD).start()

        span = pl.ds(pl.multiple_of(c * TILE, TILE), TILE)
        copy(c).wait()
        full = nt(picked[...], w_here[lax.rem(c, AHEAD + 1)]) + mm(own[...], r_here[:, span])
        full = full.astype(BF)
        for i, o in enumerate((o0, o1, o2, o3)):
            o[:, span] = full[i * size : (i + 1) * size]


def selected(picked, own, weight, res):
    picks, (model, width) = picked.shape[0], weight.shape
    return call(
        selected_kernel,
        "selected_projection",
        [((picks // 4, model), BF)] * 4,
        picked,
        own,
        weight,
        res,
        in_specs=[VM] * 2 + [ANY] * 2,
        out_specs=[VM] * 4,
        scratch_shapes=[
            pltpu.VMEM((AHEAD + 1, TILE, width), BF),
            pltpu.VMEM(res.shape, BF),
            pltpu.SemaphoreType.DMA((AHEAD + 1,)),
            pltpu.SemaphoreType.DMA,
        ],
        vmem=48,
    )


def whole_kernel(normed_ref, weight_ref, out_ref, done_ref):
    out_ref[...] = nt(normed_ref[...], weight_ref[...]).astype(BF)
    done_ref[...] = jnp.zeros_like(done_ref)


def whole_projection(normed, weight, tile=1024):
    total, (model, width) = normed.shape[0], weight.shape
    return call(
        whole_kernel,
        "whole_projection",
        [((total, model), BF), ((8, 128), F32)],
        normed,
        weight,
        grid=(model // tile,),
        in_specs=[
            pl.BlockSpec(normed.shape, lambda n: (0, 0)),
            pl.BlockSpec((tile, width), lambda n: (n, 0)),
        ],
        out_specs=[
            pl.BlockSpec((total, tile), lambda n: (0, n)),
            pl.BlockSpec((8, 128), lambda n: (0, 0)),
        ],
        cost_estimate=pl.CostEstimate(
            flops=2 * total * model * width, bytes_accessed=4 * model * width, transcendentals=0
        ),
        vmem=58,
    )


def norm_kernel(a, b, c, d, gain, done, o0, o1):
    x = a[...].astype(F32) + b[...].astype(F32) + c[...].astype(F32) + d[...].astype(F32)
    x = x * lax.rsqrt(jnp.mean(x * x, -1, keepdims=True) + 1e-06) * gain[...]
    half = o0.shape[1]
    o0[...] = x[:, :half].astype(BF)
    o1[...] = x[:, half:].astype(BF)


def forward_kernel(a_below, b_below, a_above, b_above, a_up, b_up, a_down, b_down):
    a_up[...] = a_below[0:2]
    b_up[...] = b_below[0:2]
    a_down[...] = a_above[2:4]
    b_down[...] = b_above[2:4]


def stack_kernel(a0, b0, a3, b3, a1, b1, a2, b2, held, o0, o1, same):
    for i, (a, b) in enumerate(((a0, b0), (a1, b1), (a2, b2), (a3, b3))):
        o0[i] = a[...]
        o1[i] = b[...]


def by_y(rows, y):
    return [((z * 4 + y) * rows, z) for z in range(4)]


AHEAD = 2


class Stream:
    def __init__(self, sources, spans, buf, sems):
        self.sources, self.spans, self.buf, self.sems = sources, spans, buf, sems
        self.chunks = sources[0].shape[1] // TILE

    def copies(self, c):
        slot = lax.rem(c, AHEAD + 1)
        cols = pl.ds(pl.multiple_of(c * TILE, TILE), TILE)
        made, at = [], 0
        for i, (source, (start, size)) in enumerate(zip(self.sources, self.spans)):
            made.append(
                pltpu.make_async_copy(
                    source.at[pl.ds(start, size), cols],
                    self.buf.at[slot, pl.ds(at, size)],
                    self.sems.at[slot, i],
                )
            )
            at += size
        return made

    def start(self, c):
        for copy in self.copies(c):
            copy.start()

    def begin(self):
        for c in range(AHEAD):
            self.start(c)

    def run(self, body):
        @pl.loop(0, self.chunks)
        def _(c):
            @pl.when(c + AHEAD < self.chunks)
            def _():
                self.start(c + AHEAD)

            for copy in self.copies(c):
                copy.wait()
            body(c, self.buf[lax.rem(c, AHEAD + 1)])


def down_spans(units):
    return ((2 * units, units), (2 * units, units))


def gate_up(refs_a, refs_b, x, part_a, part_b, stream):
    rows, half = refs_a[0].shape[1:]
    each = half // TILE
    part_a[...] = jnp.zeros_like(part_a)
    part_b[...] = jnp.zeros_like(part_b)

    def body(c, weights):
        for k, (refs, part) in enumerate(((refs_a, part_a), (refs_b, part_b))):

            @pl.when(c // each == k)
            def _():
                at = pl.ds(pl.multiple_of((c - k * each) * TILE, TILE), TILE)
                row = 0
                for ref in refs:
                    for i in range(ref.shape[0]):
                        x[row : row + rows, :] = ref[i, :, at]
                        row += rows
                at = 0
                for w in weights:
                    part[:, at : at + w.shape[0]] += nt(x[...], w)
                    at += w.shape[0]

    stream.run(body)


def down_product(value, stream, outs_a, outs_b):
    rows, half = outs_a[0].shape[1:]
    each = half // TILE

    def body(c, weights):
        full = mm(value[c // each], weights).astype(BF)
        for k, outs in enumerate((outs_a, outs_b)):

            @pl.when(c // each == k)
            def _():
                at = pl.ds(pl.multiple_of((c - k * each) * TILE, TILE), TILE)
                row = 0
                for out in outs:
                    for i in range(out.shape[0]):
                        out[i, :, at] = full[row : row + rows]
                        row += rows

    stream.run(body)


class Resident:
    def __init__(self, places, sources=(), sems=None):
        self.places, self.sources, self.sems = places, sources, sems
        self.chunks = places[0].shape[1] // TILE

    def copies(self, c):
        cols = pl.ds(pl.multiple_of(c * TILE, TILE), TILE)
        return [
            pltpu.make_async_copy(ref.at[pl.ds(start, size), cols], place.at[pl.ds(at, size), cols], self.sems.at[c, i])
            for i, (ref, start, size, place, at) in enumerate(self.sources)
        ]

    def start(self, c):
        for copy in self.copies(c):
            copy.start()

    def run(self, body):
        @pl.loop(0, self.chunks)
        def _(c):
            if self.sources:

                @pl.when(c + AHEAD < self.chunks)
                def _():
                    self.start(c + AHEAD)

                for copy in self.copies(c):
                    copy.wait()
            cols = pl.ds(pl.multiple_of(c * TILE, TILE), TILE)
            body(c, [place[:, cols] for place in self.places])


def near_kernel(a0, b0, a1, b1, a2, b2, mine, other, acc, w0, w1, x, part, sems):
    rows = a0.shape[1]
    block = 4 * rows
    wide = w0.shape[0]
    stream = Resident((w0, w1), ((mine, 0, wide, w0, 0), (other, 0, wide, w1, 0)), sems)
    for c in range(AHEAD):
        stream.start(c)
    gate_up((a0, a1, a2), (b0, b1, b2), x, acc.at[pl.ds(0, 3 * block)], part, stream)
    acc[3 * block :, :] = jnp.zeros((block, acc.shape[1]), F32)
    for y in range(3):
        for row, z in by_y(rows, y):
            at = y * block + z * rows
            acc[row : row + rows, :] += part[at : at + rows, :]


def far_kernel(
    acc, a3, b3, a4, b4, w0, w1, mine, other, hidden, oa3, oa4, ob3, ob4, x, part, own, value, dbuf, dsems
):
    rows = a3.shape[1]
    block = 4 * rows
    units = mine.shape[0] // 3
    downs = Stream((mine, other), down_spans(units), dbuf, dsems)
    downs.begin()
    gate_up((a3, a4), (b3, b4), x, part.at[0], part.at[1], Resident((w0, w1)))
    own[...] = acc[...]
    own[3 * block :, :] += part[0]
    for row, z in by_y(rows, 3):
        own[row : row + rows, :] += part[1, z * rows : (z + 1) * rows, :]
    for core in range(2):
        g = own[:, 2 * core * units : (2 * core + 1) * units]
        u = own[:, (2 * core + 1) * units : (2 * core + 2) * units]
        hidden[:, core * units : (core + 1) * units] = (g / (1.0 + jnp.exp(-g)) * u).astype(BF)
    value[0] = hidden[3 * block :, :]
    for row, z in by_y(rows, 3):
        value[1, z * rows : (z + 1) * rows, :] = hidden[row : row + rows, :]
    down_product(value, downs, (oa3, oa4), (ob3, ob4))


def rest_kernel(hidden, mine, other, oa0, oa1, oa2, ob0, ob1, ob2, value, dbuf, dsems):
    rows = oa0.shape[1]
    block = 4 * rows
    downs = Stream((mine, other), down_spans(mine.shape[0] // 3), dbuf, dsems)
    downs.begin()
    value[0] = hidden[: 3 * block, :]
    for y in range(3):
        for row, z in by_y(rows, y):
            at = y * block + z * rows
            value[1, at : at + rows, :] = hidden[row : row + rows, :]
    down_product(value, downs, (oa0, oa1, oa2), (ob0, ob1, ob2))


def cost(flops):
    return pl.CostEstimate(flops=flops, bytes_accessed=2**20, transcendentals=0)


def slots(rows, parts):
    return [
        pltpu.VMEM((AHEAD + 1, rows, TILE), BF),
        pltpu.SemaphoreType.DMA((AHEAD + 1, parts)),
    ]


def near(xs, mine, other):
    rows = xs[0].shape[1]
    units, model = mine.shape[0] // 3, mine.shape[1]
    wide = 4 * units
    return call(
        near_kernel,
        "near_rows",
        [((16 * rows, wide), F32)] + [((2 * units, model), BF)] * 2,
        *xs,
        mine,
        other,
        in_specs=[VM] * 6 + [ANY] * 2,
        out_specs=[VM] * 3,
        scratch_shapes=[
            pltpu.VMEM((12 * rows, TILE), BF),
            pltpu.VMEM((12 * rows, wide), F32),
            pltpu.SemaphoreType.DMA((model // TILE, 2)),
        ],
        cost_estimate=cost(2 * 12 * rows * wide * model),
        vmem=14,
    )


def far(acc, xs, w0, w1, mine, other):
    rows, half = xs[0].shape[1:]
    wide = acc.shape[1]
    return call(
        far_kernel,
        "far_rows",
        [((16 * rows, wide // 2), BF)] + [((2, rows, half), BF)] * 4,
        acc,
        *xs,
        w0,
        w1,
        mine,
        other,
        in_specs=[VM] * 7 + [ANY] * 2,
        out_specs=[VM] * 5,
        scratch_shapes=[
            pltpu.VMEM((4 * rows, TILE), BF),
            pltpu.VMEM((2, 4 * rows, wide), F32),
            pltpu.VMEM(acc.shape, F32),
            pltpu.VMEM((2, 4 * rows, wide // 2), BF),
            *slots(wide // 2, 2),
        ],
        vmem=24,
    )


def rest(hidden, mine, other, rows):
    wide, half = hidden.shape[1], mine.shape[1] // 2
    return call(
        rest_kernel,
        "rest_rows",
        [((4, rows, half), BF)] * 6,
        hidden,
        mine,
        other,
        in_specs=[VM, ANY, ANY],
        out_specs=[VM] * 6,
        scratch_shapes=[pltpu.VMEM((2, 12 * rows, wide), BF), *slots(wide, 2)],
        cost_estimate=cost(2 * 12 * rows * wide * mine.shape[1]),
        vmem=44,
    )


def fold_kernel(bl0, ab0, bl1, ab1, up0, up1, dn0, dn1, ob0, oa0, ob1, oa1):
    for below, above, up, down, o_below, o_above in (
        (bl0, ab0, up0, dn0, ob0, oa0),
        (bl1, ab1, up1, dn1, ob1, oa1),
    ):
        o_above[0:2] = (above[0:2].astype(F32) + up[...].astype(F32)).astype(BF)
        o_above[2:4] = above[2:4]
        o_below[0:2] = below[0:2]
        o_below[2:4] = (below[2:4].astype(F32) + down[...].astype(F32)).astype(BF)


def phase_kernel(m0, m1, u0, u1, d0, d1, *outs):
    for k, (m, u, d) in enumerate(((m0, u0, d0), (m1, u1, d1))):
        total = m[...].astype(F32) + u[...].astype(F32) + d[...].astype(F32)
        for i in range(4):
            outs[4 * k + i][...] = total[i].astype(BF)


def served_kernel(cap, a0, b0, a3, b3, a1, b1, a2, b2, o0, o1, o2, o3):
    half = a0.shape[1]
    rows = a0.shape[0]
    padded = o0.shape[0]
    r = lax.broadcasted_iota(jnp.int32, (padded, rows), 0)
    c = lax.broadcasted_iota(jnp.int32, (padded, rows), 1)
    for k, parts in enumerate(((a0, a1, a2, a3), (b0, b1, b2, b3))):
        total = sum(p[...].astype(F32) for p in parts).astype(BF)
        for i, o in enumerate((o0, o1, o2, o3)):
            pick = ((c == r + i * cap) & (r < cap)).astype(F32).astype(BF)
            o[:, k * half : (k + 1) * half] = mm(pick, total).astype(BF)


def home_kernel(me_ref, routes_ref, res, mixed, gain, router, late, hidden_ref, coef_ref):
    x = res[...].astype(F32) + mixed[...].astype(F32)
    hidden_ref[...] = x
    normed = (x * lax.rsqrt(jnp.mean(x * x, -1, keepdims=True) + 1e-06) * gain[...]).astype(BF)
    logits = nt(normed, router[...])
    rows, experts = logits.shape
    labels = lax.broadcasted_iota(jnp.int32, (rows, experts), 1)
    one, two = routes_ref[:, 0:1], routes_ref[:, 1:2]
    first = jnp.sum(jnp.where(one == labels, logits, 0.0), -1, keepdims=True)
    second = jnp.sum(jnp.where(two == labels, logits, 0.0), -1, keepdims=True)
    gate0 = 1.0 / (1.0 + jnp.exp(second - first))
    gate1 = 1.0 / (1.0 + jnp.exp(first - second))
    cols = coef_ref.shape[1] // 2
    place = lax.broadcasted_iota(jnp.int32, (rows, cols), 1)
    a = lax.broadcasted_iota(jnp.int32, (rows, rows), 0)
    b = lax.broadcasted_iota(jnp.int32, (rows, rows), 1)
    before = (b < a).astype(F32).astype(BF)
    total = jnp.zeros((rows, cols), F32)
    for j, off in enumerate((0, 1, 3, 2)):
        expert_id = lax.rem(me_ref[0] + off, 4)
        hit0, hit1 = (one == expert_id).astype(F32), (two == expert_id).astype(F32)
        chosen = hit0 + hit1
        rank = mm(before, jnp.broadcast_to(chosen, (rows, 128)).astype(BF))[:, 0:1].astype(jnp.int32)
        total = total + jnp.where(place == rank + 16 * j, hit0 * gate0 + hit1 * gate1, 0.0)
    hi, lo = split(total)
    coef_ref[:, :cols] = hi
    coef_ref[:, cols:] = lo


def final_kernel(hidden, coef, b0, b1, b2, b3, out, back):
    for i, b in enumerate((b0, b1, b2, b3) * 2):
        back[16 * i : 16 * i + 16, :] = b[...]
    moe = mm(coef[...], back[...])
    out[...] = (hidden[...] + moe).astype(BF)


def up_one(x, axis):
    return lax.ppermute(x, axis, ring(4, 1))


def down_one(x, axis):
    return lax.ppermute(x, axis, ring(4, -1))


def across(x, axis):
    return lax.ppermute(x, axis, ring(4, 2))


def shards(
    queries,
    keys,
    payload_vectors,
    log_decay,
    attn_gain,
    out_weight,
    residual,
    norm_gain,
    router_weight,
    picks,
    gate_weight,
    up_weight,
    down_weight,
):
    seqs, positions, width = queries.shape
    slice_len, model = residual.shape[1], residual.shape[2]
    shares = positions // slice_len
    rows = seqs * slice_len
    cap = 3 * rows // 32
    half = model // 2
    me = lax.axis_index("x").astype(jnp.int32).reshape(1)

    weight_out = lax.all_gather(out_weight.T, SEQ, axis=0, tiled=True)
    weights = jnp.concatenate([gate_weight[0], up_weight[0], down_weight[0]])
    other = lax.ppermute(weights, "core", ring(2, 1))
    routes = picks.reshape(rows, 2)
    turned = routes.T
    all_routes = [turned] + [lax.ppermute(turned, "x", ring(4, -delta)) for delta in (1, 2, 3)]

    inner, states, cum = local_part(
        queries, keys, payload_vectors, log_decay.transpose(0, 2, 1)
    )
    arrived = lax.all_to_all(states, SEQ, 0, 0, tiled=True)
    prefix = lax.all_to_all(scan_states(arrived), SEQ, 0, 0, tiled=True)
    prefix = prefix.reshape(seqs * width // HEAD, HEAD, HEAD)
    normed, other = carried(
        queries, inner, cum, prefix, attn_gain.reshape(1, width), shares, other
    )
    normed = normed.reshape(shares * rows, width)

    place, own_place = route(me, all_routes, cap)
    flat = residual.reshape(rows, model)
    gain = norm_gain.reshape(1, model)
    picked = call(
        pick_kernel,
        "pick",
        [((place.shape[0], width), BF)],
        place,
        normed,
        in_specs=[VM] * 2,
        out_specs=[VM],
        vmem=8,
    )[0]
    to_up, to_down, to_far, here = selected(picked, own_place, weight_out, flat)
    whole, done = whole_projection(normed, weight_out)

    size = here.shape[0]
    a0, b0 = call(
        norm_kernel,
        "selected_norm",
        [((size, half), BF)] * 2,
        here,
        across(to_far, "x"),
        up_one(to_up, "x"),
        down_one(to_down, "x"),
        gain,
        done,
        in_specs=[VM] * 6,
        out_specs=[VM] * 2,
    )

    a4, b4, whole = call(
        stack_kernel,
        "stack",
        [((4, size, half), BF)] * 2 + [(whole.shape, BF)],
        a0,
        b0,
        across(a0, "y"),
        across(b0, "z"),
        up_one(a0, "y"),
        up_one(b0, "z"),
        down_one(a0, "y"),
        down_one(b0, "z"),
        whole,
        in_specs=[VM] * 8 + [ANY],
        out_specs=[VM] * 2 + [ANY],
        input_output_aliases={8: 2},
        vmem=50,
    )
    mixed = lax.psum_scatter(whole, "x", scatter_dimension=0, tiled=True)
    a_below, b_below = up_one(a4, "z"), up_one(b4, "y")
    a_above, b_above = down_one(a4, "z"), down_one(b4, "y")
    a_up, b_up, a_down, b_down = call(
        forward_kernel,
        "forward",
        [((2, size, half), BF)] * 4,
        a_below,
        b_below,
        a_above,
        b_above,
        in_specs=[VM] * 4,
        out_specs=[VM] * 4,
        vmem=8,
    )
    ends_in = (up_one(a_up, "z"), up_one(b_up, "y"), down_one(a_down, "z"), down_one(b_down, "y"))

    acc, w0, w1 = near((a4, b4, a_below, b_below, a_above, b_above), weights, other)
    hidden, *ends = far(acc, ends_in, w0, w1, weights, other)
    body = rest(hidden, weights, other, size)
    oa, ob = (*body[:3], *ends[:2]), (*body[3:], *ends[2:])
    a_below, a_above, b_below, b_above = call(
        fold_kernel,
        "fold",
        [((4, size, half), BF)] * 4,
        oa[1],
        oa[2],
        ob[1],
        ob[2],
        up_one(oa[3], "z"),
        up_one(ob[3], "y"),
        down_one(oa[4], "z"),
        down_one(ob[4], "y"),
        in_specs=[VM] * 8,
        out_specs=[VM] * 4,
        vmem=16,
    )
    parts = call(
        phase_kernel,
        "phase",
        [((size, half), BF)] * 8,
        oa[0],
        ob[0],
        up_one(a_above, "z"),
        up_one(b_above, "y"),
        down_one(a_below, "z"),
        down_one(b_below, "y"),
        in_specs=[VM] * 6,
        out_specs=[VM] * 8,
        vmem=16,
    )
    s0, s1, s2, s3 = call(
        functools.partial(served_kernel, cap),
        "served",
        [((16, model), BF)] * 4,
        parts[0],
        parts[4],
        across(parts[3], "y"),
        across(parts[7], "z"),
        up_one(parts[2], "y"),
        up_one(parts[6], "z"),
        down_one(parts[1], "y"),
        down_one(parts[5], "z"),
        in_specs=[VM] * 8,
        out_specs=[VM] * 4,
    )

    hidden, coef = call(
        home_kernel,
        "home",
        [((rows, model), F32), ((rows, 128), BF)],
        me,
        routes,
        flat,
        mixed,
        gain,
        router_weight.T,
        a_below,
        in_specs=[SM] + [VM] * 6,
        out_specs=[VM] * 2,
        vmem=20,
    )
    out = call(
        final_kernel,
        "combine",
        [((rows, model), BF)],
        hidden,
        coef,
        s0,
        down_one(s1, "x"),
        up_one(s2, "x"),
        across(s3, "x"),
        in_specs=[VM] * 6,
        out_specs=[VM],
        scratch_shapes=[pltpu.VMEM((128, model), BF)],
        vmem=16,
    )[0]
    return out.reshape(seqs, slice_len, model)


def solution(mesh):
    shape = dict(mesh.shape)
    grid = Mesh(mesh.devices.reshape(4, shape["seq"] // 8, 2, shape["exp"]), SEQ + ("x",))
    everyone = SEQ + ("x",)
    placed = (
        P(None, SEQ, "x"),
        P(None, SEQ, "x"),
        P(None, SEQ, "x"),
        P(None, SEQ, "x"),
        P("x"),
        P("x", SEQ),
        P(None, everyone, None),
        P(),
        P(),
        P(None, everyone, None),
        P("x", SEQ, None),
        P("x", SEQ, None),
        P("x", SEQ, None),
    )
    return jax.shard_map(
        shards, mesh=grid, in_specs=placed, out_specs=P(None, everyone, None), check_vma=False
    )
```

```python
import functools

import jax
import jax.numpy as jnp
from jax import lax
from jax.experimental import pallas as pl
from jax.experimental.pallas import tpu as pltpu
from jax.sharding import Mesh, PartitionSpec as P

HEAD = 128
BF = jnp.bfloat16
F32 = jnp.float32
HI = lax.Precision.HIGHEST
SEQ = ("z", "y", "core")
TILE = 1024
DEC = 16
OFFS = (1, 3, 2, 0)
JREL = {0: 0, 3: 1, 1: 2, 2: 3}


VM = pl.BlockSpec(memory_space=pltpu.VMEM)
SM = pl.BlockSpec(memory_space=pltpu.SMEM)
ANY = pl.BlockSpec(memory_space=pl.ANY)
HBM = pl.BlockSpec(memory_space=pltpu.HBM)


def ring(n, k):
    return [(i, (i + k) % n) for i in range(n)]


def mm(a, b):
    return jnp.dot(a, b, preferred_element_type=F32)


def mm0(a, b):
    return lax.dot_general(a, b, (((0,), (0,)), ((), ())), preferred_element_type=F32)


def split(a):
    hi = a.astype(BF)
    return hi, (a - hi.astype(F32)).astype(BF)


def local_kernel(q_ref, k_ref, v_ref, d_ref, inner_ref, state_ref, cum_ref):
    heads, steps = d_ref.shape[1], d_ref.shape[2]
    row = lax.broadcasted_iota(jnp.int32, (steps, steps), 0)
    col = lax.broadcasted_iota(jnp.int32, (steps, steps), 1)
    later = row >= col
    upto = (row <= col).astype(F32)
    turned = jnp.dot(d_ref[0], upto, precision=HI, preferred_element_type=F32)
    cum = turned.T
    cum_ref[0] = cum
    final = cum[steps - 1 : steps, :]
    tail = jnp.exp(final - cum)
    ends = jnp.exp(final)
    piece = lax.broadcasted_iota(jnp.int32, (DEC, HEAD), 0)
    half = HEAD // 2
    for h in range(heads):
        sl = slice(h * HEAD, (h + 1) * HEAD)
        q, k, v = q_ref[0, :, sl], k_ref[0, :, sl], v_ref[0, :, sl]
        scores = lax.dot_general(q, k, (((1,), (1,)), ((), ())), preferred_element_type=F32)
        spread = cum[:, h : h + 1] - turned[h : h + 1, :]
        weights = jnp.where(later, jnp.exp(jnp.minimum(spread, 0.0)), 0.0) * scores
        whi, wlo = split(weights)
        inner_ref[0, :, sl] = mm(whi, v) + mm(wlo, v)
        khi, klo = split(k.astype(F32) * tail[:, h : h + 1])
        update = (mm0(khi, v) + mm0(klo, v)).astype(BF)
        end = jnp.broadcast_to(ends[:, h : h + 1], (DEC, HEAD))
        e1 = end.astype(BF).astype(F32)
        e2 = (end - e1).astype(BF).astype(F32)
        e3 = end - e1 - e2
        rows = jnp.where(piece == 0, e1, jnp.where(piece == 1, e2, jnp.where(piece == 2, e3, 0.0)))
        for r in range(2):
            state_ref[2 * h + r, :half, :] = update[r * half : (r + 1) * half]
            state_ref[2 * h + r, half:, :] = rows.astype(BF)


def local_part(q, k, v, d):
    seqs, steps, width = q.shape
    heads = width // HEAD
    half = HEAD // 2
    block = pl.BlockSpec((1, steps, width), lambda s: (s, 0, 0))
    thin = pl.BlockSpec((1, steps, heads), lambda s: (s, 0, 0))
    return pl.pallas_call(
        local_kernel,
        grid=(seqs,),
        in_specs=[block, block, block, pl.BlockSpec((1, heads, steps), lambda s: (s, 0, 0))],
        out_specs=[block, pl.BlockSpec((2 * heads, half + DEC, HEAD), lambda s: (s, 0, 0)), thin],
        out_shape=[
            jax.ShapeDtypeStruct((seqs, steps, width), F32),
            jax.ShapeDtypeStruct((seqs * heads * 2, half + DEC, HEAD), BF),
            jax.ShapeDtypeStruct((seqs, steps, heads), F32),
        ],
        compiler_params=pltpu.CompilerParams(vmem_limit_bytes=60 * 2**20),
        name="local_attention",
    )(q, k, v, d)


def scan_kernel(in_ref, out_ref):
    blocks = in_ref.shape[0]
    half = out_ref.shape[1]
    carry = jnp.zeros(out_ref.shape[1:], F32)
    for n in range(blocks):
        out_ref[n] = carry.astype(BF)
        dec = in_ref[n, half:, :].astype(F32)
        carry = carry * (dec[0:1] + dec[1:2] + dec[2:3]) + in_ref[n, :half, :].astype(F32)


def scan_states(arrived):
    blocks, rows, width = arrived.shape
    return pl.pallas_call(
        scan_kernel,
        out_shape=jax.ShapeDtypeStruct((blocks, rows - DEC, width), BF),
        compiler_params=pltpu.CompilerParams(vmem_limit_bytes=32 * 2**20),
        name="state_prefix",
    )(arrived)


def carry_kernel(q_ref, inner_ref, cum_ref, state_ref, gain_ref, held, out_ref, same):
    shares, slice_len = out_ref.shape[0], out_ref.shape[2]
    heads = cum_ref.shape[2]
    grow = jnp.exp(cum_ref[0])
    for h in range(heads):
        sl = slice(h * HEAD, (h + 1) * HEAD)
        head = inner_ref[0, :, sl] + mm(q_ref[0, :, sl], state_ref[h]) * grow[:, h : h + 1]
        scale = lax.rsqrt(jnp.mean(head * head, -1, keepdims=True) + 1e-06)
        normed = (head * scale * gain_ref[:, sl]).astype(BF)
        for a in range(shares):
            out_ref[a, 0, :, sl] = normed[
                a * slice_len : (a + 1) * slice_len
            ]


def carried(q, inner, cum, state, gain, shares, held):
    seqs, steps, width = q.shape
    heads = width // HEAD
    block = pl.BlockSpec((1, steps, width), lambda s: (s, 0, 0))
    return pl.pallas_call(
        carry_kernel,
        grid=(seqs,),
        in_specs=[
            block,
            block,
            pl.BlockSpec((1, steps, heads), lambda s: (s, 0, 0)),
            pl.BlockSpec((heads, HEAD, HEAD), lambda s: (s, 0, 0)),
            pl.BlockSpec((1, width), lambda s: (0, 0)),
            ANY,
        ],
        out_specs=[
            pl.BlockSpec((shares, 1, steps // shares, width), lambda s: (0, s, 0, 0)),
            ANY,
        ],
        out_shape=[
            jax.ShapeDtypeStruct((shares, seqs, steps // shares, width), BF),
            jax.ShapeDtypeStruct(held.shape, BF),
        ],
        input_output_aliases={5: 1},
        compiler_params=pltpu.CompilerParams(vmem_limit_bytes=56 * 2**20),
        name="carried_norm",
    )(q, inner, cum, state, gain, held)


def call(kernel, name, outs, *args, **kw):
    limit = kw.pop("vmem", 16)
    return pl.pallas_call(
        kernel,
        out_shape=[jax.ShapeDtypeStruct(s, d) for s, d in outs],
        compiler_params=pltpu.CompilerParams(vmem_limit_bytes=limit * 2**20),
        name=name,
        **kw,
    )(*args)


def route_kernel(cap, me_ref, r0, r1, r2, r3, place_ref, own_ref):
    homes = (r0, r1, r2, r3)
    flight, rows = len(homes), r0.shape[1]
    me = me_ref[0]
    a = lax.broadcasted_iota(jnp.int32, (rows, rows), 0)
    b = lax.broadcasted_iota(jnp.int32, (rows, rows), 1)
    before = (a < b).astype(F32).astype(BF)
    slots = lax.broadcasted_iota(jnp.int32, (flight * cap, rows), 0)
    for r, off in enumerate(OFFS):
        expert = lax.rem(me + off, flight)
        span = slice(r * flight * cap, (r + 1) * flight * cap)
        for delta, home in enumerate(homes):
            hit = (home[0:1, :] == expert) | (home[1:2, :] == expert)
            chosen = hit.astype(F32)
            rank = mm(jnp.broadcast_to(chosen, (8, rows)).astype(BF), before)[0:1]
            start = cap * JREL[(delta - off) % 4]
            target = jnp.where(chosen > 0.0, rank.astype(jnp.int32) + start, -1)
            hits = (slots == target).astype(F32).astype(BF)
            at = pl.multiple_of(lax.rem(me + delta, flight) * rows, rows)
            place_ref[span, pl.ds(at, rows)] = hits
            if delta == 0:
                own_ref[span, :] = hits


def route(me, routes, cap):
    flight, rows = len(routes), routes[0].shape[1]
    return call(
        functools.partial(route_kernel, cap),
        "route",
        [((flight * flight * cap, n), BF) for n in (flight * rows, rows)],
        me,
        *routes,
        in_specs=[SM] + [VM] * flight,
        out_specs=[VM, VM],
    )


def nt(a, b):
    return lax.dot_general(a, b, (((1,), (1,)), ((), ())), preferred_element_type=F32)


def pick_kernel(place, normed, out):
    out[...] = mm(place[...], normed[...]).astype(BF)


def selected_kernel(first, picked, own, weight, res, o0, o1, o2, o3, w_here, r_here, sems, last):
    size, half = o0.shape
    chunks = half // TILE

    def copy(c):
        slot = lax.rem(c, AHEAD + 1)
        span = pl.ds(pl.multiple_of(first + c * TILE, TILE), TILE)
        return pltpu.make_async_copy(weight.at[span], w_here.at[slot], sems.at[slot])

    rest = pltpu.make_async_copy(res.at[:, pl.ds(first, half)], r_here, last)
    copy(0).start()
    rest.start()
    for c in range(1, AHEAD):
        copy(c).start()
    rest.wait()

    @pl.loop(0, chunks)
    def _(c):
        @pl.when(c + AHEAD < chunks)
        def _():
            copy(c + AHEAD).start()

        span = pl.ds(pl.multiple_of(c * TILE, TILE), TILE)
        copy(c).wait()
        full = nt(picked[...], w_here[lax.rem(c, AHEAD + 1)]) + mm(own[...], r_here[:, span])
        full = full.astype(BF)
        for i, o in enumerate((o0, o1, o2, o3)):
            o[:, span] = full[i * size : (i + 1) * size]


def selected(first, picked, own, weight, res):
    picks, (model, width) = picked.shape[0], weight.shape
    half = model // 2
    return call(
        functools.partial(selected_kernel, first),
        "selected_projection",
        [((picks // 4, half), BF)] * 4,
        picked,
        own,
        weight,
        res,
        in_specs=[VM] * 2 + [ANY] * 2,
        out_specs=[VM] * 4,
        scratch_shapes=[
            pltpu.VMEM((AHEAD + 1, TILE, width), BF),
            pltpu.VMEM((res.shape[0], half), BF),
            pltpu.SemaphoreType.DMA((AHEAD + 1,)),
            pltpu.SemaphoreType.DMA,
        ],
        vmem=48,
    )


def whole_kernel(normed_ref, weight_ref, out_ref, done_ref):
    out_ref[...] = nt(normed_ref[...], weight_ref[...]).astype(BF)
    done_ref[...] = jnp.zeros_like(done_ref)


def whole_projection(normed, weight, tile=1024):
    total, (model, width) = normed.shape[0], weight.shape
    return call(
        whole_kernel,
        "whole_projection",
        [((total, model), BF), ((8, 128), F32)],
        normed,
        weight,
        grid=(model // tile,),
        in_specs=[
            pl.BlockSpec(normed.shape, lambda n: (0, 0)),
            pl.BlockSpec((tile, width), lambda n: (n, 0)),
        ],
        out_specs=[
            pl.BlockSpec((total, tile), lambda n: (0, n)),
            pl.BlockSpec((8, 128), lambda n: (0, 0)),
        ],
        cost_estimate=pl.CostEstimate(
            flops=2 * total * model * width, bytes_accessed=4 * model * width, transcendentals=0
        ),
        vmem=58,
    )


def norm_kernel(*refs):
    gain, _, o0, o1 = refs[8:]
    half = o0.shape[1]
    x = [sum(r[...].astype(F32) for r in refs[4 * k : 4 * k + 4]) for k in range(2)]
    squares = sum(jnp.sum(v * v, -1, keepdims=True) for v in x)
    scale = lax.rsqrt(squares / (2 * half) + 1e-06)
    o0[...] = (x[0] * scale * gain[:, :half]).astype(BF)
    o1[...] = (x[1] * scale * gain[:, half:]).astype(BF)


def forward_kernel(a_below, b_below, a_above, b_above, a_up, b_up, a_down, b_down):
    a_up[...] = a_below[0:2]
    b_up[...] = b_below[0:2]
    a_down[...] = a_above[2:4]
    b_down[...] = b_above[2:4]


def stack_kernel(a0, b0, a3, b3, a1, b1, a2, b2, held, o0, o1, same):
    for i, (a, b) in enumerate(((a0, b0), (a1, b1), (a2, b2), (a3, b3))):
        o0[i] = a[...]
        o1[i] = b[...]


def by_y(rows, y):
    return [((z * 4 + y) * rows, z) for z in range(4)]


AHEAD = 2


class Stream:
    def __init__(self, sources, spans, buf, sems):
        self.sources, self.spans, self.buf, self.sems = sources, spans, buf, sems
        self.chunks = sources[0].shape[1] // TILE

    def copies(self, c):
        slot = lax.rem(c, AHEAD + 1)
        cols = pl.ds(pl.multiple_of(c * TILE, TILE), TILE)
        made, at = [], 0
        for i, (source, (start, size)) in enumerate(zip(self.sources, self.spans)):
            made.append(
                pltpu.make_async_copy(
                    source.at[pl.ds(start, size), cols],
                    self.buf.at[slot, pl.ds(at, size)],
                    self.sems.at[slot, i],
                )
            )
            at += size
        return made

    def start(self, c):
        for copy in self.copies(c):
            copy.start()

    def begin(self):
        for c in range(AHEAD):
            self.start(c)

    def run(self, body):
        @pl.loop(0, self.chunks)
        def _(c):
            @pl.when(c + AHEAD < self.chunks)
            def _():
                self.start(c + AHEAD)

            for copy in self.copies(c):
                copy.wait()
            body(c, self.buf[lax.rem(c, AHEAD + 1)])


def down_spans(units):
    return ((2 * units, units), (2 * units, units))


def gate_up(refs_a, refs_b, x, part_a, part_b, stream, turned=False):
    rows, half = refs_a[0].shape[1:]
    each = half // TILE
    part_a[...] = jnp.zeros_like(part_a)
    part_b[...] = jnp.zeros_like(part_b)

    def body(c, weights):
        for k, (refs, part) in enumerate(((refs_a, part_a), (refs_b, part_b))):

            @pl.when(c // each == k)
            def _():
                at = pl.ds(pl.multiple_of((c - k * each) * TILE, TILE), TILE)
                row = 0
                for ref in refs:
                    for i in range(ref.shape[0]):
                        x[row : row + rows, :] = ref[i, :, at]
                        row += rows
                at = 0
                for w in weights:
                    span = slice(at, at + w.shape[0])
                    if turned:
                        part[span, :] += nt(w, x[...])
                    else:
                        part[:, span] += nt(x[...], w)
                    at += w.shape[0]

    stream.run(body)


def down_product(value, stream, outs_a, outs_b):
    rows, half = outs_a[0].shape[1:]
    each = half // TILE

    def body(c, weights):
        full = mm(value[c // each], weights).astype(BF)
        for k, outs in enumerate((outs_a, outs_b)):

            @pl.when(c // each == k)
            def _():
                at = pl.ds(pl.multiple_of((c - k * each) * TILE, TILE), TILE)
                row = 0
                for out in outs:
                    for i in range(out.shape[0]):
                        out[i, :, at] = full[row : row + rows]
                        row += rows

    stream.run(body)


class Resident:
    def __init__(self, places, sources=(), sems=None):
        self.places, self.sources, self.sems = places, sources, sems
        self.chunks = places[0].shape[1] // TILE

    def copies(self, c):
        cols = pl.ds(pl.multiple_of(c * TILE, TILE), TILE)
        return [
            pltpu.make_async_copy(ref.at[pl.ds(start, size), cols], place.at[pl.ds(at, size), cols], self.sems.at[c, i])
            for i, (ref, start, size, place, at) in enumerate(self.sources)
        ]

    def start(self, c):
        for copy in self.copies(c):
            copy.start()

    def run(self, body):
        @pl.loop(0, self.chunks)
        def _(c):
            if self.sources:

                @pl.when(c + AHEAD < self.chunks)
                def _():
                    self.start(c + AHEAD)

                for copy in self.copies(c):
                    copy.wait()
            cols = pl.ds(pl.multiple_of(c * TILE, TILE), TILE)
            body(c, [place[:, cols] for place in self.places])


def near_kernel(a0, b0, a1, b1, a2, b2, mine, other, acc, w0, w1, x, part, sems):
    rows = a0.shape[1]
    block = 4 * rows
    wide = w0.shape[0]
    stream = Resident((w0, w1), ((mine, 0, wide, w0, 0), (other, 0, wide, w1, 0)), sems)
    for c in range(AHEAD):
        stream.start(c)
    gate_up((a0, a1, a2), (b0, b1, b2), x, acc.at[pl.ds(0, 3 * block)], part, stream)
    acc[3 * block :, :] = jnp.zeros((block, acc.shape[1]), F32)
    for y in range(3):
        for row, z in by_y(rows, y):
            at = y * block + z * rows
            acc[row : row + rows, :] += part[at : at + rows, :]


def far_kernel(
    acc, a3, b3, a4, b4, w0, w1, mine, other, hidden, oa3, oa4, ob3, ob4, x, part, own, value, dbuf, dsems
):
    rows = a3.shape[1]
    block = 4 * rows
    units = mine.shape[0] // 3
    downs = Stream((mine, other), down_spans(units), dbuf, dsems)
    downs.begin()
    gate_up((a3, a4), (b3, b4), x, part.at[0], part.at[1], Resident((w0, w1)), turned=True)
    own[...] = acc[...]
    own[3 * block :, :] += part[0].T
    across_y = part[1].T
    for row, z in by_y(rows, 3):
        own[row : row + rows, :] += across_y[z * rows : (z + 1) * rows, :]
    for core in range(2):
        g = own[:, 2 * core * units : (2 * core + 1) * units]
        u = own[:, (2 * core + 1) * units : (2 * core + 2) * units]
        hidden[:, core * units : (core + 1) * units] = (g / (1.0 + jnp.exp(-g)) * u).astype(BF)
    value[0] = hidden[3 * block :, :]
    for row, z in by_y(rows, 3):
        value[1, z * rows : (z + 1) * rows, :] = hidden[row : row + rows, :]
    down_product(value, downs, (oa3, oa4), (ob3, ob4))


def rest_kernel(hidden, mine, other, oa0, oa1, oa2, ob0, ob1, ob2, value, dbuf, dsems):
    rows = oa0.shape[1]
    block = 4 * rows
    downs = Stream((mine, other), down_spans(mine.shape[0] // 3), dbuf, dsems)
    downs.begin()
    value[0] = hidden[: 3 * block, :]
    for y in range(3):
        for row, z in by_y(rows, y):
            at = y * block + z * rows
            value[1, at : at + rows, :] = hidden[row : row + rows, :]
    down_product(value, downs, (oa0, oa1, oa2), (ob0, ob1, ob2))


def cost(flops):
    return pl.CostEstimate(flops=flops, bytes_accessed=2**20, transcendentals=0)


def slots(rows, parts):
    return [
        pltpu.VMEM((AHEAD + 1, rows, TILE), BF),
        pltpu.SemaphoreType.DMA((AHEAD + 1, parts)),
    ]


def near(xs, mine, other):
    rows = xs[0].shape[1]
    units, model = mine.shape[0] // 3, mine.shape[1]
    wide = 4 * units
    return call(
        near_kernel,
        "near_rows",
        [((16 * rows, wide), F32)] + [((2 * units, model), BF)] * 2,
        *xs,
        mine,
        other,
        in_specs=[VM] * 6 + [ANY] * 2,
        out_specs=[VM] * 3,
        scratch_shapes=[
            pltpu.VMEM((12 * rows, TILE), BF),
            pltpu.VMEM((12 * rows, wide), F32),
            pltpu.SemaphoreType.DMA((model // TILE, 2)),
        ],
        cost_estimate=cost(2 * 12 * rows * wide * model),
        vmem=14,
    )


def far(acc, xs, w0, w1, mine, other):
    rows, half = xs[0].shape[1:]
    wide = acc.shape[1]
    return call(
        far_kernel,
        "far_rows",
        [((16 * rows, wide // 2), BF)] + [((2, rows, half), BF)] * 4,
        acc,
        *xs,
        w0,
        w1,
        mine,
        other,
        in_specs=[VM] * 7 + [ANY] * 2,
        out_specs=[VM] * 5,
        scratch_shapes=[
            pltpu.VMEM((4 * rows, TILE), BF),
            pltpu.VMEM((2, wide, 4 * rows), F32),
            pltpu.VMEM(acc.shape, F32),
            pltpu.VMEM((2, 4 * rows, wide // 2), BF),
            *slots(wide // 2, 2),
        ],
        vmem=20,
    )


def rest(hidden, mine, other, rows):
    wide, half = hidden.shape[1], mine.shape[1] // 2
    return call(
        rest_kernel,
        "rest_rows",
        [((4, rows, half), BF)] * 6,
        hidden,
        mine,
        other,
        in_specs=[VM, ANY, ANY],
        out_specs=[VM] * 6,
        scratch_shapes=[pltpu.VMEM((2, 12 * rows, wide), BF), *slots(wide, 2)],
        cost_estimate=cost(2 * 12 * rows * wide * mine.shape[1]),
        vmem=44,
    )


def fold_kernel(bl0, ab0, bl1, ab1, up0, up1, dn0, dn1, ob0, oa0, ob1, oa1):
    for below, above, up, down, o_below, o_above in (
        (bl0, ab0, up0, dn0, ob0, oa0),
        (bl1, ab1, up1, dn1, ob1, oa1),
    ):
        o_above[0:2] = (above[0:2].astype(F32) + up[...].astype(F32)).astype(BF)
        o_above[2:4] = above[2:4]
        o_below[0:2] = below[0:2]
        o_below[2:4] = (below[2:4].astype(F32) + down[...].astype(F32)).astype(BF)


def phase_kernel(m0, m1, u0, u1, d0, d1, *outs):
    for k, (m, u, d) in enumerate(((m0, u0, d0), (m1, u1, d1))):
        total = m[...].astype(F32) + u[...].astype(F32) + d[...].astype(F32)
        for i in range(4):
            outs[4 * k + i][...] = total[i].astype(BF)


def served_kernel(cap, a0, b0, a3, b3, a1, b1, a2, b2, o0, o1, o2, o3):
    half = a0.shape[1]
    rows = a0.shape[0]
    padded = o0.shape[0]
    r = lax.broadcasted_iota(jnp.int32, (padded, rows), 0)
    c = lax.broadcasted_iota(jnp.int32, (padded, rows), 1)
    for k, parts in enumerate(((a0, a1, a2, a3), (b0, b1, b2, b3))):
        total = sum(p[...].astype(F32) for p in parts).astype(BF)
        for i, o in enumerate((o0, o1, o2, o3)):
            pick = ((c == r + i * cap) & (r < cap)).astype(F32).astype(BF)
            o[:, k * half : (k + 1) * half] = mm(pick, total).astype(BF)


def home_kernel(me_ref, routes_ref, res, mixed, gain, router, late, hidden_ref, coef_ref):
    x = res[...].astype(F32) + mixed[...].astype(F32)
    hidden_ref[...] = x
    normed = (x * lax.rsqrt(jnp.mean(x * x, -1, keepdims=True) + 1e-06) * gain[...]).astype(BF)
    logits = nt(normed, router[...])
    rows, experts = logits.shape
    labels = lax.broadcasted_iota(jnp.int32, (rows, experts), 1)
    one, two = routes_ref[:, 0:1], routes_ref[:, 1:2]
    first = jnp.sum(jnp.where(one == labels, logits, 0.0), -1, keepdims=True)
    second = jnp.sum(jnp.where(two == labels, logits, 0.0), -1, keepdims=True)
    gate0 = 1.0 / (1.0 + jnp.exp(second - first))
    gate1 = 1.0 / (1.0 + jnp.exp(first - second))
    cols = coef_ref.shape[1] // 2
    place = lax.broadcasted_iota(jnp.int32, (rows, cols), 1)
    a = lax.broadcasted_iota(jnp.int32, (rows, rows), 0)
    b = lax.broadcasted_iota(jnp.int32, (rows, rows), 1)
    before = (b < a).astype(F32).astype(BF)
    total = jnp.zeros((rows, cols), F32)
    for j, off in enumerate((0, 1, 3, 2)):
        expert_id = lax.rem(me_ref[0] + off, 4)
        hit0, hit1 = (one == expert_id).astype(F32), (two == expert_id).astype(F32)
        chosen = hit0 + hit1
        rank = mm(before, jnp.broadcast_to(chosen, (rows, 128)).astype(BF))[:, 0:1].astype(jnp.int32)
        total = total + jnp.where(place == rank + 16 * j, hit0 * gate0 + hit1 * gate1, 0.0)
    hi, lo = split(total)
    coef_ref[:, :cols] = hi
    coef_ref[:, cols:] = lo


def final_kernel(hidden, coef, b0, b1, b2, b3, out, back):
    for i, b in enumerate((b0, b1, b2, b3) * 2):
        back[16 * i : 16 * i + 16, :] = b[...]
    moe = mm(coef[...], back[...])
    out[...] = (hidden[...] + moe).astype(BF)


def up_one(x, axis):
    return lax.ppermute(x, axis, ring(4, 1))


def down_one(x, axis):
    return lax.ppermute(x, axis, ring(4, -1))


def across(x, axis):
    return lax.ppermute(x, axis, ring(4, 2))


def shards(
    queries,
    keys,
    payload_vectors,
    log_decay,
    attn_gain,
    out_weight,
    residual,
    norm_gain,
    router_weight,
    picks,
    gate_weight,
    up_weight,
    down_weight,
):
    seqs, positions, width = queries.shape
    slice_len, model = residual.shape[1], residual.shape[2]
    shares = positions // slice_len
    rows = seqs * slice_len
    cap = 3 * rows // 32
    half = model // 2
    me = lax.axis_index("x").astype(jnp.int32).reshape(1)

    weight_out = lax.all_gather(out_weight.T, SEQ, axis=0, tiled=True)
    weights = jnp.concatenate([gate_weight[0], up_weight[0], down_weight[0]])
    other = lax.ppermute(weights, "core", ring(2, 1))
    routes = picks.reshape(rows, 2)
    turned = routes.T
    all_routes = [turned] + [lax.ppermute(turned, "x", ring(4, -delta)) for delta in (1, 2, 3)]

    inner, states, cum = local_part(
        queries, keys, payload_vectors, log_decay.transpose(0, 2, 1)
    )
    arrived = lax.all_to_all(states, SEQ, 0, 0, tiled=True)
    prefix = lax.all_to_all(scan_states(arrived), SEQ, 0, 0, tiled=True)
    prefix = prefix.reshape(seqs * width // HEAD, HEAD, HEAD)
    normed, other = carried(
        queries, inner, cum, prefix, attn_gain.reshape(1, width), shares, other
    )
    normed = normed.reshape(shares * rows, width)

    place, own_place = route(me, all_routes, cap)
    flat = residual.reshape(rows, model)
    gain = norm_gain.reshape(1, model)
    picked = call(
        pick_kernel,
        "pick",
        [((place.shape[0], width), BF)],
        place,
        normed,
        in_specs=[VM] * 2,
        out_specs=[VM],
        vmem=8,
    )[0]
    terms = []
    for first in (0, half):
        to_up, to_down, to_far, here = selected(first, picked, own_place, weight_out, flat)
        terms += [here, across(to_far, "x"), up_one(to_up, "x"), down_one(to_down, "x")]
    whole, done = whole_projection(normed, weight_out)

    size = terms[0].shape[0]
    a0, b0 = call(
        norm_kernel,
        "selected_norm",
        [((size, half), BF)] * 2,
        *terms,
        gain,
        done,
        in_specs=[VM] * 10,
        out_specs=[VM] * 2,
    )

    a4, b4, whole = call(
        stack_kernel,
        "stack",
        [((4, size, half), BF)] * 2 + [(whole.shape, BF)],
        a0,
        b0,
        across(a0, "y"),
        across(b0, "z"),
        up_one(a0, "y"),
        up_one(b0, "z"),
        down_one(a0, "y"),
        down_one(b0, "z"),
        whole,
        in_specs=[VM] * 8 + [ANY],
        out_specs=[VM] * 2 + [ANY],
        input_output_aliases={8: 2},
        vmem=50,
    )
    mixed = lax.psum_scatter(whole, "x", scatter_dimension=0, tiled=True)
    a_below, b_below = up_one(a4, "z"), up_one(b4, "y")
    a_above, b_above = down_one(a4, "z"), down_one(b4, "y")
    a_up, b_up, a_down, b_down = call(
        forward_kernel,
        "forward",
        [((2, size, half), BF)] * 4,
        a_below,
        b_below,
        a_above,
        b_above,
        in_specs=[VM] * 4,
        out_specs=[VM] * 4,
        vmem=8,
    )
    ends_in = (up_one(a_up, "z"), up_one(b_up, "y"), down_one(a_down, "z"), down_one(b_down, "y"))

    acc, w0, w1 = near((a4, b4, a_below, b_below, a_above, b_above), weights, other)
    hidden, *ends = far(acc, ends_in, w0, w1, weights, other)
    body = rest(hidden, weights, other, size)
    oa, ob = (*body[:3], *ends[:2]), (*body[3:], *ends[2:])
    a_below, a_above, b_below, b_above = call(
        fold_kernel,
        "fold",
        [((4, size, half), BF)] * 4,
        oa[1],
        oa[2],
        ob[1],
        ob[2],
        up_one(oa[3], "z"),
        up_one(ob[3], "y"),
        down_one(oa[4], "z"),
        down_one(ob[4], "y"),
        in_specs=[VM] * 8,
        out_specs=[VM] * 4,
        vmem=16,
    )
    parts = call(
        phase_kernel,
        "phase",
        [((size, half), BF)] * 8,
        oa[0],
        ob[0],
        up_one(a_above, "z"),
        up_one(b_above, "y"),
        down_one(a_below, "z"),
        down_one(b_below, "y"),
        in_specs=[VM] * 6,
        out_specs=[VM] * 8,
        vmem=16,
    )
    s0, s1, s2, s3 = call(
        functools.partial(served_kernel, cap),
        "served",
        [((16, model), BF)] * 4,
        parts[0],
        parts[4],
        across(parts[3], "y"),
        across(parts[7], "z"),
        up_one(parts[2], "y"),
        up_one(parts[6], "z"),
        down_one(parts[1], "y"),
        down_one(parts[5], "z"),
        in_specs=[VM] * 8,
        out_specs=[VM] * 4,
    )

    hidden, coef = call(
        home_kernel,
        "home",
        [((rows, model), F32), ((rows, 128), BF)],
        me,
        routes,
        flat,
        mixed,
        gain,
        router_weight.T,
        a_below,
        in_specs=[SM] + [VM] * 6,
        out_specs=[VM] * 2,
        vmem=20,
    )
    out = call(
        final_kernel,
        "combine",
        [((rows, model), BF)],
        hidden,
        coef,
        s0,
        down_one(s1, "x"),
        up_one(s2, "x"),
        across(s3, "x"),
        in_specs=[VM] * 6,
        out_specs=[VM],
        scratch_shapes=[pltpu.VMEM((128, model), BF)],
        vmem=16,
    )[0]
    return out.reshape(seqs, slice_len, model)


def solution(mesh):
    shape = dict(mesh.shape)
    grid = Mesh(mesh.devices.reshape(4, shape["seq"] // 8, 2, shape["exp"]), SEQ + ("x",))
    everyone = SEQ + ("x",)
    placed = (
        P(None, SEQ, "x"),
        P(None, SEQ, "x"),
        P(None, SEQ, "x"),
        P(None, SEQ, "x"),
        P("x"),
        P("x", SEQ),
        P(None, everyone, None),
        P(),
        P(),
        P(None, everyone, None),
        P("x", SEQ, None),
        P("x", SEQ, None),
        P("x", SEQ, None),
    )
    return jax.shard_map(
        shards, mesh=grid, in_specs=placed, out_specs=P(None, everyone, None), check_vma=False
    )
```

```python
import functools

import jax
import jax.numpy as jnp
from jax import lax
from jax.experimental import pallas as pl
from jax.experimental.pallas import tpu as pltpu
from jax.sharding import Mesh, PartitionSpec as P

HEAD = 128
BF = jnp.bfloat16
F32 = jnp.float32
HI = lax.Precision.HIGHEST
SEQ = ("z", "y", "core")
TILE = 1024
DEC = 16
OFFS = (1, 3, 2, 0)
JREL = {0: 0, 3: 1, 1: 2, 2: 3}


VM = pl.BlockSpec(memory_space=pltpu.VMEM)
SM = pl.BlockSpec(memory_space=pltpu.SMEM)
ANY = pl.BlockSpec(memory_space=pl.ANY)
HBM = pl.BlockSpec(memory_space=pltpu.HBM)


def ring(n, k):
    return [(i, (i + k) % n) for i in range(n)]


def mm(a, b):
    return jnp.dot(a, b, preferred_element_type=F32)


def mm0(a, b):
    return lax.dot_general(a, b, (((0,), (0,)), ((), ())), preferred_element_type=F32)


def split(a):
    hi = a.astype(BF)
    return hi, (a - hi.astype(F32)).astype(BF)


def local_kernel(q_ref, k_ref, v_ref, d_ref, inner_ref, state_ref, cum_ref):
    heads, steps = d_ref.shape[1], d_ref.shape[2]
    row = lax.broadcasted_iota(jnp.int32, (steps, steps), 0)
    col = lax.broadcasted_iota(jnp.int32, (steps, steps), 1)
    later = row >= col
    upto = (row <= col).astype(F32)
    turned = jnp.dot(d_ref[0], upto, precision=HI, preferred_element_type=F32)
    cum = turned.T
    cum_ref[0] = cum
    final = cum[steps - 1 : steps, :]
    tail = jnp.exp(final - cum)
    ends = jnp.exp(final)
    piece = lax.broadcasted_iota(jnp.int32, (DEC, HEAD), 0)
    half = HEAD // 2
    for h in range(heads):
        sl = slice(h * HEAD, (h + 1) * HEAD)
        q, k, v = q_ref[0, :, sl], k_ref[0, :, sl], v_ref[0, :, sl]
        scores = lax.dot_general(q, k, (((1,), (1,)), ((), ())), preferred_element_type=F32)
        spread = cum[:, h : h + 1] - turned[h : h + 1, :]
        weights = jnp.where(later, jnp.exp(jnp.minimum(spread, 0.0)), 0.0) * scores
        whi, wlo = split(weights)
        inner_ref[0, :, sl] = mm(whi, v) + mm(wlo, v)
        khi, klo = split(k.astype(F32) * tail[:, h : h + 1])
        update = (mm0(khi, v) + mm0(klo, v)).astype(BF)
        end = jnp.broadcast_to(ends[:, h : h + 1], (DEC, HEAD))
        e1 = end.astype(BF).astype(F32)
        e2 = (end - e1).astype(BF).astype(F32)
        e3 = end - e1 - e2
        rows = jnp.where(piece == 0, e1, jnp.where(piece == 1, e2, jnp.where(piece == 2, e3, 0.0)))
        for r in range(2):
            state_ref[2 * h + r, :half, :] = update[r * half : (r + 1) * half]
            state_ref[2 * h + r, half:, :] = rows.astype(BF)


def local_part(q, k, v, d):
    seqs, steps, width = q.shape
    heads = width // HEAD
    half = HEAD // 2
    block = pl.BlockSpec((1, steps, width), lambda s: (s, 0, 0))
    thin = pl.BlockSpec((1, steps, heads), lambda s: (s, 0, 0))
    return pl.pallas_call(
        local_kernel,
        grid=(seqs,),
        in_specs=[block, block, block, pl.BlockSpec((1, heads, steps), lambda s: (s, 0, 0))],
        out_specs=[block, pl.BlockSpec((2 * heads, half + DEC, HEAD), lambda s: (s, 0, 0)), thin],
        out_shape=[
            jax.ShapeDtypeStruct((seqs, steps, width), F32),
            jax.ShapeDtypeStruct((seqs * heads * 2, half + DEC, HEAD), BF),
            jax.ShapeDtypeStruct((seqs, steps, heads), F32),
        ],
        compiler_params=pltpu.CompilerParams(vmem_limit_bytes=60 * 2**20),
        name="local_attention",
    )(q, k, v, d)


def scan_kernel(in_ref, out_ref):
    blocks = in_ref.shape[0]
    half = out_ref.shape[1]
    carry = jnp.zeros(out_ref.shape[1:], F32)
    for n in range(blocks):
        out_ref[n] = carry.astype(BF)
        dec = in_ref[n, half:, :].astype(F32)
        carry = carry * (dec[0:1] + dec[1:2] + dec[2:3]) + in_ref[n, :half, :].astype(F32)


def scan_states(arrived):
    blocks, rows, width = arrived.shape
    return pl.pallas_call(
        scan_kernel,
        out_shape=jax.ShapeDtypeStruct((blocks, rows - DEC, width), BF),
        compiler_params=pltpu.CompilerParams(vmem_limit_bytes=32 * 2**20),
        name="state_prefix",
    )(arrived)


def carry_kernel(q_ref, inner_ref, cum_ref, state_ref, gain_ref, held, out_ref, same):
    shares, slice_len = out_ref.shape[0], out_ref.shape[2]
    heads = cum_ref.shape[2]
    grow = jnp.exp(cum_ref[0])
    for h in range(heads):
        sl = slice(h * HEAD, (h + 1) * HEAD)
        head = inner_ref[0, :, sl] + mm(q_ref[0, :, sl], state_ref[h]) * grow[:, h : h + 1]
        scale = lax.rsqrt(jnp.mean(head * head, -1, keepdims=True) + 1e-06)
        normed = (head * scale * gain_ref[:, sl]).astype(BF)
        for a in range(shares):
            out_ref[a, 0, :, sl] = normed[
                a * slice_len : (a + 1) * slice_len
            ]


def carried(q, inner, cum, state, gain, shares, held):
    seqs, steps, width = q.shape
    heads = width // HEAD
    block = pl.BlockSpec((1, steps, width), lambda s: (s, 0, 0))
    return pl.pallas_call(
        carry_kernel,
        grid=(seqs,),
        in_specs=[
            block,
            block,
            pl.BlockSpec((1, steps, heads), lambda s: (s, 0, 0)),
            pl.BlockSpec((heads, HEAD, HEAD), lambda s: (s, 0, 0)),
            pl.BlockSpec((1, width), lambda s: (0, 0)),
            ANY,
        ],
        out_specs=[
            pl.BlockSpec((shares, 1, steps // shares, width), lambda s: (0, s, 0, 0)),
            ANY,
        ],
        out_shape=[
            jax.ShapeDtypeStruct((shares, seqs, steps // shares, width), BF),
            jax.ShapeDtypeStruct(held.shape, BF),
        ],
        input_output_aliases={5: 1},
        compiler_params=pltpu.CompilerParams(vmem_limit_bytes=56 * 2**20),
        name="carried_norm",
    )(q, inner, cum, state, gain, held)


def call(kernel, name, outs, *args, **kw):
    limit = kw.pop("vmem", 16)
    return pl.pallas_call(
        kernel,
        out_shape=[jax.ShapeDtypeStruct(s, d) for s, d in outs],
        compiler_params=pltpu.CompilerParams(vmem_limit_bytes=limit * 2**20),
        name=name,
        **kw,
    )(*args)


def route_kernel(cap, me_ref, r0, r1, r2, r3, place_ref, own_ref):
    homes = (r0, r1, r2, r3)
    flight, rows = len(homes), r0.shape[1]
    me = me_ref[0]
    a = lax.broadcasted_iota(jnp.int32, (rows, rows), 0)
    b = lax.broadcasted_iota(jnp.int32, (rows, rows), 1)
    before = (a < b).astype(F32).astype(BF)
    slots = lax.broadcasted_iota(jnp.int32, (flight * cap, rows), 0)
    for r, off in enumerate(OFFS):
        expert = lax.rem(me + off, flight)
        span = slice(r * flight * cap, (r + 1) * flight * cap)
        for delta, home in enumerate(homes):
            hit = (home[0:1, :] == expert) | (home[1:2, :] == expert)
            chosen = hit.astype(F32)
            rank = mm(jnp.broadcast_to(chosen, (8, rows)).astype(BF), before)[0:1]
            start = cap * JREL[(delta - off) % 4]
            target = jnp.where(chosen > 0.0, rank.astype(jnp.int32) + start, -1)
            hits = (slots == target).astype(F32).astype(BF)
            at = pl.multiple_of(lax.rem(me + delta, flight) * rows, rows)
            place_ref[span, pl.ds(at, rows)] = hits
            if delta == 0:
                own_ref[span, :] = hits


def route(me, routes, cap):
    flight, rows = len(routes), routes[0].shape[1]
    return call(
        functools.partial(route_kernel, cap),
        "route",
        [((flight * flight * cap, n), BF) for n in (flight * rows, rows)],
        me,
        *routes,
        in_specs=[SM] + [VM] * flight,
        out_specs=[VM, VM],
    )


def nt(a, b):
    return lax.dot_general(a, b, (((1,), (1,)), ((), ())), preferred_element_type=F32)


def pick_kernel(place, normed, out):
    out[...] = mm(place[...], normed[...]).astype(BF)


def selected_kernel(first, picked, own, weight, res, o0, o1, o2, o3, w_here, r_here, sems, last):
    size, half = o0.shape
    chunks = half // TILE

    def copy(c):
        slot = lax.rem(c, AHEAD + 1)
        span = pl.ds(pl.multiple_of(first + c * TILE, TILE), TILE)
        return pltpu.make_async_copy(weight.at[span], w_here.at[slot], sems.at[slot])

    rest = pltpu.make_async_copy(res.at[:, pl.ds(first, half)], r_here, last)
    copy(0).start()
    rest.start()
    for c in range(1, AHEAD):
        copy(c).start()
    rest.wait()

    @pl.loop(0, chunks)
    def _(c):
        @pl.when(c + AHEAD < chunks)
        def _():
            copy(c + AHEAD).start()

        span = pl.ds(pl.multiple_of(c * TILE, TILE), TILE)
        copy(c).wait()
        full = nt(picked[...], w_here[lax.rem(c, AHEAD + 1)]) + mm(own[...], r_here[:, span])
        full = full.astype(BF)
        for i, o in enumerate((o0, o1, o2, o3)):
            o[:, span] = full[i * size : (i + 1) * size]


def selected(first, picked, own, weight, res):
    picks, (model, width) = picked.shape[0], weight.shape
    half = model // 2
    return call(
        functools.partial(selected_kernel, first),
        "selected_projection",
        [((picks // 4, half), BF)] * 4,
        picked,
        own,
        weight,
        res,
        in_specs=[VM] * 2 + [ANY] * 2,
        out_specs=[VM] * 4,
        scratch_shapes=[
            pltpu.VMEM((AHEAD + 1, TILE, width), BF),
            pltpu.VMEM((res.shape[0], half), BF),
            pltpu.SemaphoreType.DMA((AHEAD + 1,)),
            pltpu.SemaphoreType.DMA,
        ],
        vmem=48,
    )


def whole_kernel(normed_ref, weight_ref, out_ref, done_ref):
    out_ref[...] = nt(normed_ref[...], weight_ref[...]).astype(BF)
    done_ref[...] = jnp.zeros_like(done_ref)


def whole_projection(normed, weight, tile=1024):
    total, (model, width) = normed.shape[0], weight.shape
    return call(
        whole_kernel,
        "whole_projection",
        [((total, model), BF), ((8, 128), F32)],
        normed,
        weight,
        grid=(model // tile,),
        in_specs=[
            pl.BlockSpec(normed.shape, lambda n: (0, 0)),
            pl.BlockSpec((tile, width), lambda n: (n, 0)),
        ],
        out_specs=[
            pl.BlockSpec((total, tile), lambda n: (0, n)),
            pl.BlockSpec((8, 128), lambda n: (0, 0)),
        ],
        cost_estimate=pl.CostEstimate(
            flops=2 * total * model * width, bytes_accessed=4 * model * width, transcendentals=0
        ),
        vmem=58,
    )


def norm_kernel(*refs):
    gain, _, _, o0, o1, _ = refs[8:]
    half = o0.shape[1]
    x = [sum(r[...].astype(F32) for r in refs[4 * k : 4 * k + 4]) for k in range(2)]
    squares = sum(jnp.sum(v * v, -1, keepdims=True) for v in x)
    scale = lax.rsqrt(squares / (2 * half) + 1e-06)
    o0[...] = (x[0] * scale * gain[:, :half]).astype(BF)
    o1[...] = (x[1] * scale * gain[:, half:]).astype(BF)


def forward_kernel(a_below, b_below, a_above, b_above, a_up, b_up, a_down, b_down):
    a_up[...] = a_below[0:2]
    b_up[...] = b_below[0:2]
    a_down[...] = a_above[2:4]
    b_down[...] = b_above[2:4]


def stack_kernel(a0, b0, a3, b3, a1, b1, a2, b2, o0, o1):
    for i, (a, b) in enumerate(((a0, b0), (a1, b1), (a2, b2), (a3, b3))):
        o0[i] = a[...]
        o1[i] = b[...]


def by_y(rows, y):
    return [((z * 4 + y) * rows, z) for z in range(4)]


AHEAD = 2


class Stream:
    def __init__(self, sources, spans, buf, sems):
        self.sources, self.spans, self.buf, self.sems = sources, spans, buf, sems
        self.chunks = sources[0].shape[1] // TILE

    def copies(self, c):
        slot = lax.rem(c, AHEAD + 1)
        cols = pl.ds(pl.multiple_of(c * TILE, TILE), TILE)
        made, at = [], 0
        for i, (source, (start, size)) in enumerate(zip(self.sources, self.spans)):
            made.append(
                pltpu.make_async_copy(
                    source.at[pl.ds(start, size), cols],
                    self.buf.at[slot, pl.ds(at, size)],
                    self.sems.at[slot, i],
                )
            )
            at += size
        return made

    def start(self, c):
        for copy in self.copies(c):
            copy.start()

    def begin(self):
        for c in range(AHEAD):
            self.start(c)

    def run(self, body):
        @pl.loop(0, self.chunks)
        def _(c):
            @pl.when(c + AHEAD < self.chunks)
            def _():
                self.start(c + AHEAD)

            for copy in self.copies(c):
                copy.wait()
            body(c, self.buf[lax.rem(c, AHEAD + 1)])


def down_spans(units):
    return ((2 * units, units), (2 * units, units))


def gate_up(refs_a, refs_b, x, part_a, part_b, stream, turned=False):
    rows, half = refs_a[0].shape[1:]
    each = half // TILE
    part_a[...] = jnp.zeros_like(part_a)
    part_b[...] = jnp.zeros_like(part_b)

    def body(c, weights):
        for k, (refs, part) in enumerate(((refs_a, part_a), (refs_b, part_b))):

            @pl.when(c // each == k)
            def _():
                at = pl.ds(pl.multiple_of((c - k * each) * TILE, TILE), TILE)
                row = 0
                for ref in refs:
                    for i in range(ref.shape[0]):
                        x[row : row + rows, :] = ref[i, :, at]
                        row += rows
                at = 0
                for w in weights:
                    span = slice(at, at + w.shape[0])
                    if turned:
                        part[span, :] += nt(w, x[...])
                    else:
                        part[:, span] += nt(x[...], w)
                    at += w.shape[0]

    stream.run(body)


def down_product(value, stream, outs_a, outs_b):
    rows, half = outs_a[0].shape[1:]
    each = half // TILE

    def body(c, weights):
        full = mm(value[c // each], weights).astype(BF)
        for k, outs in enumerate((outs_a, outs_b)):

            @pl.when(c // each == k)
            def _():
                at = pl.ds(pl.multiple_of((c - k * each) * TILE, TILE), TILE)
                row = 0
                for out in outs:
                    for i in range(out.shape[0]):
                        out[i, :, at] = full[row : row + rows]
                        row += rows

    stream.run(body)


class Resident:
    def __init__(self, places, sources=(), sems=None):
        self.places, self.sources, self.sems = places, sources, sems
        self.chunks = places[0].shape[1] // TILE

    def copies(self, c):
        cols = pl.ds(pl.multiple_of(c * TILE, TILE), TILE)
        return [
            pltpu.make_async_copy(ref.at[pl.ds(start, size), cols], place.at[pl.ds(at, size), cols], self.sems.at[c, i])
            for i, (ref, start, size, place, at) in enumerate(self.sources)
        ]

    def start(self, c):
        for copy in self.copies(c):
            copy.start()

    def run(self, body):
        @pl.loop(0, self.chunks)
        def _(c):
            if self.sources:

                @pl.when(c + AHEAD < self.chunks)
                def _():
                    self.start(c + AHEAD)

                for copy in self.copies(c):
                    copy.wait()
            cols = pl.ds(pl.multiple_of(c * TILE, TILE), TILE)
            body(c, [place[:, cols] for place in self.places])


def near_kernel(a0, b0, a1, b1, a2, b2, mine, other, acc, w0, w1, x, part, sems):
    rows = a0.shape[1]
    block = 4 * rows
    wide = w0.shape[0]
    stream = Resident((w0, w1), ((mine, 0, wide, w0, 0), (other, 0, wide, w1, 0)), sems)
    for c in range(AHEAD):
        stream.start(c)
    gate_up((a0, a1, a2), (b0, b1, b2), x, acc.at[pl.ds(0, 3 * block)], part, stream)
    acc[3 * block :, :] = jnp.zeros((block, acc.shape[1]), F32)
    for y in range(3):
        for row, z in by_y(rows, y):
            at = y * block + z * rows
            acc[row : row + rows, :] += part[at : at + rows, :]


def far_kernel(
    acc, a3, b3, a4, b4, w0, w1, mine, other, hidden, oa3, oa4, ob3, ob4, x, part, own, value, dbuf, dsems
):
    rows = a3.shape[1]
    block = 4 * rows
    units = mine.shape[0] // 3
    downs = Stream((mine, other), down_spans(units), dbuf, dsems)
    downs.begin()
    gate_up((a3, a4), (b3, b4), x, part.at[0], part.at[1], Resident((w0, w1)), turned=True)
    own[...] = acc[...]
    own[3 * block :, :] += part[0].T
    across_y = part[1].T
    for row, z in by_y(rows, 3):
        own[row : row + rows, :] += across_y[z * rows : (z + 1) * rows, :]
    for core in range(2):
        g = own[:, 2 * core * units : (2 * core + 1) * units]
        u = own[:, (2 * core + 1) * units : (2 * core + 2) * units]
        hidden[:, core * units : (core + 1) * units] = (g / (1.0 + jnp.exp(-g)) * u).astype(BF)
    value[0] = hidden[3 * block :, :]
    for row, z in by_y(rows, 3):
        value[1, z * rows : (z + 1) * rows, :] = hidden[row : row + rows, :]
    down_product(value, downs, (oa3, oa4), (ob3, ob4))


def rest_kernel(hidden, mine, other, oa0, oa1, oa2, ob0, ob1, ob2, value, dbuf, dsems):
    rows = oa0.shape[1]
    block = 4 * rows
    downs = Stream((mine, other), down_spans(mine.shape[0] // 3), dbuf, dsems)
    downs.begin()
    value[0] = hidden[: 3 * block, :]
    for y in range(3):
        for row, z in by_y(rows, y):
            at = y * block + z * rows
            value[1, at : at + rows, :] = hidden[row : row + rows, :]
    down_product(value, downs, (oa0, oa1, oa2), (ob0, ob1, ob2))


def cost(flops):
    return pl.CostEstimate(flops=flops, bytes_accessed=2**20, transcendentals=0)


def slots(rows, parts):
    return [
        pltpu.VMEM((AHEAD + 1, rows, TILE), BF),
        pltpu.SemaphoreType.DMA((AHEAD + 1, parts)),
    ]


def near(xs, mine, other):
    rows = xs[0].shape[1]
    units, model = mine.shape[0] // 3, mine.shape[1]
    wide = 4 * units
    return call(
        near_kernel,
        "near_rows",
        [((16 * rows, wide), F32)] + [((2 * units, model), BF)] * 2,
        *xs,
        mine,
        other,
        in_specs=[VM] * 6 + [ANY] * 2,
        out_specs=[VM] * 3,
        scratch_shapes=[
            pltpu.VMEM((12 * rows, TILE), BF),
            pltpu.VMEM((12 * rows, wide), F32),
            pltpu.SemaphoreType.DMA((model // TILE, 2)),
        ],
        cost_estimate=cost(2 * 12 * rows * wide * model),
        vmem=14,
    )


def far(acc, xs, w0, w1, mine, other):
    rows, half = xs[0].shape[1:]
    wide = acc.shape[1]
    return call(
        far_kernel,
        "far_rows",
        [((16 * rows, wide // 2), BF)] + [((2, rows, half), BF)] * 4,
        acc,
        *xs,
        w0,
        w1,
        mine,
        other,
        in_specs=[VM] * 7 + [ANY] * 2,
        out_specs=[VM] * 5,
        scratch_shapes=[
            pltpu.VMEM((4 * rows, TILE), BF),
            pltpu.VMEM((2, wide, 4 * rows), F32),
            pltpu.VMEM(acc.shape, F32),
            pltpu.VMEM((2, 4 * rows, wide // 2), BF),
            *slots(wide // 2, 2),
        ],
        vmem=20,
    )


def rest(hidden, mine, other, rows):
    wide, half = hidden.shape[1], mine.shape[1] // 2
    return call(
        rest_kernel,
        "rest_rows",
        [((4, rows, half), BF)] * 6,
        hidden,
        mine,
        other,
        in_specs=[VM, ANY, ANY],
        out_specs=[VM] * 6,
        scratch_shapes=[pltpu.VMEM((2, 12 * rows, wide), BF), *slots(wide, 2)],
        cost_estimate=cost(2 * 12 * rows * wide * mine.shape[1]),
        vmem=44,
    )


def fold_kernel(bl0, ab0, bl1, ab1, up0, up1, dn0, dn1, ob0, oa0, ob1, oa1):
    for below, above, up, down, o_below, o_above in (
        (bl0, ab0, up0, dn0, ob0, oa0),
        (bl1, ab1, up1, dn1, ob1, oa1),
    ):
        o_above[0:2] = (above[0:2].astype(F32) + up[...].astype(F32)).astype(BF)
        o_above[2:4] = above[2:4]
        o_below[0:2] = below[0:2]
        o_below[2:4] = (below[2:4].astype(F32) + down[...].astype(F32)).astype(BF)


def phase_kernel(m0, m1, u0, u1, d0, d1, *outs):
    for k, (m, u, d) in enumerate(((m0, u0, d0), (m1, u1, d1))):
        total = m[...].astype(F32) + u[...].astype(F32) + d[...].astype(F32)
        for i in range(4):
            outs[4 * k + i][...] = total[i].astype(BF)


def served_kernel(cap, a0, b0, a3, b3, a1, b1, a2, b2, o0, o1, o2, o3):
    half = a0.shape[1]
    rows = a0.shape[0]
    padded = o0.shape[0]
    r = lax.broadcasted_iota(jnp.int32, (padded, rows), 0)
    c = lax.broadcasted_iota(jnp.int32, (padded, rows), 1)
    for k, parts in enumerate(((a0, a1, a2, a3), (b0, b1, b2, b3))):
        total = sum(p[...].astype(F32) for p in parts).astype(BF)
        for i, o in enumerate((o0, o1, o2, o3)):
            pick = ((c == r + i * cap) & (r < cap)).astype(F32).astype(BF)
            o[:, k * half : (k + 1) * half] = mm(pick, total).astype(BF)


def home_kernel(me_ref, routes_ref, res, mixed, gain, router, late, hidden_ref, coef_ref):
    x = res[...].astype(F32) + mixed[...].astype(F32)
    hidden_ref[...] = x
    normed = (x * lax.rsqrt(jnp.mean(x * x, -1, keepdims=True) + 1e-06) * gain[...]).astype(BF)
    logits = nt(normed, router[...])
    rows, experts = logits.shape
    labels = lax.broadcasted_iota(jnp.int32, (rows, experts), 1)
    one, two = routes_ref[:, 0:1], routes_ref[:, 1:2]
    first = jnp.sum(jnp.where(one == labels, logits, 0.0), -1, keepdims=True)
    second = jnp.sum(jnp.where(two == labels, logits, 0.0), -1, keepdims=True)
    gate0 = 1.0 / (1.0 + jnp.exp(second - first))
    gate1 = 1.0 / (1.0 + jnp.exp(first - second))
    cols = coef_ref.shape[1] // 2
    place = lax.broadcasted_iota(jnp.int32, (rows, cols), 1)
    a = lax.broadcasted_iota(jnp.int32, (rows, rows), 0)
    b = lax.broadcasted_iota(jnp.int32, (rows, rows), 1)
    before = (b < a).astype(F32).astype(BF)
    total = jnp.zeros((rows, cols), F32)
    for j, off in enumerate((0, 1, 3, 2)):
        expert_id = lax.rem(me_ref[0] + off, 4)
        hit0, hit1 = (one == expert_id).astype(F32), (two == expert_id).astype(F32)
        chosen = hit0 + hit1
        rank = mm(before, jnp.broadcast_to(chosen, (rows, 128)).astype(BF))[:, 0:1].astype(jnp.int32)
        total = total + jnp.where(place == rank + 16 * j, hit0 * gate0 + hit1 * gate1, 0.0)
    hi, lo = split(total)
    coef_ref[:, :cols] = hi
    coef_ref[:, cols:] = lo


def final_kernel(hidden, coef, b0, b1, b2, b3, out, back):
    for i, b in enumerate((b0, b1, b2, b3) * 2):
        back[16 * i : 16 * i + 16, :] = b[...]
    moe = mm(coef[...], back[...])
    out[...] = (hidden[...] + moe).astype(BF)


def up_one(x, axis):
    return lax.ppermute(x, axis, ring(4, 1))


def down_one(x, axis):
    return lax.ppermute(x, axis, ring(4, -1))


def across(x, axis):
    return lax.ppermute(x, axis, ring(4, 2))


def shards(
    queries,
    keys,
    payload_vectors,
    log_decay,
    attn_gain,
    out_weight,
    residual,
    norm_gain,
    router_weight,
    picks,
    gate_weight,
    up_weight,
    down_weight,
):
    seqs, positions, width = queries.shape
    slice_len, model = residual.shape[1], residual.shape[2]
    shares = positions // slice_len
    rows = seqs * slice_len
    cap = 3 * rows // 32
    half = model // 2
    me = lax.axis_index("x").astype(jnp.int32).reshape(1)

    weight_out = lax.all_gather(out_weight.T, SEQ, axis=0, tiled=True)
    weights = jnp.concatenate([gate_weight[0], up_weight[0], down_weight[0]])
    other = lax.ppermute(weights, "core", ring(2, 1))
    routes = picks.reshape(rows, 2)
    turned = routes.T
    all_routes = [turned] + [lax.ppermute(turned, "x", ring(4, -delta)) for delta in (1, 2, 3)]

    inner, states, cum = local_part(
        queries, keys, payload_vectors, log_decay.transpose(0, 2, 1)
    )
    arrived = lax.all_to_all(states, SEQ, 0, 0, tiled=True)
    prefix = lax.all_to_all(scan_states(arrived), SEQ, 0, 0, tiled=True)
    prefix = prefix.reshape(seqs * width // HEAD, HEAD, HEAD)
    normed, other = carried(
        queries, inner, cum, prefix, attn_gain.reshape(1, width), shares, other
    )
    normed = normed.reshape(shares * rows, width)

    place, own_place = route(me, all_routes, cap)
    flat = residual.reshape(rows, model)
    gain = norm_gain.reshape(1, model)
    picked = call(
        pick_kernel,
        "pick",
        [((place.shape[0], width), BF)],
        place,
        normed,
        in_specs=[VM] * 2,
        out_specs=[VM],
        vmem=8,
    )[0]
    terms = []
    for first in (0, half):
        to_up, to_down, to_far, here = selected(first, picked, own_place, weight_out, flat)
        terms += [here, across(to_far, "x"), up_one(to_up, "x"), down_one(to_down, "x")]
    whole, done = whole_projection(normed, weight_out)

    size = terms[0].shape[0]
    a0, b0, whole = call(
        norm_kernel,
        "selected_norm",
        [((size, half), BF)] * 2 + [(whole.shape, BF)],
        *terms,
        gain,
        done,
        whole,
        in_specs=[VM] * 10 + [ANY],
        out_specs=[VM] * 2 + [ANY],
        input_output_aliases={10: 2},
        vmem=50,
    )
    mixed = lax.psum_scatter(whole, "x", scatter_dimension=0, tiled=True)

    a4, b4 = call(
        stack_kernel,
        "stack",
        [((4, size, half), BF)] * 2,
        a0,
        b0,
        across(a0, "y"),
        across(b0, "z"),
        up_one(a0, "y"),
        up_one(b0, "z"),
        down_one(a0, "y"),
        down_one(b0, "z"),
        in_specs=[VM] * 8,
        out_specs=[VM] * 2,
        vmem=8,
    )
    a_below, b_below = up_one(a4, "z"), up_one(b4, "y")
    a_above, b_above = down_one(a4, "z"), down_one(b4, "y")
    a_up, b_up, a_down, b_down = call(
        forward_kernel,
        "forward",
        [((2, size, half), BF)] * 4,
        a_below,
        b_below,
        a_above,
        b_above,
        in_specs=[VM] * 4,
        out_specs=[VM] * 4,
        vmem=8,
    )
    ends_in = (up_one(a_up, "z"), up_one(b_up, "y"), down_one(a_down, "z"), down_one(b_down, "y"))

    acc, w0, w1 = near((a4, b4, a_below, b_below, a_above, b_above), weights, other)
    hidden, *ends = far(acc, ends_in, w0, w1, weights, other)
    body = rest(hidden, weights, other, size)
    oa, ob = (*body[:3], *ends[:2]), (*body[3:], *ends[2:])
    a_below, a_above, b_below, b_above = call(
        fold_kernel,
        "fold",
        [((4, size, half), BF)] * 4,
        oa[1],
        oa[2],
        ob[1],
        ob[2],
        up_one(oa[3], "z"),
        up_one(ob[3], "y"),
        down_one(oa[4], "z"),
        down_one(ob[4], "y"),
        in_specs=[VM] * 8,
        out_specs=[VM] * 4,
        vmem=16,
    )
    parts = call(
        phase_kernel,
        "phase",
        [((size, half), BF)] * 8,
        oa[0],
        ob[0],
        up_one(a_above, "z"),
        up_one(b_above, "y"),
        down_one(a_below, "z"),
        down_one(b_below, "y"),
        in_specs=[VM] * 6,
        out_specs=[VM] * 8,
        vmem=16,
    )
    s0, s1, s2, s3 = call(
        functools.partial(served_kernel, cap),
        "served",
        [((16, model), BF)] * 4,
        parts[0],
        parts[4],
        across(parts[3], "y"),
        across(parts[7], "z"),
        up_one(parts[2], "y"),
        up_one(parts[6], "z"),
        down_one(parts[1], "y"),
        down_one(parts[5], "z"),
        in_specs=[VM] * 8,
        out_specs=[VM] * 4,
    )

    hidden, coef = call(
        home_kernel,
        "home",
        [((rows, model), F32), ((rows, 128), BF)],
        me,
        routes,
        flat,
        mixed,
        gain,
        router_weight.T,
        a_below,
        in_specs=[SM] + [VM] * 6,
        out_specs=[VM] * 2,
        vmem=20,
    )
    out = call(
        final_kernel,
        "combine",
        [((rows, model), BF)],
        hidden,
        coef,
        s0,
        down_one(s1, "x"),
        up_one(s2, "x"),
        across(s3, "x"),
        in_specs=[VM] * 6,
        out_specs=[VM],
        scratch_shapes=[pltpu.VMEM((128, model), BF)],
        vmem=16,
    )[0]
    return out.reshape(seqs, slice_len, model)


def solution(mesh):
    shape = dict(mesh.shape)
    grid = Mesh(mesh.devices.reshape(4, shape["seq"] // 8, 2, shape["exp"]), SEQ + ("x",))
    everyone = SEQ + ("x",)
    placed = (
        P(None, SEQ, "x"),
        P(None, SEQ, "x"),
        P(None, SEQ, "x"),
        P(None, SEQ, "x"),
        P("x"),
        P("x", SEQ),
        P(None, everyone, None),
        P(),
        P(),
        P(None, everyone, None),
        P("x", SEQ, None),
        P("x", SEQ, None),
        P("x", SEQ, None),
    )
    return jax.shard_map(
        shards, mesh=grid, in_specs=placed, out_specs=P(None, everyone, None), check_vma=False
    )
```
